512 devices in a mesh: lat: 8 (over y_hi, x), lon: 64 (over z, y_lo, core).
Axes of the slice: x: 4, y: 4 (y_hi: 2, y_lo: 2; y = y_hi * 2 + y_lo), z: 16, core: 2. Of those that a mesh axis runs over, the one named last changes fastest.
Arguments:
- patches: bfloat16 [96, 2304, 512], P('lat', 'lon'), may hold values from -6 to 6
- query_key_value_weight: bfloat16 [512, 1536], P('lon'), may hold values from -0.25 to 0.25
- attention_output_weight: bfloat16 [512, 512], P('lon'), may hold values from -0.25 to 0.25
- feedforward_in_weight: bfloat16 [512, 2048], P('lon'), may hold values from -0.25 to 0.25
- feedforward_out_weight: bfloat16 [2048, 512], P('lon'), may hold values from -0.125 to 0.125
- merging_reduction_weight: bfloat16 [2048, 1024], P('lon'), may hold values from -0.125 to 0.125
- head_scale_logarithm: float32 [8], replicated, may hold values from 2.3 to 5.3
- bias_network_first_weight: float32 [2, 512], replicated, may hold values from -4 to 4
- bias_network_first_bias: float32 [512], replicated, may hold values from -4 to 4
- bias_network_second_weight: float32 [512, 8], replicated, may hold values from -0.25 to 0.25
- attention_norm_gain: float32 [512], replicated, may hold values from 0.1 to 1.9
- attention_norm_offset: float32 [512], replicated, may hold values from -3 to 3
- feedforward_norm_gain: float32 [512], replicated, may hold values from 0.1 to 1.9
- feedforward_norm_offset: float32 [512], replicated, may hold values from -3 to 3
- merging_norm_gain: float32 [1024], replicated, may hold values from 0.1 to 1.9
- merging_norm_offset: float32 [1024], replicated, may hold values from -3 to 3
Outputs:
- merged: bfloat16 [48, 1152, 1024], P('lat', 'lon')
The draws below stay inside these ranges and needn't reach their ends.
All inputs are finite; a program needn't handle non-finite values.
Results may differ from the reference program's by a relative error of at most 0.012.
Values may be sent and summed in bfloat16 or wider, within the bound.
No kernel may reach another device: no remote copies, remote signals or barrier semaphores. Data moves between devices by JAX's collectives and lax.ppermute only.
A program may use at most 64 MiB of HBM per device.

```python
import jax
import jax.numpy as jnp
from jax import lax

D = 512
HEAD_COUNT = 8
BIAS_NET_HIDDEN = 512
WIN_ROWS = 6
WIN_COLS = 12
FFN = 2048
SHIFT_ROWS = 3
SHIFT_COLS = 6
HEIGHT = 96
WIDTH = 2304


def levels(rng, dims, shards, low, high):
    def one(position, shards_of):
        draws = jax.random.uniform(jax.random.fold_in(jax.random.fold_in(rng, 6), position), (shards_of,), jnp.float32, low / len(shards), high / len(shards))
        return jnp.repeat(jnp.exp(draws), dims[position] // shards_of).reshape((-1,) + (1,) * (len(dims) - position - 1))

    gain = one(*shards[0])
    for cut in shards[1:]:
        gain = gain * one(*cut)
    return gain


def bell_draw(rng, dims, spread, limit, cuts=(), held_as=jnp.bfloat16):
    loudness = levels(rng, dims, cuts, -0.22, 0.18) if cuts else 1.0
    entries = jax.random.normal(rng, dims, jnp.float32) * spread * loudness
    return jnp.minimum(jnp.maximum(entries, -limit), limit).astype(held_as)


def setup_inputs(seed: int = 0) -> dict:
    seeds = jax.random.split(jax.random.key(seed), 17)
    patches = bell_draw(seeds[0], (HEIGHT, WIDTH, D), 1.0, 6.0, ((0, 8), (1, 64)))
    query_key_value_weight = bell_draw(seeds[1], (D, 3 * D), D ** -0.5, 0.25, ((0, 64),))
    attention_output_weight = bell_draw(seeds[2], (D, D), D ** -0.5, 0.25, ((0, 64),))
    feedforward_in_weight = bell_draw(seeds[3], (D, FFN), D ** -0.5, 0.25, ((0, 64),))
    feedforward_out_weight = bell_draw(seeds[4], (FFN, D), FFN ** -0.5, 0.125, ((0, 64),))
    merging_reduction_weight = bell_draw(seeds[5], (4 * D, 2 * D), (4 * D) ** -0.5, 0.125, ((0, 64),))
    head_scale_logarithm = jnp.clip(jax.random.uniform(seeds[6], (HEAD_COUNT,), jnp.float32, 2.3, 5.3), 2.3, 5.3)
    bias_network_first_weight = bell_draw(seeds[7], (2, BIAS_NET_HIDDEN), 2 ** -0.5, 4.0, (), jnp.float32)
    bias_network_first_bias = bell_draw(seeds[8], (BIAS_NET_HIDDEN,), 1.0, 4.0, (), jnp.float32)
    bias_network_second_weight = bell_draw(seeds[9], (BIAS_NET_HIDDEN, HEAD_COUNT), BIAS_NET_HIDDEN ** -0.5, 0.25, (), jnp.float32)
    attention_norm_gain = jnp.clip(1.0 + 0.18 * jax.random.normal(seeds[10], (D,), jnp.float32), 0.1, 1.9)
    attention_norm_offset = bell_draw(seeds[11], (D,), 0.5, 3.0, (), jnp.float32)
    feedforward_norm_gain = jnp.clip(1.0 + 0.18 * jax.random.normal(seeds[12], (D,), jnp.float32), 0.1, 1.9)
    feedforward_norm_offset = bell_draw(seeds[13], (D,), 0.5, 3.0, (), jnp.float32)
    merging_norm_gain = jnp.clip(1.0 + 0.18 * jax.random.normal(seeds[14], (2 * D,), jnp.float32), 0.1, 1.9)
    merging_norm_offset = bell_draw(seeds[15], (2 * D,), 0.5, 3.0, (), jnp.float32)
    return {"patches": patches, "query_key_value_weight": query_key_value_weight, "attention_output_weight": attention_output_weight, "feedforward_in_weight": feedforward_in_weight, "feedforward_out_weight": feedforward_out_weight, "merging_reduction_weight": merging_reduction_weight, "head_scale_logarithm": head_scale_logarithm, "bias_network_first_weight": bias_network_first_weight, "bias_network_first_bias": bias_network_first_bias, "bias_network_second_weight": bias_network_second_weight, "attention_norm_gain": attention_norm_gain, "attention_norm_offset": attention_norm_offset, "feedforward_norm_gain": feedforward_norm_gain, "feedforward_norm_offset": feedforward_norm_offset, "merging_norm_gain": merging_norm_gain, "merging_norm_offset": merging_norm_offset}


def layer_norm(values, norm_gain, norm_shift):
    average = lax.optimization_barrier(jnp.mean(values, axis=-1, keepdims=True))
    centred = values - average
    variance = lax.optimization_barrier(jnp.mean(centred * centred, axis=-1, keepdims=True))
    return centred * lax.rsqrt(variance + 1e-05) * norm_gain + norm_shift

def bias_by_position(bias_network_first_weight, bias_network_first_bias, bias_network_second_weight):
    span_rows = 2 * WIN_ROWS - 1
    span_cols = 2 * WIN_COLS - 1
    entry_index = jnp.arange(span_rows * span_cols, dtype=jnp.int32)
    offset_rows = entry_index // span_cols - (WIN_ROWS - 1)
    offset_cols = entry_index % span_cols - (WIN_COLS - 1)
    relative_coordinates = jnp.stack([offset_rows.astype(jnp.float32) * (8.0 / (WIN_ROWS - 1)), offset_cols.astype(jnp.float32) * (8.0 / (WIN_COLS - 1))], axis=1)
    relative_coordinates = jnp.sign(relative_coordinates) * jnp.log2(jnp.abs(relative_coordinates) + 1.0) / 3.0
    bias_hidden_layer = jax.nn.relu(jnp.dot(relative_coordinates, bias_network_first_weight, precision=lax.Precision.HIGHEST) + bias_network_first_bias)
    table_entries = 16.0 * jax.nn.sigmoid(jnp.dot(bias_hidden_layer, bias_network_second_weight, precision=lax.Precision.HIGHEST))
    window_tokens = WIN_ROWS * WIN_COLS
    token_row = jnp.arange(window_tokens, dtype=jnp.int32) // WIN_COLS
    token_col = jnp.arange(window_tokens, dtype=jnp.int32) % WIN_COLS
    lookup = (token_row[:, None] - token_row[None, :] + WIN_ROWS - 1) * span_cols + token_col[:, None] - token_col[None, :] + WIN_COLS - 1
    one_hot = (lookup[:, :, None] == entry_index[None, None, :]).astype(jnp.float32)
    return jnp.einsum('qkr,rh->hqk', one_hot, table_entries, precision=lax.Precision.HIGHEST)

def unit_rows(vectors):
    square_sum = lax.optimization_barrier(jnp.sum(vectors * vectors, axis=-1, keepdims=True)) + 1e-06
    return (vectors * lax.rsqrt(square_sum)).astype(jnp.bfloat16)

def window_attention(triple, region, relative_position_bias, head_scale, band_rows):
    tile_rows, tile_cols, triple_width = triple.shape
    model_width = triple_width // 3
    head_dim = model_width // HEAD_COUNT
    band_count = tile_rows // band_rows
    col_count = tile_cols // WIN_COLS
    window_tokens = band_rows * WIN_COLS
    windows = triple.reshape(band_count, band_rows, col_count, WIN_COLS, triple_width).transpose(0, 2, 1, 3, 4)
    windows = windows.reshape(band_count * col_count, window_tokens, 3, HEAD_COUNT, head_dim)
    unit_q = unit_rows(windows[:, :, 0].astype(jnp.float32))
    unit_k = unit_rows(windows[:, :, 1].astype(jnp.float32))
    values_all = windows[:, :, 2]
    scores = jnp.einsum('wqhd,wkhd->whqk', unit_q.astype(jnp.float32), unit_k.astype(jnp.float32))
    scores = scores * head_scale[None, :, None, None] + relative_position_bias[None, :, :window_tokens, :window_tokens]
    labels = jnp.broadcast_to(region.reshape(band_count, 1, band_rows, 1), (band_count, col_count, band_rows, WIN_COLS)).reshape(band_count * col_count, window_tokens)
    allowed = labels[:, :, None] == labels[:, None, :]
    scores = jnp.where(allowed[:, None], scores, -jnp.inf)
    peak = lax.optimization_barrier(jnp.max(scores, axis=-1, keepdims=True))
    expo = jnp.exp(scores - peak)
    weights = (expo / lax.optimization_barrier(jnp.sum(expo, axis=-1, keepdims=True))).astype(jnp.bfloat16)
    mixed = jnp.einsum('whqk,wkhd->wqhd', weights.astype(jnp.float32), values_all.astype(jnp.float32)).astype(jnp.bfloat16)
    mixed = mixed.reshape(band_count, col_count, band_rows, WIN_COLS, model_width).transpose(0, 2, 1, 3, 4)
    return mixed.reshape(tile_rows, tile_cols, model_width)

def block_tail(first_rows, feedforward_in_weight, feedforward_out_weight, merging_reduction_weight, feedforward_norm_gain, feedforward_norm_offset, merging_norm_gain, merging_norm_offset):
    tile_rows, tile_cols, model_width = first_rows.shape
    tokens_flat = first_rows.reshape(-1, model_width)
    hidden = jax.nn.gelu(jnp.dot(tokens_flat, feedforward_in_weight, preferred_element_type=jnp.float32), approximate=False).astype(jnp.bfloat16)
    branch_two = layer_norm(jnp.dot(hidden, feedforward_out_weight, preferred_element_type=jnp.float32), feedforward_norm_gain, feedforward_norm_offset)
    second = (tokens_flat.astype(jnp.float32) + branch_two).astype(jnp.bfloat16).reshape(tile_rows, tile_cols, model_width)
    quads = second.reshape(tile_rows // 2, 2, tile_cols // 2, 2, model_width).transpose(0, 2, 3, 1, 4)
    quads = quads.reshape(tile_rows // 2 * (tile_cols // 2), 4 * model_width)
    reduced = layer_norm(jnp.dot(quads, merging_reduction_weight, preferred_element_type=jnp.float32), merging_norm_gain, merging_norm_offset)
    return reduced.astype(jnp.bfloat16).reshape(tile_rows // 2, tile_cols // 2, 2 * model_width)

def reference(patches, query_key_value_weight, attention_output_weight, feedforward_in_weight, feedforward_out_weight, merging_reduction_weight, head_scale_logarithm, bias_network_first_weight, bias_network_first_bias, bias_network_second_weight, attention_norm_gain, attention_norm_offset, feedforward_norm_gain, feedforward_norm_offset, merging_norm_gain, merging_norm_offset):
    grid_rows, grid_cols, model_width = patches.shape
    relative_position_bias = bias_by_position(bias_network_first_weight, bias_network_first_bias, bias_network_second_weight)
    head_scale = jnp.exp(jnp.minimum(head_scale_logarithm, jnp.log(100.0)))
    rolled = jnp.roll(patches, (-SHIFT_ROWS, -SHIFT_COLS), axis=(0, 1))
    row_steps = jnp.arange(WIN_ROWS, dtype=jnp.int32)

    def band_branch(band):
        start = band * WIN_ROWS
        tile = lax.dynamic_slice_in_dim(rolled, start, WIN_ROWS, 0)
        global_rows = start + row_steps
        region = (global_rows >= grid_rows - WIN_ROWS).astype(jnp.int32) + (global_rows >= grid_rows - SHIFT_ROWS).astype(jnp.int32)
        triple = jnp.dot(tile.reshape(-1, model_width), query_key_value_weight, preferred_element_type=jnp.float32).astype(jnp.bfloat16)
        attended = window_attention(triple.reshape(WIN_ROWS, grid_cols, 3 * model_width), region, relative_position_bias, head_scale, WIN_ROWS)
        projected = jnp.dot(attended.reshape(-1, model_width), attention_output_weight, preferred_element_type=jnp.float32)
        return layer_norm(projected, attention_norm_gain, attention_norm_offset).astype(jnp.bfloat16).reshape(WIN_ROWS, grid_cols, model_width)
    branch_rolled = lax.map(band_branch, jnp.arange(grid_rows // WIN_ROWS, dtype=jnp.int32))
    branch_rolled = branch_rolled.reshape(grid_rows, grid_cols, model_width)
    attn_branch = jnp.roll(branch_rolled, (SHIFT_ROWS, SHIFT_COLS), axis=(0, 1))
    first = (patches.astype(jnp.float32) + attn_branch.astype(jnp.float32)).astype(jnp.bfloat16)

    def pair_tail(pair):
        first_rows = lax.dynamic_slice_in_dim(first, pair * 2, 2, 0)
        return block_tail(first_rows, feedforward_in_weight, feedforward_out_weight, merging_reduction_weight, feedforward_norm_gain, feedforward_norm_offset, merging_norm_gain, merging_norm_offset)
    merged = lax.map(pair_tail, jnp.arange(grid_rows // 2, dtype=jnp.int32))
    return merged.reshape(grid_rows // 2, grid_cols // 2, 2 * model_width)
```

```python
import jax
import jax.numpy as jnp
import numpy as np
from jax import lax
from jax.experimental import pallas as pl
from jax.experimental.pallas import tpu as pltpu
from jax.sharding import Mesh
from jax.sharding import PartitionSpec as P

D = 512
HEAD_COUNT = 8
WIN_ROWS = 6
WIN_COLS = 12
PAD_COLS = 16
SHIFT_ROWS = 3
SHIFT_COLS = 6
FFN = 2048
WIN_PAD = WIN_ROWS * PAD_COLS
KEY_PAD = 128
BANDS = 3
WINS = 4
QUAD_ROWS = 112
LAT = ("y_hi", "x")
LON = ("z", "y_lo", "core")
PLANE = ("y_hi", "x", "y_lo")
OFF = -1e30
BF16 = jnp.bfloat16
F32 = jnp.float32
QUERY_ROWS = ((48, 48), (0, 96), (0, 48))


def shifted(block, axes, by, wrap):
    size = lax.axis_size(axes)
    pairs = [(i, (i + by) % size) for i in range(size) if wrap or 0 <= i + by < size]
    return lax.ppermute(block, axes, pairs)


def spread(block, axes):
    size = lax.axis_size(axes)
    return lax.all_to_all(jnp.broadcast_to(block[None], (size,) + block.shape), axes, 0, 0)


def bias_entries(first_weight, first_bias, second_weight):
    span_rows = 2 * WIN_ROWS - 1
    span_cols = 2 * WIN_COLS - 1
    entry = np.arange(span_rows * span_cols)
    coordinates = np.stack(
        [
            (entry // span_cols - (WIN_ROWS - 1)) * (8.0 / (WIN_ROWS - 1)),
            (entry % span_cols - (WIN_COLS - 1)) * (8.0 / (WIN_COLS - 1)),
        ],
        axis=1,
    )
    coordinates = np.sign(coordinates) * np.log2(np.abs(coordinates) + 1.0) / 3.0
    coordinates = jnp.asarray(coordinates, F32)
    hidden = jax.nn.relu(
        coordinates[:, :1] * first_weight[:1] + coordinates[:, 1:] * first_weight[1:] + first_bias
    )
    return 16.0 * jax.nn.sigmoid(
        lax.dot_general(
            second_weight, hidden, (((0,), (1,)), ((), ())), precision=lax.Precision.HIGHEST
        )
    )


def bias_lookup():
    q = np.arange(WIN_PAD)
    k = np.arange(KEY_PAD)
    qa, qb = q // PAD_COLS, np.minimum(q % PAD_COLS, WIN_COLS - 1)
    ka, kb = np.minimum(k // PAD_COLS, WIN_ROWS - 1), np.minimum(k % PAD_COLS, WIN_COLS - 1)
    rows = qa[:, None] - ka[None] + WIN_ROWS - 1
    cols = qb[:, None] - kb[None] + WIN_COLS - 1
    return rows * (2 * WIN_COLS - 1) + cols


def unit_norm(triple, ones):
    rounded = triple.astype(BF16)
    exact = rounded.astype(F32)
    square = exact * exact
    high = square.astype(BF16)
    low = (square - high.astype(F32)).astype(BF16)
    parts = []
    for i in range(D // 256):
        cut = slice(i * 256, i * 256 + 256)
        total = jnp.dot(high[:, cut], ones, preferred_element_type=F32)
        total += jnp.dot(low[:, cut], ones, preferred_element_type=F32)
        parts.append((exact[:, cut] * lax.rsqrt(total + 1e-06)).astype(BF16))
    return parts


def norm_rows(values, gain, offset):
    average = jnp.mean(values, axis=-1, keepdims=True)
    centred = values - average
    variance = jnp.mean(centred * centred, axis=-1, keepdims=True)
    return centred * lax.rsqrt(variance + 1e-05) * gain + offset


def attention_kernel(
    core_ref,
    scale_ref,
    windows_ref,
    bias_ref,
    patches_ref,
    select_ref,
    gain_ref,
    offset_ref,
    mine_ref,
    other_ref,
    out_ref,
    weight,
    queries,
    keys,
    values,
    heads,
    sems,
):
    core = core_ref[0]
    copies = []
    for m in range(16):
        lat, y_lo = m // 2, m % 2
        for part, (ref, of) in enumerate(((mine_ref, core), (other_ref, 1 - core))):
            column = pl.multiple_of((lat * 2 + of) * 128, 128)
            copies.append(
                pltpu.make_async_copy(
                    ref.at[m],
                    weight.at[:, pl.ds(y_lo * 16, 16), pl.ds(column, 128)],
                    sems.at[m * 2 + part],
                )
            )
    for copy in copies:
        copy.start()
    for copy in copies:
        copy.wait()

    row = lax.broadcasted_iota(jnp.int32, (256, 256), 0)
    lane = lax.broadcasted_iota(jnp.int32, (256, 256), 1)
    ones = jnp.where(row // 64 == lane // 64, 1.0, 0.0).astype(BF16)
    row2 = lax.broadcasted_iota(jnp.int32, (256, 128), 0)
    lane2 = lax.broadcasted_iota(jnp.int32, (256, 128), 1)
    counts = jnp.where((row2 >= 128) == (lane2 >= 64), 1.0, 0.0).astype(BF16)
    low_half = lax.broadcasted_iota(jnp.int32, (WIN_PAD, 128), 1) < 64
    zero = jnp.zeros((WIN_PAD, 128), BF16)
    gap = jnp.zeros((KEY_PAD - WIN_PAD, 128), BF16)
    half = WINS * WIN_PAD

    def columns(start, width):
        return weight[:, :, start : start + width].reshape(D, width)

    def both(block):
        return jnp.concatenate(
            [jnp.where(low_half, block, zero), gap, jnp.where(low_half, zero, block), gap], axis=0
        )

    done = 0
    for band in range(BANDS):
        tokens = windows_ref[band * half : (band + 1) * half, :]
        for target, start in ((queries, 0), (keys, D)):
            total = jnp.dot(tokens, columns(start, D), preferred_element_type=F32)
            for i, part in enumerate(unit_norm(total, ones)):
                target[:, i * 256 : i * 256 + 256] = part
        values[...] = jnp.dot(tokens, columns(2 * D, D), preferred_element_type=F32).astype(BF16)
        first, count = QUERY_ROWS[band]

        def window(w, _, band=band, first=first, count=count, done=done):
            base = pl.multiple_of(w * WIN_PAD, WIN_PAD)
            for pair in range(HEAD_COUNT // 2):
                cut = slice(pair * 128, pair * 128 + 128)
                query = queries[pl.ds(base + first, count), cut]
                key = both(keys[pl.ds(base, WIN_PAD), cut])
                value = both(values[pl.ds(base, WIN_PAD), cut])
                scores = lax.dot_general(
                    query, key, (((1,), (1,)), ((), ())), preferred_element_type=F32
                )
                expo = []
                for h in range(2):
                    head = pair * 2 + h
                    one = scores[:, h * 128 : h * 128 + 128] * scale_ref[head]
                    one = one + bias_ref[band, head, first : first + count, :]
                    peak = jnp.max(one, axis=-1, keepdims=True)
                    expo.append(jnp.exp(one - peak).astype(BF16))
                mixed = jnp.dot(
                    jnp.concatenate(expo, axis=1),
                    jnp.concatenate([value, counts], axis=1),
                    preferred_element_type=F32,
                )
                place = pl.multiple_of(done + w * count, 16)
                heads[pl.ds(place, count), cut] = (mixed[:, :128] / mixed[:, 128:]).astype(BF16)
            return 0

        lax.fori_loop(0, WINS, window, 0)
        done += WINS * count

    own = jnp.dot(select_ref[...], heads[...], preferred_element_type=F32).astype(BF16)
    projected = jnp.dot(own, columns(3 * D, D), preferred_element_type=F32)
    branch = norm_rows(projected, gain_ref[...], offset_ref[...]).astype(BF16)
    out_ref[...] = (patches_ref[...].astype(F32) + branch.astype(F32)).astype(BF16)


def feedforward_kernel(
    core_ref,
    first_ref,
    gain_ref,
    offset_ref,
    merge_gain_ref,
    merge_offset_ref,
    mine_ref,
    other_ref,
    merge_ref,
    out_ref,
    up,
    down,
    merge,
    up_sems,
    down_sems,
    merge_sems,
):
    core = core_ref[0]
    ups, downs, merges = [], [], []
    for m in range(16):
        y_hi, x, y_lo = m // 8, m // 2 % 4, m % 2
        for part, (ref, of) in enumerate(((mine_ref, core), (other_ref, 1 - core))):
            column = pl.multiple_of((m // 2 * 2 + of) * 128, 128)
            ups.append(
                pltpu.make_async_copy(
                    ref.at[m, 0],
                    up.at[:, pl.ds(y_lo * 16, 16), pl.ds(column, 128)],
                    up_sems.at[m * 2 + part],
                )
            )
            start = pl.multiple_of(y_lo * 64 + of * 32 + y_hi * 16, 16)
            downs.append(
                pltpu.make_async_copy(
                    ref.at[m, 1],
                    down.at[:, pl.ds(start, 16), pl.ds(x * 128, 128)],
                    down_sems.at[m * 2 + part],
                )
            )
        x, y_lo, of = m // 4, m // 2 % 2, m % 2
        merges.append(
            pltpu.make_async_copy(
                merge_ref.at[m],
                merge.at[:, pl.ds(y_lo * 64 + of * 32, 32), pl.ds(x * 256, 256)],
                merge_sems.at[m],
            )
        )
    for copy in ups + downs + merges:
        copy.start()
    for copy in ups:
        copy.wait()
    tokens = first_ref[...]
    total = None
    for n in range(FFN // 512):
        cut = slice(n * 512, n * 512 + 512)
        hidden = jnp.dot(tokens, up[:, :, cut].reshape(D, 512), preferred_element_type=F32)
        hidden = (0.5 * hidden * (1.0 + lax.erf(hidden * (0.5**0.5)))).astype(BF16)
        if n == 0:
            for copy in downs:
                copy.wait()
        piece = jnp.dot(
            hidden, down[n * 4 : n * 4 + 4].reshape(512, D), preferred_element_type=F32
        )
        total = piece if total is None else total + piece
    branch = norm_rows(total, gain_ref[...], offset_ref[...])
    second = (tokens.astype(F32) + branch).astype(BF16)
    for copy in merges:
        copy.wait()
    total = None
    for n in range(4):
        piece = jnp.dot(
            second[n * QUAD_ROWS : (n + 1) * QUAD_ROWS],
            merge[n * 4 : n * 4 + 4].reshape(512, 2 * D),
            preferred_element_type=F32,
        )
        total = piece if total is None else total + piece
    reduced = norm_rows(total, merge_gain_ref[...], merge_offset_ref[...])
    for i in range(6):
        out_ref[i] = reduced[i * 18 : i * 18 + 18].astype(BF16)


def selection():
    place = np.full((12, 36), -1)
    done = 0
    for band in range(BANDS):
        first, count = QUERY_ROWS[band]
        for w in range(WINS):
            for r in range(count):
                a, b = (first + r) // PAD_COLS, (first + r) % PAD_COLS
                i = band * WIN_ROWS + a - SHIFT_ROWS
                j = w * WIN_COLS + b - SHIFT_COLS
                if b < WIN_COLS and 0 <= j < 36:
                    place[i, j] = done + r
            done += count
    order = place.reshape(6, 2, 18, 2).transpose(3, 1, 0, 2).reshape(4, 108)
    order = np.pad(order, ((0, 0), (0, QUAD_ROWS - 108)), constant_values=-1).reshape(-1)
    return (order[:, None] == np.arange(done)[None]).astype(np.float32)


def local(
    patches,
    query_key_value_weight,
    attention_output_weight,
    feedforward_in_weight,
    feedforward_out_weight,
    merging_reduction_weight,
    head_scale_logarithm,
    bias_network_first_weight,
    bias_network_first_bias,
    bias_network_second_weight,
    attention_norm_gain,
    attention_norm_offset,
    feedforward_norm_gain,
    feedforward_norm_offset,
    merging_norm_gain,
    merging_norm_offset,
):
    lat = lax.axis_index(LAT)
    core = lax.axis_index("core")
    x = lax.axis_index("x")

    mine = jnp.concatenate(
        [query_key_value_weight, attention_output_weight, feedforward_in_weight], axis=1
    )
    theirs = shifted(mine, "core", 1, True)
    rows = jnp.concatenate(
        [jnp.where(core == 0, mine, theirs), jnp.where(core == 0, theirs, mine)], axis=0
    )
    at = (lat * 2 + core) * 128
    units = jnp.stack(
        [
            lax.dynamic_slice(rows, (0, at), (16, 128)),
            lax.dynamic_slice(rows, (0, 2048 + at), (16, 128)),
            lax.dynamic_slice(
                feedforward_out_weight, (lax.axis_index("y_hi") * 16, x * 128), (16, 128)
            ),
        ]
    )
    along_z = spread(units, "z")
    merge_part = lax.dynamic_slice(merging_reduction_weight, (0, x * 256), (32, 256))
    merge_z = spread(merge_part, "z")
    merge_all = lax.all_gather(merge_z, ("x", "y_lo", "core"), axis=0)
    attn_mine = spread(along_z[:, 0], PLANE)
    attn_other = shifted(attn_mine, "core", 1, True)
    ffn_mine = spread(along_z[:, 1:].transpose(1, 0, 2, 3), PLANE)
    ffn_other = shifted(ffn_mine, "core", 1, True)

    east = shifted(patches[:, :SHIFT_COLS], LON, -1, True)
    west = shifted(patches[:, 36 - SHIFT_COLS :], LON, 1, True)
    wide = jnp.concatenate([west, patches, east], axis=1)
    south = shifted(wide[:SHIFT_ROWS], LAT, -1, False)
    north = shifted(wide[12 - SHIFT_ROWS :], LAT, 1, False)
    tall = jnp.concatenate([north, wide, south], axis=0)
    windows = tall.reshape(BANDS, WIN_ROWS, WINS, WIN_COLS, D).transpose(0, 2, 1, 3, 4)
    windows = jnp.pad(windows, ((0, 0), (0, 0), (0, 0), (0, PAD_COLS - WIN_COLS), (0, 0)))
    windows = windows.reshape(BANDS * WINS * WIN_PAD, D)
    ordered = patches.reshape(6, 2, 18, 2, D).transpose(3, 1, 0, 2, 4).reshape(4, 108, D)
    ordered = jnp.pad(ordered, ((0, 0), (0, QUAD_ROWS - 108), (0, 0))).reshape(4 * QUAD_ROWS, D)

    table = bias_entries(
        bias_network_first_weight, bias_network_first_bias, bias_network_second_weight
    )
    lookup = bias_lookup()
    entries = table.shape[1]
    one_hot = (
        jnp.asarray(lookup.reshape(-1), jnp.int32)[None, :]
        == jnp.arange(entries, dtype=jnp.int32)[:, None]
    ).astype(F32)
    bias = jnp.dot(table, one_hot, precision=lax.Precision.HIGHEST)
    bias = bias.reshape(HEAD_COUNT, WIN_PAD, KEY_PAD)
    key = np.arange(KEY_PAD)
    held = (key < WIN_PAD) & (key % PAD_COLS < WIN_COLS)
    bias = jnp.where(jnp.asarray(held), bias, OFF)
    apart = (np.arange(WIN_PAD)[:, None] // 48) != (key[None] // 48)
    seam = jnp.stack([lat == 0, jnp.bool_(False), lat == 7])
    bias = jnp.where(seam[:, None, None, None] & jnp.asarray(apart), OFF, bias[None])
    head_scale = jnp.exp(jnp.minimum(head_scale_logarithm, jnp.log(100.0)))

    vmem = pl.BlockSpec(memory_space=pltpu.VMEM)
    smem = pl.BlockSpec(memory_space=pltpu.SMEM)
    anywhere = pl.BlockSpec(memory_space=pl.ANY)
    core_index = core.astype(jnp.int32).reshape(1)
    half = WINS * WIN_PAD
    first = pl.pallas_call(
        attention_kernel,
        out_shape=jax.ShapeDtypeStruct((4 * QUAD_ROWS, D), BF16),
        in_specs=[smem, smem] + [vmem] * 6 + [anywhere] * 2,
        out_specs=vmem,
        scratch_shapes=[
            pltpu.VMEM((16, 32, 2048), BF16),
            pltpu.VMEM((half, D), BF16),
            pltpu.VMEM((half, D), BF16),
            pltpu.VMEM((half, D), BF16),
            pltpu.VMEM((768, D), BF16),
            pltpu.SemaphoreType.DMA((32,)),
        ],
        compiler_params=pltpu.CompilerParams(vmem_limit_bytes=40 * 1024 * 1024),
        cost_estimate=pl.CostEstimate(
            flops=6_000_000_000, bytes_accessed=20_000_000, transcendentals=1_000_000
        ),
        name="attention",
    )(
        core_index,
        head_scale,
        windows,
        bias,
        ordered,
        jnp.asarray(selection(), BF16),
        attention_norm_gain.reshape(1, D),
        attention_norm_offset.reshape(1, D),
        attn_mine,
        attn_other,
    )
    return pl.pallas_call(
        feedforward_kernel,
        out_shape=jax.ShapeDtypeStruct((6, 18, 2 * D), BF16),
        in_specs=[smem] + [vmem] * 5 + [anywhere] * 3,
        out_specs=vmem,
        scratch_shapes=[
            pltpu.VMEM((16, 32, FFN), BF16),
            pltpu.VMEM((16, 128, D), BF16),
            pltpu.VMEM((16, 128, 2 * D), BF16),
            pltpu.SemaphoreType.DMA((32,)),
            pltpu.SemaphoreType.DMA((32,)),
            pltpu.SemaphoreType.DMA((16,)),
        ],
        compiler_params=pltpu.CompilerParams(vmem_limit_bytes=40 * 1024 * 1024),
        cost_estimate=pl.CostEstimate(
            flops=3_000_000_000, bytes_accessed=20_000_000, transcendentals=1_000_000
        ),
        name="feedforward",
    )(
        core_index,
        first,
        feedforward_norm_gain.reshape(1, D),
        feedforward_norm_offset.reshape(1, D),
        merging_norm_gain.reshape(1, 2 * D),
        merging_norm_offset.reshape(1, 2 * D),
        ffn_mine,
        ffn_other,
        merge_all.reshape(16, 16, 32, 256),
    )


def solution(mesh):
    fine = Mesh(mesh.devices.reshape(2, 4, 16, 2, 2), ("y_hi", "x", "z", "y_lo", "core"))
    in_specs = (P(LAT, LON, None),) + (P(LON, None),) * 5 + (P(),) * 10
    return jax.shard_map(
        local, mesh=fine, in_specs=in_specs, out_specs=P(LAT, LON, None), check_vma=False
    )
```

```python
import jax
import jax.numpy as jnp
import numpy as np
from jax import lax
from jax.experimental import pallas as pl
from jax.experimental.pallas import tpu as pltpu
from jax.sharding import Mesh
from jax.sharding import PartitionSpec as P

D = 512
HEAD_COUNT = 8
WIN_ROWS = 6
WIN_COLS = 12
PAD_COLS = 16
SHIFT_ROWS = 3
SHIFT_COLS = 6
FFN = 2048
WIN_PAD = WIN_ROWS * PAD_COLS
KEY_PAD = 128
BANDS = 3
WINS = 4
QUAD_ROWS = 112
LAT = ("y_hi", "x")
LON = ("z", "y_lo", "core")
PLANE = ("y_hi", "x", "y_lo")
OFF = -1e30
BF16 = jnp.bfloat16
F32 = jnp.float32
QUERY_ROWS = ((48, 48), (0, 96), (0, 48))


def shifted(block, axes, by, wrap):
    size = lax.axis_size(axes)
    pairs = [(i, (i + by) % size) for i in range(size) if wrap or 0 <= i + by < size]
    return lax.ppermute(block, axes, pairs)


def spread(block, axes):
    size = lax.axis_size(axes)
    return lax.all_to_all(jnp.broadcast_to(block[None], (size,) + block.shape), axes, 0, 0)


def bias_entries(first_weight, first_bias, second_weight):
    span_rows = 2 * WIN_ROWS - 1
    span_cols = 2 * WIN_COLS - 1
    entry = np.arange(span_rows * span_cols)
    coordinates = np.stack(
        [
            (entry // span_cols - (WIN_ROWS - 1)) * (8.0 / (WIN_ROWS - 1)),
            (entry % span_cols - (WIN_COLS - 1)) * (8.0 / (WIN_COLS - 1)),
        ],
        axis=1,
    )
    coordinates = np.sign(coordinates) * np.log2(np.abs(coordinates) + 1.0) / 3.0
    coordinates = jnp.asarray(coordinates, F32)
    hidden = jax.nn.relu(
        coordinates[:, :1] * first_weight[:1] + coordinates[:, 1:] * first_weight[1:] + first_bias
    )
    return 16.0 * jax.nn.sigmoid(
        lax.dot_general(
            second_weight, hidden, (((0,), (1,)), ((), ())), precision=lax.Precision.HIGHEST
        )
    )


def bias_lookup():
    q = np.arange(WIN_PAD)
    k = np.arange(KEY_PAD)
    qa, qb = q // PAD_COLS, np.minimum(q % PAD_COLS, WIN_COLS - 1)
    ka, kb = np.minimum(k // PAD_COLS, WIN_ROWS - 1), np.minimum(k % PAD_COLS, WIN_COLS - 1)
    rows = qa[:, None] - ka[None] + WIN_ROWS - 1
    cols = qb[:, None] - kb[None] + WIN_COLS - 1
    return rows * (2 * WIN_COLS - 1) + cols


def unit_norm(triple, ones):
    rounded = triple.astype(BF16)
    exact = rounded.astype(F32)
    square = exact * exact
    high = square.astype(BF16)
    low = (square - high.astype(F32)).astype(BF16)
    parts = []
    for i in range(D // 256):
        cut = slice(i * 256, i * 256 + 256)
        total = jnp.dot(high[:, cut], ones, preferred_element_type=F32)
        total += jnp.dot(low[:, cut], ones, preferred_element_type=F32)
        parts.append((exact[:, cut] * lax.rsqrt(total + 1e-06)).astype(BF16))
    return parts


def norm_rows(values, gain, offset):
    average = jnp.mean(values, axis=-1, keepdims=True)
    centred = values - average
    variance = jnp.mean(centred * centred, axis=-1, keepdims=True)
    return centred * lax.rsqrt(variance + 1e-05) * gain + offset


def attention_kernel(
    core_ref,
    scale_ref,
    tall_ref,
    bias_ref,
    arrange_ref,
    patch_select_ref,
    select_ref,
    gain_ref,
    offset_ref,
    mine_ref,
    other_ref,
    out_ref,
    weight,
    queries,
    keys,
    values,
    heads,
    sems,
):
    core = core_ref[0]
    copies = []
    for m in range(16):
        lat, y_lo = m // 2, m % 2
        for part, (ref, of) in enumerate(((mine_ref, core), (other_ref, 1 - core))):
            column = pl.multiple_of((lat * 2 + of) * 128, 128)
            copies.append(
                pltpu.make_async_copy(
                    ref.at[m],
                    weight.at[:, pl.ds(y_lo * 16, 16), pl.ds(column, 128)],
                    sems.at[m * 2 + part],
                )
            )
    for copy in copies:
        copy.start()
    for copy in copies:
        copy.wait()

    row = lax.broadcasted_iota(jnp.int32, (256, 256), 0)
    lane = lax.broadcasted_iota(jnp.int32, (256, 256), 1)
    ones = jnp.where(row // 64 == lane // 64, 1.0, 0.0).astype(BF16)
    row2 = lax.broadcasted_iota(jnp.int32, (256, 128), 0)
    lane2 = lax.broadcasted_iota(jnp.int32, (256, 128), 1)
    counts = jnp.where((row2 >= 128) == (lane2 >= 64), 1.0, 0.0).astype(BF16)
    low_half = lax.broadcasted_iota(jnp.int32, (WIN_PAD, 128), 1) < 64
    zero = jnp.zeros((WIN_PAD, 128), BF16)
    gap = jnp.zeros((KEY_PAD - WIN_PAD, 128), BF16)

    def columns(start, width):
        return weight[:, :, start : start + width].reshape(D, width)

    def both(block):
        return jnp.concatenate(
            [jnp.where(low_half, block, zero), gap, jnp.where(low_half, zero, block), gap], axis=0
        )

    done = 0
    for band in range(BANDS):
        strip = tall_ref[band * WIN_ROWS : (band + 1) * WIN_ROWS].reshape(WIN_ROWS * 48, D)
        tokens = jnp.dot(arrange_ref[...], strip, preferred_element_type=F32).astype(BF16)
        for target, start in ((queries, 0), (keys, D)):
            total = jnp.dot(tokens, columns(start, D), preferred_element_type=F32)
            for i, part in enumerate(unit_norm(total, ones)):
                target[:, i * 256 : i * 256 + 256] = part
        values[...] = jnp.dot(tokens, columns(2 * D, D), preferred_element_type=F32).astype(BF16)
        first, count = QUERY_ROWS[band]

        def window(w, _, band=band, first=first, count=count, done=done):
            base = pl.multiple_of(w * WIN_PAD, WIN_PAD)
            for pair in range(HEAD_COUNT // 2):
                cut = slice(pair * 128, pair * 128 + 128)
                query = queries[pl.ds(base + first, count), cut]
                key = both(keys[pl.ds(base, WIN_PAD), cut])
                value = both(values[pl.ds(base, WIN_PAD), cut])
                scores = lax.dot_general(
                    query, key, (((1,), (1,)), ((), ())), preferred_element_type=F32
                )
                expo = []
                for h in range(2):
                    head = pair * 2 + h
                    one = scores[:, h * 128 : h * 128 + 128] * scale_ref[head]
                    one = one + bias_ref[band, head, first : first + count, :]
                    peak = jnp.max(one, axis=-1, keepdims=True)
                    expo.append(jnp.exp(one - peak).astype(BF16))
                mixed = jnp.dot(
                    jnp.concatenate(expo, axis=1),
                    jnp.concatenate([value, counts], axis=1),
                    preferred_element_type=F32,
                )
                place = pl.multiple_of(done + w * count, 16)
                heads[pl.ds(place, count), cut] = (mixed[:, :128] / mixed[:, 128:]).astype(BF16)
            return 0

        lax.fori_loop(0, WINS, window, 0)
        done += WINS * count

    own = jnp.dot(select_ref[...], heads[...], preferred_element_type=F32).astype(BF16)
    projected = jnp.dot(own, columns(3 * D, D), preferred_element_type=F32)
    branch = norm_rows(projected, gain_ref[...], offset_ref[...]).astype(BF16)
    patches = jnp.dot(
        patch_select_ref[...], tall_ref[...].reshape(18 * 48, D), preferred_element_type=F32
    )
    out_ref[...] = (patches + branch.astype(F32)).astype(BF16)


def feedforward_kernel(
    core_ref,
    first_ref,
    gain_ref,
    offset_ref,
    merge_gain_ref,
    merge_offset_ref,
    mine_ref,
    other_ref,
    merge_ref,
    out_ref,
    up,
    down,
    merge,
    up_sems,
    down_sems,
    merge_sems,
):
    core = core_ref[0]
    ups, downs, merges = [], [], []
    for m in range(16):
        y_hi, x, y_lo = m // 8, m // 2 % 4, m % 2
        for part, (ref, of) in enumerate(((mine_ref, core), (other_ref, 1 - core))):
            column = pl.multiple_of((m // 2 * 2 + of) * 128, 128)
            ups.append(
                pltpu.make_async_copy(
                    ref.at[m, :, pl.ds(0, 16), :],
                    up.at[:, pl.ds(y_lo * 16, 16), pl.ds(column, 128)],
                    up_sems.at[m * 2 + part],
                )
            )
            start = pl.multiple_of(y_lo * 64 + of * 32 + y_hi * 16, 16)
            downs.append(
                pltpu.make_async_copy(
                    ref.at[m, :, pl.ds(16, 16), :],
                    down.at[:, pl.ds(start, 16), pl.ds(x * 128, 128)],
                    down_sems.at[m * 2 + part],
                )
            )
        x, y_lo, of = m // 4, m // 2 % 2, m % 2
        for part in range(2):
            merges.append(
                pltpu.make_async_copy(
                    merge_ref.at[m, :, pl.ds(part * 32, 32), :],
                    merge.at[
                        :, pl.ds(y_lo * 64 + of * 32, 32), pl.ds(x * 256 + part * 128, 128)
                    ],
                    merge_sems.at[m * 2 + part],
                )
            )
    for copy in ups + downs + merges:
        copy.start()
    for copy in ups:
        copy.wait()
    tokens = first_ref[...]
    total = None
    for n in range(FFN // 512):
        cut = slice(n * 512, n * 512 + 512)
        hidden = jnp.dot(tokens, up[:, :, cut].reshape(D, 512), preferred_element_type=F32)
        hidden = (0.5 * hidden * (1.0 + lax.erf(hidden * (0.5**0.5)))).astype(BF16)
        if n == 0:
            for copy in downs:
                copy.wait()
        piece = jnp.dot(
            hidden, down[n * 4 : n * 4 + 4].reshape(512, D), preferred_element_type=F32
        )
        total = piece if total is None else total + piece
    branch = norm_rows(total, gain_ref[...], offset_ref[...])
    second = (tokens.astype(F32) + branch).astype(BF16)
    for copy in merges:
        copy.wait()
    total = None
    for n in range(4):
        piece = jnp.dot(
            second[n * QUAD_ROWS : (n + 1) * QUAD_ROWS],
            merge[n * 4 : n * 4 + 4].reshape(512, 2 * D),
            preferred_element_type=F32,
        )
        total = piece if total is None else total + piece
    reduced = norm_rows(total, merge_gain_ref[...], merge_offset_ref[...])
    for i in range(6):
        out_ref[i] = reduced[i * 18 : i * 18 + 18].astype(BF16)


def quads_order(place):
    order = place.reshape(6, 2, 18, 2).transpose(3, 1, 0, 2).reshape(4, 108)
    return np.pad(order, ((0, 0), (0, QUAD_ROWS - 108)), constant_values=-1).reshape(-1)


def one_hot_rows(order, size):
    return (order[:, None] == np.arange(size)[None]).astype(np.float32)


def selection():
    place = np.full((12, 36), -1)
    done = 0
    for band in range(BANDS):
        first, count = QUERY_ROWS[band]
        for w in range(WINS):
            for r in range(count):
                a, b = (first + r) // PAD_COLS, (first + r) % PAD_COLS
                i = band * WIN_ROWS + a - SHIFT_ROWS
                j = w * WIN_COLS + b - SHIFT_COLS
                if b < WIN_COLS and 0 <= j < 36:
                    place[i, j] = done + r
            done += count
    return one_hot_rows(quads_order(place), done)


def patch_selection():
    i, j = np.arange(12)[:, None] + SHIFT_ROWS, np.arange(36)[None] + SHIFT_COLS
    return one_hot_rows(quads_order(i * 48 + j), 18 * 48)


def arrangement():
    r = np.arange(WINS * WIN_PAD)
    w, a, b = r // WIN_PAD, r % WIN_PAD // PAD_COLS, r % PAD_COLS
    return one_hot_rows(np.where(b < WIN_COLS, a * 48 + w * WIN_COLS + b, -1), WIN_ROWS * 48)


def local(
    patches,
    query_key_value_weight,
    attention_output_weight,
    feedforward_in_weight,
    feedforward_out_weight,
    merging_reduction_weight,
    head_scale_logarithm,
    bias_network_first_weight,
    bias_network_first_bias,
    bias_network_second_weight,
    attention_norm_gain,
    attention_norm_offset,
    feedforward_norm_gain,
    feedforward_norm_offset,
    merging_norm_gain,
    merging_norm_offset,
):
    lat = lax.axis_index(LAT)
    core = lax.axis_index("core")
    x = lax.axis_index("x")

    mine = jnp.concatenate(
        [query_key_value_weight, attention_output_weight, feedforward_in_weight], axis=1
    )
    theirs = shifted(mine, "core", 1, True)
    rows = jnp.concatenate(
        [jnp.where(core == 0, mine, theirs), jnp.where(core == 0, theirs, mine)], axis=0
    )
    at = (lat * 2 + core) * 128
    units = jnp.concatenate(
        [
            lax.dynamic_slice(rows, (0, at), (16, 128)),
            lax.dynamic_slice(rows, (0, 2048 + at), (16, 128)),
            lax.dynamic_slice(
                feedforward_out_weight, (lax.axis_index("y_hi") * 16, x * 128), (16, 128)
            ),
            lax.dynamic_slice(merging_reduction_weight, (0, x * 256), (32, 128)),
            lax.dynamic_slice(merging_reduction_weight, (0, x * 256 + 128), (32, 128)),
        ]
    )
    units, patches = lax.optimization_barrier((units, patches))
    along_z = spread(units, "z")
    east = shifted(patches[:, :SHIFT_COLS], LON, -1, True)
    west = shifted(patches[:, 36 - SHIFT_COLS :], LON, 1, True)
    wide = jnp.concatenate([west, patches, east], axis=1)
    south = shifted(wide[:SHIFT_ROWS], LAT, -1, False)
    north = shifted(wide[12 - SHIFT_ROWS :], LAT, 1, False)
    tall = jnp.concatenate([north, wide, south], axis=0)

    along_z, tall = lax.optimization_barrier((along_z, tall))
    merge_all = lax.all_gather(along_z[:, 48:], ("x", "y_lo", "core"), axis=0)
    attn_mine = spread(along_z[:, :16], PLANE)

    table = bias_entries(
        bias_network_first_weight, bias_network_first_bias, bias_network_second_weight
    )
    lookup = bias_lookup()
    entries = table.shape[1]
    one_hot = (
        jnp.asarray(lookup.reshape(-1), jnp.int32)[None, :]
        == jnp.arange(entries, dtype=jnp.int32)[:, None]
    ).astype(F32)
    bias = jnp.dot(table, one_hot, precision=lax.Precision.HIGHEST)
    bias = bias.reshape(HEAD_COUNT, WIN_PAD, KEY_PAD)
    key = np.arange(KEY_PAD)
    held = (key < WIN_PAD) & (key % PAD_COLS < WIN_COLS)
    bias = jnp.where(jnp.asarray(held), bias, OFF)
    apart = (np.arange(WIN_PAD)[:, None] // 48) != (key[None] // 48)
    seam = jnp.stack([lat == 0, jnp.bool_(False), lat == 7])
    bias = jnp.where(seam[:, None, None, None] & jnp.asarray(apart), OFF, bias[None])
    head_scale = jnp.exp(jnp.minimum(head_scale_logarithm, jnp.log(100.0)))

    attn_mine, ffn_z, bias = lax.optimization_barrier((attn_mine, along_z[:, 16:48], bias))
    attn_other = shifted(attn_mine, "core", 1, True)
    ffn_mine = spread(ffn_z, PLANE)

    vmem = pl.BlockSpec(memory_space=pltpu.VMEM)
    smem = pl.BlockSpec(memory_space=pltpu.SMEM)
    anywhere = pl.BlockSpec(memory_space=pltpu.HBM)
    core_index = core.astype(jnp.int32).reshape(1)
    half = WINS * WIN_PAD
    first = pl.pallas_call(
        attention_kernel,
        out_shape=jax.ShapeDtypeStruct((4 * QUAD_ROWS, D), BF16),
        in_specs=[smem, smem] + [vmem] * 7 + [anywhere] * 2,
        out_specs=vmem,
        scratch_shapes=[
            pltpu.VMEM((16, 32, 2048), BF16),
            pltpu.VMEM((half, D), BF16),
            pltpu.VMEM((half, D), BF16),
            pltpu.VMEM((half, D), BF16),
            pltpu.VMEM((768, D), BF16),
            pltpu.SemaphoreType.DMA((32,)),
        ],
        compiler_params=pltpu.CompilerParams(vmem_limit_bytes=24 * 1024 * 1024),
        cost_estimate=pl.CostEstimate(
            flops=20_000_000_000, bytes_accessed=20_000_000, transcendentals=1_000_000
        ),
        name="attention",
    )(
        core_index,
        head_scale,
        tall,
        bias,
        jnp.asarray(arrangement(), BF16),
        jnp.asarray(patch_selection(), BF16),
        jnp.asarray(selection(), BF16),
        attention_norm_gain.reshape(1, D),
        attention_norm_offset.reshape(1, D),
        attn_mine,
        attn_other,
    )
    first, ffn_mine = lax.optimization_barrier((first, ffn_mine))
    ffn_other = shifted(ffn_mine, "core", 1, True)
    return pl.pallas_call(
        feedforward_kernel,
        out_shape=jax.ShapeDtypeStruct((6, 18, 2 * D), BF16),
        in_specs=[smem] + [vmem] * 5 + [anywhere] * 3,
        out_specs=vmem,
        scratch_shapes=[
            pltpu.VMEM((16, 32, FFN), BF16),
            pltpu.VMEM((16, 128, D), BF16),
            pltpu.VMEM((16, 128, 2 * D), BF16),
            pltpu.SemaphoreType.DMA((32,)),
            pltpu.SemaphoreType.DMA((32,)),
            pltpu.SemaphoreType.DMA((32,)),
        ],
        compiler_params=pltpu.CompilerParams(vmem_limit_bytes=24 * 1024 * 1024),
        cost_estimate=pl.CostEstimate(
            flops=3_000_000_000, bytes_accessed=20_000_000, transcendentals=1_000_000
        ),
        name="feedforward",
    )(
        core_index,
        first,
        feedforward_norm_gain.reshape(1, D),
        feedforward_norm_offset.reshape(1, D),
        merging_norm_gain.reshape(1, 2 * D),
        merging_norm_offset.reshape(1, 2 * D),
        ffn_mine,
        ffn_other,
        merge_all,
    )


def solution(mesh):
    fine = Mesh(mesh.devices.reshape(2, 4, 16, 2, 2), ("y_hi", "x", "z", "y_lo", "core"))
    in_specs = (P(LAT, LON, None),) + (P(LON, None),) * 5 + (P(),) * 10
    return jax.shard_map(
        local, mesh=fine, in_specs=in_specs, out_specs=P(LAT, LON, None), check_vma=False
    )
```

```python
import jax
import jax.numpy as jnp
import numpy as np
from jax import lax
from jax.experimental import pallas as pl
from jax.experimental.pallas import tpu as pltpu
from jax.sharding import Mesh
from jax.sharding import PartitionSpec as P

D = 512
HEAD_COUNT = 8
WIN_ROWS = 6
WIN_COLS = 12
PAD_COLS = 16
SHIFT_ROWS = 3
SHIFT_COLS = 6
FFN = 2048
WIN_PAD = WIN_ROWS * PAD_COLS
KEY_PAD = 128
BANDS = 3
WINS = 4
QUAD_ROWS = 112
LAT = ("y_hi", "x")
LON = ("z", "y_lo", "core")
PLANE = ("y_hi", "x", "y_lo")
OFF = -1e30
BF16 = jnp.bfloat16
F32 = jnp.float32
QUERY_ROWS = ((48, 48), (0, 96), (0, 48))


def shifted(block, axes, by, wrap):
    size = lax.axis_size(axes)
    pairs = [(i, (i + by) % size) for i in range(size) if wrap or 0 <= i + by < size]
    return lax.ppermute(block, axes, pairs)


def spread(block, axes):
    size = lax.axis_size(axes)
    return lax.all_to_all(jnp.broadcast_to(block[None], (size,) + block.shape), axes, 0, 0)


def bias_entries(first_weight, first_bias, second_weight):
    span_rows = 2 * WIN_ROWS - 1
    span_cols = 2 * WIN_COLS - 1
    entry = np.arange(span_rows * span_cols)
    coordinates = np.stack(
        [
            (entry // span_cols - (WIN_ROWS - 1)) * (8.0 / (WIN_ROWS - 1)),
            (entry % span_cols - (WIN_COLS - 1)) * (8.0 / (WIN_COLS - 1)),
        ],
        axis=1,
    )
    coordinates = np.sign(coordinates) * np.log2(np.abs(coordinates) + 1.0) / 3.0
    coordinates = jnp.asarray(coordinates, F32)
    hidden = jax.nn.relu(
        coordinates[:, :1] * first_weight[:1] + coordinates[:, 1:] * first_weight[1:] + first_bias
    )
    return 16.0 * jax.nn.sigmoid(
        lax.dot_general(
            second_weight, hidden, (((0,), (1,)), ((), ())), precision=lax.Precision.HIGHEST
        )
    )


def bias_lookup():
    q = np.arange(WIN_PAD)
    k = np.arange(KEY_PAD)
    qa, qb = q // PAD_COLS, np.minimum(q % PAD_COLS, WIN_COLS - 1)
    ka, kb = np.minimum(k // PAD_COLS, WIN_ROWS - 1), np.minimum(k % PAD_COLS, WIN_COLS - 1)
    rows = qa[:, None] - ka[None] + WIN_ROWS - 1
    cols = qb[:, None] - kb[None] + WIN_COLS - 1
    return rows * (2 * WIN_COLS - 1) + cols


def unit_norm(triple, ones):
    rounded = triple.astype(BF16)
    exact = rounded.astype(F32)
    square = exact * exact
    high = square.astype(BF16)
    low = (square - high.astype(F32)).astype(BF16)
    parts = []
    for i in range(D // 256):
        cut = slice(i * 256, i * 256 + 256)
        total = jnp.dot(high[:, cut], ones, preferred_element_type=F32)
        total += jnp.dot(low[:, cut], ones, preferred_element_type=F32)
        parts.append((exact[:, cut] * lax.rsqrt(total + 1e-06)).astype(BF16))
    return parts


def norm_rows(values, gain, offset):
    average = jnp.mean(values, axis=-1, keepdims=True)
    centred = values - average
    variance = jnp.mean(centred * centred, axis=-1, keepdims=True)
    return centred * lax.rsqrt(variance + 1e-05) * gain + offset


def attention_kernel(
    core_ref,
    scale_ref,
    tall_ref,
    bias_ref,
    arrange_ref,
    patch_select_ref,
    select_ref,
    gain_ref,
    offset_ref,
    mine_ref,
    other_ref,
    out_ref,
    weight,
    queries,
    keys,
    values,
    heads,
    patch_select,
    select,
    sems,
):
    core = core_ref[0]
    copies = []
    for m in range(16):
        lat, y_lo = m // 2, m % 2
        for part, (ref, of) in enumerate(((mine_ref, core), (other_ref, 1 - core))):
            column = pl.multiple_of((lat * 2 + of) * 128, 128)
            copies.append(
                pltpu.make_async_copy(
                    ref.at[m],
                    weight.at[:, pl.ds(y_lo * 16, 16), pl.ds(column, 128)],
                    sems.at[m * 2 + part],
                )
            )
    late = [
        pltpu.make_async_copy(select_ref, select, sems.at[32]),
        pltpu.make_async_copy(patch_select_ref, patch_select, sems.at[33]),
    ]
    for copy in copies + late:
        copy.start()
    for copy in copies:
        copy.wait()

    row = lax.broadcasted_iota(jnp.int32, (256, 256), 0)
    lane = lax.broadcasted_iota(jnp.int32, (256, 256), 1)
    ones = jnp.where(row // 64 == lane // 64, 1.0, 0.0).astype(BF16)
    row2 = lax.broadcasted_iota(jnp.int32, (256, 128), 0)
    lane2 = lax.broadcasted_iota(jnp.int32, (256, 128), 1)
    counts = jnp.where((row2 >= 128) == (lane2 >= 64), 1.0, 0.0).astype(BF16)
    low_half = lax.broadcasted_iota(jnp.int32, (WIN_PAD, 128), 1) < 64
    zero = jnp.zeros((WIN_PAD, 128), BF16)
    gap = jnp.zeros((KEY_PAD - WIN_PAD, 128), BF16)

    def columns(start, width):
        return weight[:, :, start : start + width].reshape(D, width)

    def both(block):
        return jnp.concatenate(
            [jnp.where(low_half, block, zero), gap, jnp.where(low_half, zero, block), gap], axis=0
        )

    done = 0
    for band in range(BANDS):
        strip = tall_ref[band * WIN_ROWS : (band + 1) * WIN_ROWS].reshape(WIN_ROWS * 48, D)
        tokens = jnp.dot(arrange_ref[...], strip, preferred_element_type=F32).astype(BF16)
        for target, start in ((queries, 0), (keys, D)):
            total = jnp.dot(tokens, columns(start, D), preferred_element_type=F32)
            for i, part in enumerate(unit_norm(total, ones)):
                target[:, i * 256 : i * 256 + 256] = part
        values[...] = jnp.dot(tokens, columns(2 * D, D), preferred_element_type=F32).astype(BF16)
        first, count = QUERY_ROWS[band]

        def window(w, _, band=band, first=first, count=count, done=done):
            base = pl.multiple_of(w * WIN_PAD, WIN_PAD)
            for pair in range(HEAD_COUNT // 2):
                cut = slice(pair * 128, pair * 128 + 128)
                query = queries[pl.ds(base + first, count), cut]
                key = both(keys[pl.ds(base, WIN_PAD), cut])
                value = both(values[pl.ds(base, WIN_PAD), cut])
                scores = lax.dot_general(
                    query, key, (((1,), (1,)), ((), ())), preferred_element_type=F32
                )
                expo = []
                for h in range(2):
                    head = pair * 2 + h
                    one = scores[:, h * 128 : h * 128 + 128] * scale_ref[head]
                    one = one + bias_ref[band, head, first : first + count, :]
                    peak = jnp.max(one, axis=-1, keepdims=True)
                    expo.append(jnp.exp(one - peak).astype(BF16))
                mixed = jnp.dot(
                    jnp.concatenate(expo, axis=1),
                    jnp.concatenate([value, counts], axis=1),
                    preferred_element_type=F32,
                )
                place = pl.multiple_of(done + w * count, 16)
                heads[pl.ds(place, count), cut] = (mixed[:, :128] / mixed[:, 128:]).astype(BF16)
            return 0

        lax.fori_loop(0, WINS, window, 0)
        done += WINS * count

    for copy in late:
        copy.wait()
    own = jnp.dot(select[...], heads[...], preferred_element_type=F32).astype(BF16)
    projected = jnp.dot(own, columns(3 * D, D), preferred_element_type=F32)
    branch = norm_rows(projected, gain_ref[...], offset_ref[...]).astype(BF16)
    patches = jnp.dot(
        patch_select[...], tall_ref[...].reshape(18 * 48, D), preferred_element_type=F32
    )
    out_ref[...] = (patches + branch.astype(F32)).astype(BF16)


def feedforward_kernel(
    core_ref,
    first_ref,
    gain_ref,
    offset_ref,
    merge_gain_ref,
    merge_offset_ref,
    mine_ref,
    other_ref,
    out_ref,
    up,
    down,
    merge,
    tokens_in,
    up_sems,
    down_sems,
    merge_sems,
):
    core = core_ref[0]
    ups, downs, merges = [], [], []
    for m in range(16):
        y_hi, x, y_lo = m // 8, m // 2 % 4, m % 2
        for part, (ref, of) in enumerate(((mine_ref, core), (other_ref, 1 - core))):
            column = pl.multiple_of((m // 2 * 2 + of) * 128, 128)
            ups.append(
                pltpu.make_async_copy(
                    ref.at[m, :, pl.ds(0, 16), :],
                    up.at[:, pl.ds(y_lo * 16, 16), pl.ds(column, 128)],
                    up_sems.at[m * 2 + part],
                )
            )
            start = pl.multiple_of(y_lo * 64 + of * 32 + y_hi * 16, 16)
            downs.append(
                pltpu.make_async_copy(
                    ref.at[m, :, pl.ds(16, 16), :],
                    down.at[:, pl.ds(start, 16), pl.ds(x * 128, 128)],
                    down_sems.at[m * 2 + part],
                )
            )
            start = pl.multiple_of(y_lo * 64 + of * 32, 32)
            merges.append(
                pltpu.make_async_copy(
                    ref.at[m, :, pl.ds(32, 32), :],
                    merge.at[:, pl.ds(start, 32), pl.ds(m // 2 * 128, 128)],
                    merge_sems.at[m * 2 + part],
                )
            )
    ups.append(pltpu.make_async_copy(first_ref, tokens_in, up_sems.at[32]))
    for copy in ups + downs + merges:
        copy.start()
    for copy in ups:
        copy.wait()
    tokens = tokens_in[...]
    total = None
    for n in range(FFN // 512):
        cut = slice(n * 512, n * 512 + 512)
        hidden = jnp.dot(tokens, up[:, :, cut].reshape(D, 512), preferred_element_type=F32)
        hidden = (0.5 * hidden * (1.0 + lax.erf(hidden * (0.5**0.5)))).astype(BF16)
        if n == 0:
            for copy in downs:
                copy.wait()
        piece = jnp.dot(
            hidden, down[n * 4 : n * 4 + 4].reshape(512, D), preferred_element_type=F32
        )
        total = piece if total is None else total + piece
    branch = norm_rows(total, gain_ref[...], offset_ref[...])
    second = (tokens.astype(F32) + branch).astype(BF16)
    for copy in merges:
        copy.wait()
    total = None
    for n in range(4):
        piece = jnp.dot(
            second[n * QUAD_ROWS : (n + 1) * QUAD_ROWS],
            merge[n * 4 : n * 4 + 4].reshape(512, 2 * D),
            preferred_element_type=F32,
        )
        total = piece if total is None else total + piece
    reduced = norm_rows(total, merge_gain_ref[...], merge_offset_ref[...])
    for i in range(6):
        out_ref[i] = reduced[i * 18 : i * 18 + 18].astype(BF16)


def quads_order(place):
    order = place.reshape(6, 2, 18, 2).transpose(3, 1, 0, 2).reshape(4, 108)
    return np.pad(order, ((0, 0), (0, QUAD_ROWS - 108)), constant_values=-1).reshape(-1)


def one_hot_rows(order, size):
    return (order[:, None] == np.arange(size)[None]).astype(np.float32)


def selection():
    place = np.full((12, 36), -1)
    done = 0
    for band in range(BANDS):
        first, count = QUERY_ROWS[band]
        for w in range(WINS):
            for r in range(count):
                a, b = (first + r) // PAD_COLS, (first + r) % PAD_COLS
                i = band * WIN_ROWS + a - SHIFT_ROWS
                j = w * WIN_COLS + b - SHIFT_COLS
                if b < WIN_COLS and 0 <= j < 36:
                    place[i, j] = done + r
            done += count
    return one_hot_rows(quads_order(place), done)


def patch_selection():
    i, j = np.arange(12)[:, None] + SHIFT_ROWS, np.arange(36)[None] + SHIFT_COLS
    return one_hot_rows(quads_order(i * 48 + j), 18 * 48)


def arrangement():
    r = np.arange(WINS * WIN_PAD)
    w, a, b = r // WIN_PAD, r % WIN_PAD // PAD_COLS, r % PAD_COLS
    return one_hot_rows(np.where(b < WIN_COLS, a * 48 + w * WIN_COLS + b, -1), WIN_ROWS * 48)


def local(
    patches,
    query_key_value_weight,
    attention_output_weight,
    feedforward_in_weight,
    feedforward_out_weight,
    merging_reduction_weight,
    head_scale_logarithm,
    bias_network_first_weight,
    bias_network_first_bias,
    bias_network_second_weight,
    attention_norm_gain,
    attention_norm_offset,
    feedforward_norm_gain,
    feedforward_norm_offset,
    merging_norm_gain,
    merging_norm_offset,
):
    lat = lax.axis_index(LAT)
    core = lax.axis_index("core")
    x = lax.axis_index("x")

    mine = jnp.concatenate(
        [query_key_value_weight, attention_output_weight, feedforward_in_weight], axis=1
    )
    theirs = shifted(mine, "core", 1, True)
    rows = jnp.concatenate(
        [jnp.where(core == 0, mine, theirs), jnp.where(core == 0, theirs, mine)], axis=0
    )
    at = (lat * 2 + core) * 128
    units = jnp.concatenate(
        [
            lax.dynamic_slice(rows, (0, at), (16, 128)),
            lax.dynamic_slice(rows, (0, 2048 + at), (16, 128)),
            lax.dynamic_slice(
                feedforward_out_weight, (lax.axis_index("y_hi") * 16, x * 128), (16, 128)
            ),
            lax.dynamic_slice(merging_reduction_weight, (0, lat * 128), (32, 128)),
        ]
    )

    east = shifted(patches[:, :SHIFT_COLS], LON, -1, True)
    west = shifted(patches[:, 36 - SHIFT_COLS :], LON, 1, True)
    wide = jnp.concatenate([west, patches, east], axis=1)
    units, wide = lax.optimization_barrier((units, wide))
    along_z = spread(units, "z")
    south = shifted(wide[:SHIFT_ROWS], LAT, -1, False)
    north = shifted(wide[12 - SHIFT_ROWS :], LAT, 1, False)
    tall = jnp.concatenate([north, wide, south], axis=0)

    along_z, tall = lax.optimization_barrier((along_z, tall))
    attn_mine = spread(along_z[:, :16], PLANE)

    table = bias_entries(
        bias_network_first_weight, bias_network_first_bias, bias_network_second_weight
    )
    lookup = bias_lookup()
    entries = table.shape[1]
    one_hot = (
        jnp.asarray(lookup.reshape(-1), jnp.int32)[None, :]
        == jnp.arange(entries, dtype=jnp.int32)[:, None]
    ).astype(F32)
    bias = jnp.dot(table, one_hot, precision=lax.Precision.HIGHEST)
    bias = bias.reshape(HEAD_COUNT, WIN_PAD, KEY_PAD)
    key = np.arange(KEY_PAD)
    held = (key < WIN_PAD) & (key % PAD_COLS < WIN_COLS)
    bias = jnp.where(jnp.asarray(held), bias, OFF)
    apart = (np.arange(WIN_PAD)[:, None] // 48) != (key[None] // 48)
    seam = jnp.stack([lat == 0, jnp.bool_(False), lat == 7])
    bias = jnp.where(seam[:, None, None, None] & jnp.asarray(apart), OFF, bias[None])
    head_scale = jnp.exp(jnp.minimum(head_scale_logarithm, jnp.log(100.0)))

    attn_mine, along_z, bias = lax.optimization_barrier((attn_mine, along_z, bias))
    attn_other = shifted(attn_mine, "core", 1, True)
    rest_mine = spread(along_z[:, 16:], PLANE)

    vmem = pl.BlockSpec(memory_space=pltpu.VMEM)
    smem = pl.BlockSpec(memory_space=pltpu.SMEM)
    hbm = pl.BlockSpec(memory_space=pltpu.HBM)
    anywhere = pl.BlockSpec(memory_space=pl.ANY)

    def far(block):
        return pltpu.with_memory_space_constraint(block, pltpu.HBM)

    params = pltpu.CompilerParams(vmem_limit_bytes=24 * 1024 * 1024)
    core_index = core.astype(jnp.int32).reshape(1)
    half = WINS * WIN_PAD
    first = pl.pallas_call(
        attention_kernel,
        out_shape=jax.ShapeDtypeStruct((4 * QUAD_ROWS, D), BF16),
        in_specs=[smem, smem] + [vmem] * 3 + [hbm] * 2 + [vmem] * 2 + [anywhere] * 2,
        out_specs=vmem,
        scratch_shapes=[
            pltpu.VMEM((16, 32, 2048), BF16),
            pltpu.VMEM((half, D), BF16),
            pltpu.VMEM((half, D), BF16),
            pltpu.VMEM((half, D), BF16),
            pltpu.VMEM((768, D), BF16),
            pltpu.VMEM((4 * QUAD_ROWS, 864), BF16),
            pltpu.VMEM((4 * QUAD_ROWS, 768), BF16),
            pltpu.SemaphoreType.DMA((34,)),
        ],
        compiler_params=params,
        cost_estimate=pl.CostEstimate(
            flops=20_000_000_000, bytes_accessed=20_000_000, transcendentals=1_000_000
        ),
        name="attention",
    )(
        core_index,
        head_scale,
        tall,
        bias,
        jnp.asarray(arrangement(), BF16),
        far(jnp.asarray(patch_selection(), BF16)),
        far(jnp.asarray(selection(), BF16)),
        attention_norm_gain.reshape(1, D),
        attention_norm_offset.reshape(1, D),
        attn_mine,
        attn_other,
    )
    first, rest_mine = lax.optimization_barrier((first, rest_mine))
    rest_other = shifted(rest_mine, "core", 1, True)
    return pl.pallas_call(
        feedforward_kernel,
        out_shape=jax.ShapeDtypeStruct((6, 18, 2 * D), BF16),
        in_specs=[smem, hbm] + [vmem] * 4 + [anywhere] * 2,
        out_specs=vmem,
        scratch_shapes=[
            pltpu.VMEM((16, 32, FFN), BF16),
            pltpu.VMEM((16, 128, D), BF16),
            pltpu.VMEM((16, 128, 2 * D), BF16),
            pltpu.VMEM((4 * QUAD_ROWS, D), BF16),
            pltpu.SemaphoreType.DMA((33,)),
            pltpu.SemaphoreType.DMA((32,)),
            pltpu.SemaphoreType.DMA((32,)),
        ],
        compiler_params=params,
        cost_estimate=pl.CostEstimate(
            flops=6_000_000_000, bytes_accessed=20_000_000, transcendentals=1_000_000
        ),
        name="feedforward",
    )(
        core_index,
        far(first),
        feedforward_norm_gain.reshape(1, D),
        feedforward_norm_offset.reshape(1, D),
        merging_norm_gain.reshape(1, 2 * D),
        merging_norm_offset.reshape(1, 2 * D),
        rest_mine,
        rest_other,
    )


def solution(mesh):
    fine = Mesh(mesh.devices.reshape(2, 4, 16, 2, 2), ("y_hi", "x", "z", "y_lo", "core"))
    in_specs = (P(LAT, LON, None),) + (P(LON, None),) * 5 + (P(),) * 10
    return jax.shard_map(
        local, mesh=fine, in_specs=in_specs, out_specs=P(LAT, LON, None), check_vma=False
    )
```

```python
import jax
import jax.numpy as jnp
import numpy as np
from jax import lax
from jax.experimental import pallas as pl
from jax.experimental.pallas import tpu as pltpu
from jax.sharding import Mesh
from jax.sharding import PartitionSpec as P

D = 512
HEAD_COUNT = 8
WIN_ROWS = 6
WIN_COLS = 12
PAD_COLS = 16
SHIFT_ROWS = 3
SHIFT_COLS = 6
FFN = 2048
WIN_PAD = WIN_ROWS * PAD_COLS
KEY_PAD = 128
BANDS = 3
WINS = 4
QUAD_ROWS = 112
LAT = ("y_hi", "x")
LON = ("z", "y_lo", "core")
ALL = ("y_hi", "x", "z", "y_lo", "core")
OFF = -1e30
BF16 = jnp.bfloat16
F32 = jnp.float32
QUERY_ROWS = ((48, 48), (0, 96), (0, 48))


def shifted(block, axes, by, wrap):
    size = lax.axis_size(axes)
    pairs = [(i, (i + by) % size) for i in range(size) if wrap or 0 <= i + by < size]
    return lax.ppermute(block, axes, pairs)


def spread(block, axes):
    size = lax.axis_size(axes)
    return lax.all_to_all(jnp.broadcast_to(block[None], (size,) + block.shape), axes, 0, 0)


def rings(x_core):
    ids = np.arange(512).reshape(2, 4, 16, 2, 2)
    along_x = ids.transpose(0, 2, 3, 4, 1)[:, :, :, x_core].reshape(-1, 4)
    along_y = ids.transpose(1, 2, 4, 0, 3)[:, :, 1 - x_core].reshape(-1, 4)
    return np.concatenate([along_x, along_y]).tolist()


def spread_ring(block, x_core):
    copies = jnp.broadcast_to(block[None], (4,) + block.shape)
    return lax.all_to_all(copies, ALL, 0, 0, axis_index_groups=rings(x_core))


def place(m, of):
    outer, inner = m // 4, m % 4

    def pick(on_first, on_second):
        return on_first + of * (on_second - on_first)

    return pick(outer // 2, inner // 2), pick(inner, outer), pick(outer % 2, inner % 2)


def bias_entries(first_weight, first_bias, second_weight):
    span_rows = 2 * WIN_ROWS - 1
    span_cols = 2 * WIN_COLS - 1
    entry = np.arange(span_rows * span_cols)
    coordinates = np.stack(
        [
            (entry // span_cols - (WIN_ROWS - 1)) * (8.0 / (WIN_ROWS - 1)),
            (entry % span_cols - (WIN_COLS - 1)) * (8.0 / (WIN_COLS - 1)),
        ],
        axis=1,
    )
    coordinates = np.sign(coordinates) * np.log2(np.abs(coordinates) + 1.0) / 3.0
    coordinates = jnp.asarray(coordinates, F32)
    hidden = jax.nn.relu(
        coordinates[:, :1] * first_weight[:1] + coordinates[:, 1:] * first_weight[1:] + first_bias
    )
    return 16.0 * jax.nn.sigmoid(
        lax.dot_general(
            second_weight, hidden, (((0,), (1,)), ((), ())), precision=lax.Precision.HIGHEST
        )
    )


def bias_lookup():
    q = np.arange(WIN_PAD)
    k = np.arange(KEY_PAD)
    qa, qb = q // PAD_COLS, np.minimum(q % PAD_COLS, WIN_COLS - 1)
    ka, kb = np.minimum(k // PAD_COLS, WIN_ROWS - 1), np.minimum(k % PAD_COLS, WIN_COLS - 1)
    rows = qa[:, None] - ka[None] + WIN_ROWS - 1
    cols = qb[:, None] - kb[None] + WIN_COLS - 1
    return rows * (2 * WIN_COLS - 1) + cols


def unit_norm(triple, ones):
    rounded = triple.astype(BF16)
    exact = rounded.astype(F32)
    square = exact * exact
    high = square.astype(BF16)
    low = (square - high.astype(F32)).astype(BF16)
    parts = []
    for i in range(D // 256):
        cut = slice(i * 256, i * 256 + 256)
        total = jnp.dot(high[:, cut], ones, preferred_element_type=F32)
        total += jnp.dot(low[:, cut], ones, preferred_element_type=F32)
        parts.append((exact[:, cut] * lax.rsqrt(total + 1e-06)).astype(BF16))
    return parts


def norm_rows(values, gain, offset):
    average = jnp.mean(values, axis=-1, keepdims=True)
    centred = values - average
    variance = jnp.mean(centred * centred, axis=-1, keepdims=True)
    return centred * lax.rsqrt(variance + 1e-05) * gain + offset


def attention_kernel(
    core_ref,
    scale_ref,
    tall_ref,
    bias_ref,
    arrange_ref,
    patch_select_ref,
    select_ref,
    gain_ref,
    offset_ref,
    mine_ref,
    other_ref,
    out_ref,
    weight,
    queries,
    keys,
    values,
    heads,
    patch_select,
    select,
    sems,
):
    core = core_ref[0]
    copies = []
    for m in range(16):
        for part, (ref, of) in enumerate(((mine_ref, core), (other_ref, 1 - core))):
            y_hi, x, y_lo = place(m, of)
            row = pl.multiple_of(y_lo * 16, 16)
            column = pl.multiple_of((y_hi * 8 + x * 2 + of) * 128, 128)
            copies.append(
                pltpu.make_async_copy(
                    ref.at[m],
                    weight.at[:, pl.ds(row, 16), pl.ds(column, 128)],
                    sems.at[m * 2 + part],
                )
            )
    late = [
        pltpu.make_async_copy(select_ref, select, sems.at[32]),
        pltpu.make_async_copy(patch_select_ref, patch_select, sems.at[33]),
    ]
    for copy in copies + late:
        copy.start()
    for copy in copies:
        copy.wait()

    row = lax.broadcasted_iota(jnp.int32, (256, 256), 0)
    lane = lax.broadcasted_iota(jnp.int32, (256, 256), 1)
    ones = jnp.where(row // 64 == lane // 64, 1.0, 0.0).astype(BF16)
    row2 = lax.broadcasted_iota(jnp.int32, (256, 128), 0)
    lane2 = lax.broadcasted_iota(jnp.int32, (256, 128), 1)
    counts = jnp.where((row2 >= 128) == (lane2 >= 64), 1.0, 0.0).astype(BF16)
    low_half = lax.broadcasted_iota(jnp.int32, (WIN_PAD, 128), 1) < 64
    zero = jnp.zeros((WIN_PAD, 128), BF16)
    gap = jnp.zeros((KEY_PAD - WIN_PAD, 128), BF16)

    def columns(start, width):
        return weight[:, :, start : start + width].reshape(D, width)

    def both(block):
        return jnp.concatenate(
            [jnp.where(low_half, block, zero), gap, jnp.where(low_half, zero, block), gap], axis=0
        )

    done = 0
    for band in range(BANDS):
        strip = tall_ref[band * WIN_ROWS : (band + 1) * WIN_ROWS].reshape(WIN_ROWS * 48, D)
        tokens = jnp.dot(arrange_ref[...], strip, preferred_element_type=F32).astype(BF16)
        for target, start in ((queries, 0), (keys, D)):
            total = jnp.dot(tokens, columns(start, D), preferred_element_type=F32)
            for i, part in enumerate(unit_norm(total, ones)):
                target[:, i * 256 : i * 256 + 256] = part
        values[...] = jnp.dot(tokens, columns(2 * D, D), preferred_element_type=F32).astype(BF16)
        first, count = QUERY_ROWS[band]

        def window(w, _, band=band, first=first, count=count, done=done):
            base = pl.multiple_of(w * WIN_PAD, WIN_PAD)
            for pair in range(HEAD_COUNT // 2):
                cut = slice(pair * 128, pair * 128 + 128)
                query = queries[pl.ds(base + first, count), cut]
                key = both(keys[pl.ds(base, WIN_PAD), cut])
                value = both(values[pl.ds(base, WIN_PAD), cut])
                scores = lax.dot_general(
                    query, key, (((1,), (1,)), ((), ())), preferred_element_type=F32
                )
                expo = []
                for h in range(2):
                    head = pair * 2 + h
                    one = scores[:, h * 128 : h * 128 + 128] * scale_ref[head]
                    one = one + bias_ref[band, head, first : first + count, :]
                    peak = jnp.max(one, axis=-1, keepdims=True)
                    expo.append(jnp.exp(one - peak).astype(BF16))
                mixed = jnp.dot(
                    jnp.concatenate(expo, axis=1),
                    jnp.concatenate([value, counts], axis=1),
                    preferred_element_type=F32,
                )
                place = pl.multiple_of(done + w * count, 16)
                heads[pl.ds(place, count), cut] = (mixed[:, :128] / mixed[:, 128:]).astype(BF16)
            return 0

        lax.fori_loop(0, WINS, window, 0)
        done += WINS * count

    for copy in late:
        copy.wait()
    own = jnp.dot(select[...], heads[...], preferred_element_type=F32).astype(BF16)
    projected = jnp.dot(own, columns(3 * D, D), preferred_element_type=F32)
    branch = norm_rows(projected, gain_ref[...], offset_ref[...]).astype(BF16)
    patches = jnp.dot(
        patch_select[...], tall_ref[...].reshape(18 * 48, D), preferred_element_type=F32
    )
    out_ref[...] = (patches + branch.astype(F32)).astype(BF16)


def feedforward_kernel(
    core_ref,
    first_ref,
    gain_ref,
    offset_ref,
    merge_gain_ref,
    merge_offset_ref,
    mine_ref,
    other_ref,
    out_ref,
    up,
    down,
    merge,
    tokens_in,
    up_sems,
    down_sems,
    merge_sems,
):
    core = core_ref[0]
    ups, downs, merges = [], [], []
    for m in range(16):
        for part, (ref, of) in enumerate(((mine_ref, core), (other_ref, 1 - core))):
            y_hi, x, y_lo = place(m, of)
            row = pl.multiple_of(y_lo * 16, 16)
            column = pl.multiple_of((y_hi * 8 + x * 2 + of) * 128, 128)
            ups.append(
                pltpu.make_async_copy(
                    ref.at[m, :, pl.ds(0, 16), :],
                    up.at[:, pl.ds(row, 16), pl.ds(column, 128)],
                    up_sems.at[m * 2 + part],
                )
            )
            row = pl.multiple_of(y_lo * 64 + of * 32 + y_hi * 16, 16)
            column = pl.multiple_of(x * 128, 128)
            downs.append(
                pltpu.make_async_copy(
                    ref.at[m, :, pl.ds(16, 16), :],
                    down.at[:, pl.ds(row, 16), pl.ds(column, 128)],
                    down_sems.at[m * 2 + part],
                )
            )
            row = pl.multiple_of(y_lo * 64 + of * 32, 32)
            column = pl.multiple_of((y_hi * 4 + x) * 128, 128)
            merges.append(
                pltpu.make_async_copy(
                    ref.at[m, :, pl.ds(32, 32), :],
                    merge.at[:, pl.ds(row, 32), pl.ds(column, 128)],
                    merge_sems.at[m * 2 + part],
                )
            )
    ups.append(pltpu.make_async_copy(first_ref, tokens_in, up_sems.at[32]))
    for copy in ups + downs + merges:
        copy.start()
    for copy in ups:
        copy.wait()
    tokens = tokens_in[...]
    total = None
    for n in range(FFN // 512):
        cut = slice(n * 512, n * 512 + 512)
        hidden = jnp.dot(tokens, up[:, :, cut].reshape(D, 512), preferred_element_type=F32)
        hidden = (0.5 * hidden * (1.0 + lax.erf(hidden * (0.5**0.5)))).astype(BF16)
        if n == 0:
            for copy in downs:
                copy.wait()
        piece = jnp.dot(
            hidden, down[n * 4 : n * 4 + 4].reshape(512, D), preferred_element_type=F32
        )
        total = piece if total is None else total + piece
    branch = norm_rows(total, gain_ref[...], offset_ref[...])
    second = (tokens.astype(F32) + branch).astype(BF16)
    for copy in merges:
        copy.wait()
    total = None
    for n in range(4):
        piece = jnp.dot(
            second[n * QUAD_ROWS : (n + 1) * QUAD_ROWS],
            merge[n * 4 : n * 4 + 4].reshape(512, 2 * D),
            preferred_element_type=F32,
        )
        total = piece if total is None else total + piece
    reduced = norm_rows(total, merge_gain_ref[...], merge_offset_ref[...])
    for i in range(6):
        out_ref[i] = reduced[i * 18 : i * 18 + 18].astype(BF16)


def quads_order(place):
    order = place.reshape(6, 2, 18, 2).transpose(3, 1, 0, 2).reshape(4, 108)
    return np.pad(order, ((0, 0), (0, QUAD_ROWS - 108)), constant_values=-1).reshape(-1)


def one_hot_rows(order, size):
    return (order[:, None] == np.arange(size)[None]).astype(np.float32)


def selection():
    place = np.full((12, 36), -1)
    done = 0
    for band in range(BANDS):
        first, count = QUERY_ROWS[band]
        for w in range(WINS):
            for r in range(count):
                a, b = (first + r) // PAD_COLS, (first + r) % PAD_COLS
                i = band * WIN_ROWS + a - SHIFT_ROWS
                j = w * WIN_COLS + b - SHIFT_COLS
                if b < WIN_COLS and 0 <= j < 36:
                    place[i, j] = done + r
            done += count
    return one_hot_rows(quads_order(place), done)


def patch_selection():
    i, j = np.arange(12)[:, None] + SHIFT_ROWS, np.arange(36)[None] + SHIFT_COLS
    return one_hot_rows(quads_order(i * 48 + j), 18 * 48)


def arrangement():
    r = np.arange(WINS * WIN_PAD)
    w, a, b = r // WIN_PAD, r % WIN_PAD // PAD_COLS, r % PAD_COLS
    return one_hot_rows(np.where(b < WIN_COLS, a * 48 + w * WIN_COLS + b, -1), WIN_ROWS * 48)


def local(
    patches,
    query_key_value_weight,
    attention_output_weight,
    feedforward_in_weight,
    feedforward_out_weight,
    merging_reduction_weight,
    head_scale_logarithm,
    bias_network_first_weight,
    bias_network_first_bias,
    bias_network_second_weight,
    attention_norm_gain,
    attention_norm_offset,
    feedforward_norm_gain,
    feedforward_norm_offset,
    merging_norm_gain,
    merging_norm_offset,
):
    lat = lax.axis_index(LAT)
    core = lax.axis_index("core")
    x = lax.axis_index("x")

    mine = jnp.concatenate(
        [query_key_value_weight, attention_output_weight, feedforward_in_weight], axis=1
    )
    theirs = shifted(mine, "core", 1, True)
    rows = jnp.concatenate(
        [jnp.where(core == 0, mine, theirs), jnp.where(core == 0, theirs, mine)], axis=0
    )
    at = (lat * 2 + core) * 128
    units = jnp.concatenate(
        [
            lax.dynamic_slice(rows, (0, at), (16, 128)),
            lax.dynamic_slice(rows, (0, 2048 + at), (16, 128)),
            lax.dynamic_slice(
                feedforward_out_weight, (lax.axis_index("y_hi") * 16, x * 128), (16, 128)
            ),
            lax.dynamic_slice(merging_reduction_weight, (0, lat * 128), (32, 128)),
        ]
    )

    east = shifted(patches[:, :SHIFT_COLS], LON, -1, True)
    west = shifted(patches[:, 36 - SHIFT_COLS :], LON, 1, True)
    wide = jnp.concatenate([west, patches, east], axis=1)
    units, wide = lax.optimization_barrier((units, wide))
    along_z = spread(units, "z")
    south = shifted(wide[:SHIFT_ROWS], LAT, -1, False)
    north = shifted(wide[12 - SHIFT_ROWS :], LAT, 1, False)
    tall = jnp.concatenate([north, wide, south], axis=0)

    along_z, tall = lax.optimization_barrier((along_z, tall))
    in_ring = spread_ring(along_z, 0)
    attn_mine = spread_ring(in_ring[:, :, :16], 1).reshape(16, 16, 16, 128)

    table = bias_entries(
        bias_network_first_weight, bias_network_first_bias, bias_network_second_weight
    )
    lookup = bias_lookup()
    entries = table.shape[1]
    one_hot = (
        jnp.asarray(lookup.reshape(-1), jnp.int32)[None, :]
        == jnp.arange(entries, dtype=jnp.int32)[:, None]
    ).astype(F32)
    bias = jnp.dot(table, one_hot, precision=lax.Precision.HIGHEST)
    bias = bias.reshape(HEAD_COUNT, WIN_PAD, KEY_PAD)
    key = np.arange(KEY_PAD)
    held = (key < WIN_PAD) & (key % PAD_COLS < WIN_COLS)
    bias = jnp.where(jnp.asarray(held), bias, OFF)
    apart = (np.arange(WIN_PAD)[:, None] // 48) != (key[None] // 48)
    seam = jnp.stack([lat == 0, jnp.bool_(False), lat == 7])
    bias = jnp.where(seam[:, None, None, None] & jnp.asarray(apart), OFF, bias[None])
    head_scale = jnp.exp(jnp.minimum(head_scale_logarithm, jnp.log(100.0)))

    attn_mine, in_ring, bias = lax.optimization_barrier((attn_mine, in_ring, bias))
    attn_other = shifted(attn_mine, "core", 1, True)
    rest_mine = spread_ring(in_ring[:, :, 16:], 1).reshape(16, 16, 64, 128)

    vmem = pl.BlockSpec(memory_space=pltpu.VMEM)
    smem = pl.BlockSpec(memory_space=pltpu.SMEM)
    hbm = pl.BlockSpec(memory_space=pltpu.HBM)
    anywhere = pl.BlockSpec(memory_space=pl.ANY)

    def far(block):
        return pltpu.with_memory_space_constraint(block, pltpu.HBM)

    params = pltpu.CompilerParams(vmem_limit_bytes=24 * 1024 * 1024)
    core_index = core.astype(jnp.int32).reshape(1)
    half = WINS * WIN_PAD
    first = pl.pallas_call(
        attention_kernel,
        out_shape=jax.ShapeDtypeStruct((4 * QUAD_ROWS, D), BF16),
        in_specs=[smem, smem] + [vmem] * 3 + [hbm] * 2 + [vmem] * 2 + [anywhere] * 2,
        out_specs=vmem,
        scratch_shapes=[
            pltpu.VMEM((16, 32, 2048), BF16),
            pltpu.VMEM((half, D), BF16),
            pltpu.VMEM((half, D), BF16),
            pltpu.VMEM((half, D), BF16),
            pltpu.VMEM((768, D), BF16),
            pltpu.VMEM((4 * QUAD_ROWS, 864), BF16),
            pltpu.VMEM((4 * QUAD_ROWS, 768), BF16),
            pltpu.SemaphoreType.DMA((34,)),
        ],
        compiler_params=params,
        cost_estimate=pl.CostEstimate(
            flops=20_000_000_000, bytes_accessed=20_000_000, transcendentals=1_000_000
        ),
        name="attention",
    )(
        core_index,
        head_scale,
        tall,
        bias,
        jnp.asarray(arrangement(), BF16),
        far(jnp.asarray(patch_selection(), BF16)),
        far(jnp.asarray(selection(), BF16)),
        attention_norm_gain.reshape(1, D),
        attention_norm_offset.reshape(1, D),
        attn_mine,
        attn_other,
    )
    first, rest_mine = lax.optimization_barrier((first, rest_mine))
    rest_other = shifted(rest_mine, "core", 1, True)
    return pl.pallas_call(
        feedforward_kernel,
        out_shape=jax.ShapeDtypeStruct((6, 18, 2 * D), BF16),
        in_specs=[smem, hbm] + [vmem] * 4 + [anywhere] * 2,
        out_specs=vmem,
        scratch_shapes=[
            pltpu.VMEM((16, 32, FFN), BF16),
            pltpu.VMEM((16, 128, D), BF16),
            pltpu.VMEM((16, 128, 2 * D), BF16),
            pltpu.VMEM((4 * QUAD_ROWS, D), BF16),
            pltpu.SemaphoreType.DMA((33,)),
            pltpu.SemaphoreType.DMA((32,)),
            pltpu.SemaphoreType.DMA((32,)),
        ],
        compiler_params=params,
        cost_estimate=pl.CostEstimate(
            flops=6_000_000_000, bytes_accessed=20_000_000, transcendentals=1_000_000
        ),
        name="feedforward",
    )(
        core_index,
        far(first),
        feedforward_norm_gain.reshape(1, D),
        feedforward_norm_offset.reshape(1, D),
        merging_norm_gain.reshape(1, 2 * D),
        merging_norm_offset.reshape(1, 2 * D),
        rest_mine,
        rest_other,
    )


def solution(mesh):
    fine = Mesh(mesh.devices.reshape(2, 4, 16, 2, 2), ("y_hi", "x", "z", "y_lo", "core"))
    in_specs = (P(LAT, LON, None),) + (P(LON, None),) * 5 + (P(),) * 10
    return jax.shard_map(
        local, mesh=fine, in_specs=in_specs, out_specs=P(LAT, LON, None), check_vma=False
    )
```

```python
import jax
import jax.numpy as jnp
import numpy as np
from jax import lax
from jax.experimental import pallas as pl
from jax.experimental.pallas import tpu as pltpu
from jax.sharding import Mesh
from jax.sharding import PartitionSpec as P

D = 512
HEAD_COUNT = 8
WIN_ROWS = 6
WIN_COLS = 12
PAD_COLS = 16
SHIFT_ROWS = 3
SHIFT_COLS = 6
FFN = 2048
WIN_PAD = WIN_ROWS * PAD_COLS
KEY_PAD = 128
BANDS = 3
WINS = 4
QUAD_ROWS = 112
LAT = ("y_hi", "x")
LON = ("z", "y_lo", "core")
ALL = ("y_hi", "x", "z", "y_lo", "core")
OFF = -1e30
BF16 = jnp.bfloat16
F32 = jnp.float32
QUERY_ROWS = ((48, 48), (0, 96), (0, 48))


def shifted(block, axes, by, wrap):
    size = lax.axis_size(axes)
    pairs = [(i, (i + by) % size) for i in range(size) if wrap or 0 <= i + by < size]
    return lax.ppermute(block, axes, pairs)


def spread(block, axes):
    size = lax.axis_size(axes)
    return lax.all_to_all(jnp.broadcast_to(block[None], (size,) + block.shape), axes, 0, 0)


def rings(x_core):
    ids = np.arange(512).reshape(2, 4, 16, 2, 2)
    along_x = ids.transpose(0, 2, 3, 4, 1)[:, :, :, x_core].reshape(-1, 4)
    along_y = ids.transpose(1, 2, 4, 0, 3)[:, :, 1 - x_core].reshape(-1, 4)
    return np.concatenate([along_x, along_y]).tolist()


def four(block):
    return jnp.broadcast_to(block[None], (4,) + block.shape)


def spread_ring(copies, x_core):
    return lax.all_to_all(copies, ALL, 0, 0, axis_index_groups=rings(x_core))


def place(m, of):
    outer, inner = m // 4, m % 4

    def pick(on_first, on_second):
        return on_first + of * (on_second - on_first)

    return pick(outer // 2, inner // 2), pick(inner, outer), pick(outer % 2, inner % 2)


def bias_entries(first_weight, first_bias, second_weight):
    span_rows = 2 * WIN_ROWS - 1
    span_cols = 2 * WIN_COLS - 1
    entry = np.arange(span_rows * span_cols)
    coordinates = np.stack(
        [
            (entry // span_cols - (WIN_ROWS - 1)) * (8.0 / (WIN_ROWS - 1)),
            (entry % span_cols - (WIN_COLS - 1)) * (8.0 / (WIN_COLS - 1)),
        ],
        axis=1,
    )
    coordinates = np.sign(coordinates) * np.log2(np.abs(coordinates) + 1.0) / 3.0
    coordinates = jnp.asarray(coordinates, F32)
    hidden = jax.nn.relu(
        coordinates[:, :1] * first_weight[:1] + coordinates[:, 1:] * first_weight[1:] + first_bias
    )
    return 16.0 * jax.nn.sigmoid(
        lax.dot_general(
            second_weight, hidden, (((0,), (1,)), ((), ())), precision=lax.Precision.HIGHEST
        )
    )


def bias_lookup():
    q = np.arange(WIN_PAD)
    k = np.arange(KEY_PAD)
    qa, qb = q // PAD_COLS, np.minimum(q % PAD_COLS, WIN_COLS - 1)
    ka, kb = np.minimum(k // PAD_COLS, WIN_ROWS - 1), np.minimum(k % PAD_COLS, WIN_COLS - 1)
    rows = qa[:, None] - ka[None] + WIN_ROWS - 1
    cols = qb[:, None] - kb[None] + WIN_COLS - 1
    return rows * (2 * WIN_COLS - 1) + cols


def unit_norm(triple, ones):
    rounded = triple.astype(BF16)
    exact = rounded.astype(F32)
    square = exact * exact
    high = square.astype(BF16)
    low = (square - high.astype(F32)).astype(BF16)
    parts = []
    for i in range(D // 256):
        cut = slice(i * 256, i * 256 + 256)
        total = jnp.dot(high[:, cut], ones, preferred_element_type=F32)
        total += jnp.dot(low[:, cut], ones, preferred_element_type=F32)
        parts.append((exact[:, cut] * lax.rsqrt(total + 1e-06)).astype(BF16))
    return parts


def norm_rows(values, gain, offset):
    average = jnp.mean(values, axis=-1, keepdims=True)
    centred = values - average
    variance = jnp.mean(centred * centred, axis=-1, keepdims=True)
    return centred * lax.rsqrt(variance + 1e-05) * gain + offset


def attention_kernel(
    core_ref,
    scale_ref,
    tall_ref,
    bias_ref,
    arrange_ref,
    patch_select_ref,
    select_ref,
    gain_ref,
    offset_ref,
    mine_ref,
    other_ref,
    out_ref,
    weight,
    queries,
    keys,
    values,
    heads,
    patch_select,
    select,
    sems,
):
    core = core_ref[0]
    copies = []
    for m in range(16):
        for part, (ref, of) in enumerate(((mine_ref, core), (other_ref, 1 - core))):
            y_hi, x, y_lo = place(m, of)
            row = pl.multiple_of(y_lo * 16, 16)
            column = pl.multiple_of((y_hi * 8 + x * 2 + of) * 128, 128)
            copies.append(
                pltpu.make_async_copy(
                    ref.at[m],
                    weight.at[:, pl.ds(row, 16), pl.ds(column, 128)],
                    sems.at[m * 2 + part],
                )
            )
    late = [
        pltpu.make_async_copy(select_ref, select, sems.at[32]),
        pltpu.make_async_copy(patch_select_ref, patch_select, sems.at[33]),
    ]
    for copy in copies + late:
        copy.start()
    for copy in copies:
        copy.wait()

    row = lax.broadcasted_iota(jnp.int32, (256, 256), 0)
    lane = lax.broadcasted_iota(jnp.int32, (256, 256), 1)
    ones = jnp.where(row // 64 == lane // 64, 1.0, 0.0).astype(BF16)
    row2 = lax.broadcasted_iota(jnp.int32, (256, 128), 0)
    lane2 = lax.broadcasted_iota(jnp.int32, (256, 128), 1)
    counts = jnp.where((row2 >= 128) == (lane2 >= 64), 1.0, 0.0).astype(BF16)
    low_half = lax.broadcasted_iota(jnp.int32, (WIN_PAD, 128), 1) < 64
    zero = jnp.zeros((WIN_PAD, 128), BF16)
    gap = jnp.zeros((KEY_PAD - WIN_PAD, 128), BF16)

    def columns(start, width):
        return weight[:, :, start : start + width].reshape(D, width)

    def both(block):
        return jnp.concatenate(
            [jnp.where(low_half, block, zero), gap, jnp.where(low_half, zero, block), gap], axis=0
        )

    done = 0
    for band in range(BANDS):
        strip = tall_ref[band * WIN_ROWS : (band + 1) * WIN_ROWS].reshape(WIN_ROWS * 48, D)
        tokens = jnp.dot(arrange_ref[...], strip, preferred_element_type=F32).astype(BF16)
        for target, start in ((queries, 0), (keys, D)):
            total = jnp.dot(tokens, columns(start, D), preferred_element_type=F32)
            for i, part in enumerate(unit_norm(total, ones)):
                target[:, i * 256 : i * 256 + 256] = part
        values[...] = jnp.dot(tokens, columns(2 * D, D), preferred_element_type=F32).astype(BF16)
        first, count = QUERY_ROWS[band]

        def window(w, _, band=band, first=first, count=count, done=done):
            base = pl.multiple_of(w * WIN_PAD, WIN_PAD)
            for pair in range(HEAD_COUNT // 2):
                cut = slice(pair * 128, pair * 128 + 128)
                query = queries[pl.ds(base + first, count), cut]
                key = both(keys[pl.ds(base, WIN_PAD), cut])
                value = both(values[pl.ds(base, WIN_PAD), cut])
                scores = lax.dot_general(
                    query, key, (((1,), (1,)), ((), ())), preferred_element_type=F32
                )
                expo = []
                for h in range(2):
                    head = pair * 2 + h
                    one = scores[:, h * 128 : h * 128 + 128] * scale_ref[head]
                    one = one + bias_ref[band, head, first : first + count, :]
                    peak = jnp.max(one, axis=-1, keepdims=True)
                    expo.append(jnp.exp(one - peak).astype(BF16))
                mixed = jnp.dot(
                    jnp.concatenate(expo, axis=1),
                    jnp.concatenate([value, counts], axis=1),
                    preferred_element_type=F32,
                )
                place = pl.multiple_of(done + w * count, 16)
                heads[pl.ds(place, count), cut] = (mixed[:, :128] / mixed[:, 128:]).astype(BF16)
            return 0

        lax.fori_loop(0, WINS, window, 0)
        done += WINS * count

    for copy in late:
        copy.wait()
    own = jnp.dot(select[...], heads[...], preferred_element_type=F32).astype(BF16)
    projected = jnp.dot(own, columns(3 * D, D), preferred_element_type=F32)
    branch = norm_rows(projected, gain_ref[...], offset_ref[...]).astype(BF16)
    patches = jnp.dot(
        patch_select[...], tall_ref[...].reshape(18 * 48, D), preferred_element_type=F32
    )
    out_ref[...] = (patches + branch.astype(F32)).astype(BF16)


def feedforward_kernel(
    core_ref,
    first_ref,
    gain_ref,
    offset_ref,
    merge_gain_ref,
    merge_offset_ref,
    mine_ref,
    other_ref,
    out_ref,
    up,
    down,
    merge,
    tokens_in,
    up_sems,
    down_sems,
    merge_sems,
):
    core = core_ref[0]
    ups, downs, merges = [], [], []
    for m in range(16):
        for part, (ref, of) in enumerate(((mine_ref, core), (other_ref, 1 - core))):
            y_hi, x, y_lo = place(m, of)
            row = pl.multiple_of(y_lo * 16, 16)
            column = pl.multiple_of((y_hi * 8 + x * 2 + of) * 128, 128)
            ups.append(
                pltpu.make_async_copy(
                    ref.at[m, :, pl.ds(0, 16), :],
                    up.at[:, pl.ds(row, 16), pl.ds(column, 128)],
                    up_sems.at[m * 2 + part],
                )
            )
            row = pl.multiple_of(y_lo * 64 + of * 32 + y_hi * 16, 16)
            column = pl.multiple_of(x * 128, 128)
            downs.append(
                pltpu.make_async_copy(
                    ref.at[m, :, pl.ds(16, 16), :],
                    down.at[:, pl.ds(row, 16), pl.ds(column, 128)],
                    down_sems.at[m * 2 + part],
                )
            )
            row = pl.multiple_of(y_lo * 64 + of * 32, 32)
            column = pl.multiple_of((y_hi * 4 + x) * 128, 128)
            merges.append(
                pltpu.make_async_copy(
                    ref.at[m, :, pl.ds(32, 32), :],
                    merge.at[:, pl.ds(row, 32), pl.ds(column, 128)],
                    merge_sems.at[m * 2 + part],
                )
            )
    ups.append(pltpu.make_async_copy(first_ref, tokens_in, up_sems.at[32]))
    for copy in ups + downs + merges:
        copy.start()
    for copy in ups:
        copy.wait()
    tokens = tokens_in[...]
    total = None
    for n in range(FFN // 512):
        cut = slice(n * 512, n * 512 + 512)
        hidden = jnp.dot(tokens, up[:, :, cut].reshape(D, 512), preferred_element_type=F32)
        hidden = (0.5 * hidden * (1.0 + lax.erf(hidden * (0.5**0.5)))).astype(BF16)
        if n == 0:
            for copy in downs:
                copy.wait()
        piece = jnp.dot(
            hidden, down[n * 4 : n * 4 + 4].reshape(512, D), preferred_element_type=F32
        )
        total = piece if total is None else total + piece
    branch = norm_rows(total, gain_ref[...], offset_ref[...])
    second = (tokens.astype(F32) + branch).astype(BF16)
    for copy in merges:
        copy.wait()
    total = None
    for n in range(4):
        piece = jnp.dot(
            second[n * QUAD_ROWS : (n + 1) * QUAD_ROWS],
            merge[n * 4 : n * 4 + 4].reshape(512, 2 * D),
            preferred_element_type=F32,
        )
        total = piece if total is None else total + piece
    reduced = norm_rows(total, merge_gain_ref[...], merge_offset_ref[...])
    for i in range(6):
        out_ref[i] = reduced[i * 18 : i * 18 + 18].astype(BF16)


def quads_order(place):
    order = place.reshape(6, 2, 18, 2).transpose(3, 1, 0, 2).reshape(4, 108)
    return np.pad(order, ((0, 0), (0, QUAD_ROWS - 108)), constant_values=-1).reshape(-1)


def one_hot_rows(order, size):
    return (order[:, None] == np.arange(size)[None]).astype(np.float32)


def selection():
    place = np.full((12, 36), -1)
    done = 0
    for band in range(BANDS):
        first, count = QUERY_ROWS[band]
        for w in range(WINS):
            for r in range(count):
                a, b = (first + r) // PAD_COLS, (first + r) % PAD_COLS
                i = band * WIN_ROWS + a - SHIFT_ROWS
                j = w * WIN_COLS + b - SHIFT_COLS
                if b < WIN_COLS and 0 <= j < 36:
                    place[i, j] = done + r
            done += count
    return one_hot_rows(quads_order(place), done)


def patch_selection():
    i, j = np.arange(12)[:, None] + SHIFT_ROWS, np.arange(36)[None] + SHIFT_COLS
    return one_hot_rows(quads_order(i * 48 + j), 18 * 48)


def arrangement():
    r = np.arange(WINS * WIN_PAD)
    w, a, b = r // WIN_PAD, r % WIN_PAD // PAD_COLS, r % PAD_COLS
    return one_hot_rows(np.where(b < WIN_COLS, a * 48 + w * WIN_COLS + b, -1), WIN_ROWS * 48)


def local(
    patches,
    query_key_value_weight,
    attention_output_weight,
    feedforward_in_weight,
    feedforward_out_weight,
    merging_reduction_weight,
    head_scale_logarithm,
    bias_network_first_weight,
    bias_network_first_bias,
    bias_network_second_weight,
    attention_norm_gain,
    attention_norm_offset,
    feedforward_norm_gain,
    feedforward_norm_offset,
    merging_norm_gain,
    merging_norm_offset,
):
    lat = lax.axis_index(LAT)
    core = lax.axis_index("core")
    x = lax.axis_index("x")

    mine = jnp.concatenate(
        [query_key_value_weight, attention_output_weight, feedforward_in_weight], axis=1
    )
    theirs = shifted(mine, "core", 1, True)
    rows = jnp.concatenate(
        [jnp.where(core == 0, mine, theirs), jnp.where(core == 0, theirs, mine)], axis=0
    )
    at = (lat * 2 + core) * 128
    units = jnp.concatenate(
        [
            lax.dynamic_slice(rows, (0, at), (16, 128)),
            lax.dynamic_slice(rows, (0, 2048 + at), (16, 128)),
            lax.dynamic_slice(
                feedforward_out_weight, (lax.axis_index("y_hi") * 16, x * 128), (16, 128)
            ),
            lax.dynamic_slice(merging_reduction_weight, (0, lat * 128), (32, 128)),
        ]
    )

    units, patches = lax.optimization_barrier((units, patches))
    along_z = spread(units, "z")
    south = shifted(patches[:SHIFT_ROWS], LAT, -1, False)
    north = shifted(patches[12 - SHIFT_ROWS :], LAT, 1, False)
    strip = jnp.concatenate([north, patches, south], axis=0)

    table = bias_entries(
        bias_network_first_weight, bias_network_first_bias, bias_network_second_weight
    )
    lookup = bias_lookup()
    entries = table.shape[1]
    one_hot = (
        jnp.asarray(lookup.reshape(-1), jnp.int32)[None, :]
        == jnp.arange(entries, dtype=jnp.int32)[:, None]
    ).astype(F32)
    bias = jnp.dot(table, one_hot, precision=lax.Precision.HIGHEST)
    bias = bias.reshape(HEAD_COUNT, WIN_PAD, KEY_PAD)
    key = np.arange(KEY_PAD)
    held = (key < WIN_PAD) & (key % PAD_COLS < WIN_COLS)
    bias = jnp.where(jnp.asarray(held), bias, OFF)
    apart = (np.arange(WIN_PAD)[:, None] // 48) != (key[None] // 48)
    seam = jnp.stack([lat == 0, jnp.bool_(False), lat == 7])
    bias = jnp.where(seam[:, None, None, None] & jnp.asarray(apart), OFF, bias[None])
    head_scale = jnp.exp(jnp.minimum(head_scale_logarithm, jnp.log(100.0)))

    along_z, strip, bias = lax.optimization_barrier((along_z, strip, bias))
    in_ring = spread_ring(four(along_z), 0)
    east = shifted(strip[:, :SHIFT_COLS], LON, -1, True)
    west = shifted(strip[:, 36 - SHIFT_COLS :], LON, 1, True)
    tall = jnp.concatenate([west, strip, east], axis=1)
    in_ring, tall = lax.optimization_barrier((in_ring, tall))
    attn_mine = spread_ring(four(in_ring[:, :, :16]), 1).reshape(16, 16, 16, 128)
    rest_copies = four(in_ring[:, :, 16:])
    attn_mine, rest_copies = lax.optimization_barrier((attn_mine, rest_copies))
    attn_other = shifted(attn_mine, "core", 1, True)
    rest_mine = spread_ring(rest_copies, 1).reshape(16, 16, 64, 128)

    vmem = pl.BlockSpec(memory_space=pltpu.VMEM)
    smem = pl.BlockSpec(memory_space=pltpu.SMEM)
    hbm = pl.BlockSpec(memory_space=pltpu.HBM)
    anywhere = pl.BlockSpec(memory_space=pl.ANY)

    def far(block):
        return pltpu.with_memory_space_constraint(block, pltpu.HBM)

    params = pltpu.CompilerParams(vmem_limit_bytes=24 * 1024 * 1024)
    core_index = core.astype(jnp.int32).reshape(1)
    half = WINS * WIN_PAD
    first = pl.pallas_call(
        attention_kernel,
        out_shape=jax.ShapeDtypeStruct((4 * QUAD_ROWS, D), BF16),
        in_specs=[smem, smem] + [vmem] * 3 + [hbm] * 2 + [vmem] * 2 + [anywhere] * 2,
        out_specs=vmem,
        scratch_shapes=[
            pltpu.VMEM((16, 32, 2048), BF16),
            pltpu.VMEM((half, D), BF16),
            pltpu.VMEM((half, D), BF16),
            pltpu.VMEM((half, D), BF16),
            pltpu.VMEM((768, D), BF16),
            pltpu.VMEM((4 * QUAD_ROWS, 864), BF16),
            pltpu.VMEM((4 * QUAD_ROWS, 768), BF16),
            pltpu.SemaphoreType.DMA((34,)),
        ],
        compiler_params=params,
        cost_estimate=pl.CostEstimate(
            flops=20_000_000_000, bytes_accessed=20_000_000, transcendentals=1_000_000
        ),
        name="attention",
    )(
        core_index,
        head_scale,
        tall,
        bias,
        jnp.asarray(arrangement(), BF16),
        far(jnp.asarray(patch_selection(), BF16)),
        far(jnp.asarray(selection(), BF16)),
        attention_norm_gain.reshape(1, D),
        attention_norm_offset.reshape(1, D),
        attn_mine,
        attn_other,
    )
    first, rest_mine = lax.optimization_barrier((first, rest_mine))
    rest_other = shifted(rest_mine, "core", 1, True)
    return pl.pallas_call(
        feedforward_kernel,
        out_shape=jax.ShapeDtypeStruct((6, 18, 2 * D), BF16),
        in_specs=[smem, hbm] + [vmem] * 4 + [anywhere] * 2,
        out_specs=vmem,
        scratch_shapes=[
            pltpu.VMEM((16, 32, FFN), BF16),
            pltpu.VMEM((16, 128, D), BF16),
            pltpu.VMEM((16, 128, 2 * D), BF16),
            pltpu.VMEM((4 * QUAD_ROWS, D), BF16),
            pltpu.SemaphoreType.DMA((33,)),
            pltpu.SemaphoreType.DMA((32,)),
            pltpu.SemaphoreType.DMA((32,)),
        ],
        compiler_params=params,
        cost_estimate=pl.CostEstimate(
            flops=6_000_000_000, bytes_accessed=20_000_000, transcendentals=1_000_000
        ),
        name="feedforward",
    )(
        core_index,
        far(first),
        feedforward_norm_gain.reshape(1, D),
        feedforward_norm_offset.reshape(1, D),
        merging_norm_gain.reshape(1, 2 * D),
        merging_norm_offset.reshape(1, 2 * D),
        rest_mine,
        rest_other,
    )


def solution(mesh):
    fine = Mesh(mesh.devices.reshape(2, 4, 16, 2, 2), ("y_hi", "x", "z", "y_lo", "core"))
    in_specs = (P(LAT, LON, None),) + (P(LON, None),) * 5 + (P(),) * 10
    return jax.shard_map(
        local, mesh=fine, in_specs=in_specs, out_specs=P(LAT, LON, None), check_vma=False
    )
```

```python
import jax
import jax.numpy as jnp
import numpy as np
from jax import lax
from jax.experimental import pallas as pl
from jax.experimental.pallas import tpu as pltpu
from jax.sharding import Mesh
from jax.sharding import PartitionSpec as P

D = 512
HEAD_COUNT = 8
WIN_ROWS = 6
WIN_COLS = 12
PAD_COLS = 16
SHIFT_ROWS = 3
SHIFT_COLS = 6
FFN = 2048
WIN_PAD = WIN_ROWS * PAD_COLS
KEY_PAD = 128
BANDS = 3
WINS = 4
QUAD_ROWS = 112
LAT = ("y_hi", "x")
LON = ("z", "y_lo", "core")
ALL = ("y_hi", "x", "z", "y_lo", "core")
OFF = -1e30
BF16 = jnp.bfloat16
F32 = jnp.float32
QUERY_ROWS = ((48, 48), (0, 96), (0, 48))


def shifted(block, axes, by, wrap):
    size = lax.axis_size(axes)
    pairs = [(i, (i + by) % size) for i in range(size) if wrap or 0 <= i + by < size]
    return lax.ppermute(block, axes, pairs)


def spread(block, axes):
    size = lax.axis_size(axes)
    return lax.all_to_all(jnp.broadcast_to(block[None], (size,) + block.shape), axes, 0, 0)


def rings(x_core):
    ids = np.arange(512).reshape(2, 4, 16, 2, 2)
    along_x = ids.transpose(0, 2, 3, 4, 1)[:, :, :, x_core].reshape(-1, 4)
    along_y = ids.transpose(1, 2, 4, 0, 3)[:, :, 1 - x_core].reshape(-1, 4)
    return np.concatenate([along_x, along_y]).tolist()


def four(block):
    return jnp.broadcast_to(block[None], (4,) + block.shape)


def spread_ring(copies, x_core):
    return lax.all_to_all(copies, ALL, 0, 0, axis_index_groups=rings(x_core))


def ring_shift(block, x_core, by):
    pairs = [(ring[i], ring[(i + by) % 4]) for ring in rings(x_core) for i in range(4)]
    return lax.ppermute(block, ALL, pairs)


def place_by(step, inner, of, x, y):
    outer = ((1 - of) * y + of * x + 4 - step) & 3

    def pick(on_first, on_second):
        return on_first + of * (on_second - on_first)

    return pick(outer >> 1, inner // 2), pick(inner, outer), pick(outer & 1, inner % 2)


def place(m, of):
    outer, inner = m // 4, m % 4

    def pick(on_first, on_second):
        return on_first + of * (on_second - on_first)

    return pick(outer // 2, inner // 2), pick(inner, outer), pick(outer % 2, inner % 2)


def bias_entries(first_weight, first_bias, second_weight):
    span_rows = 2 * WIN_ROWS - 1
    span_cols = 2 * WIN_COLS - 1
    entry = np.arange(span_rows * span_cols)
    coordinates = np.stack(
        [
            (entry // span_cols - (WIN_ROWS - 1)) * (8.0 / (WIN_ROWS - 1)),
            (entry % span_cols - (WIN_COLS - 1)) * (8.0 / (WIN_COLS - 1)),
        ],
        axis=1,
    )
    coordinates = np.sign(coordinates) * np.log2(np.abs(coordinates) + 1.0) / 3.0
    coordinates = jnp.asarray(coordinates, F32)
    hidden = jax.nn.relu(
        coordinates[:, :1] * first_weight[:1] + coordinates[:, 1:] * first_weight[1:] + first_bias
    )
    return 16.0 * jax.nn.sigmoid(
        lax.dot_general(
            second_weight, hidden, (((0,), (1,)), ((), ())), precision=lax.Precision.HIGHEST
        )
    )


def bias_lookup():
    q = np.arange(WIN_PAD)
    k = np.arange(KEY_PAD)
    qa, qb = q // PAD_COLS, np.minimum(q % PAD_COLS, WIN_COLS - 1)
    ka, kb = np.minimum(k // PAD_COLS, WIN_ROWS - 1), np.minimum(k % PAD_COLS, WIN_COLS - 1)
    rows = qa[:, None] - ka[None] + WIN_ROWS - 1
    cols = qb[:, None] - kb[None] + WIN_COLS - 1
    return rows * (2 * WIN_COLS - 1) + cols


def unit_norm(triple, ones):
    rounded = triple.astype(BF16)
    exact = rounded.astype(F32)
    square = exact * exact
    high = square.astype(BF16)
    low = (square - high.astype(F32)).astype(BF16)
    parts = []
    for i in range(D // 256):
        cut = slice(i * 256, i * 256 + 256)
        total = jnp.dot(high[:, cut], ones, preferred_element_type=F32)
        total += jnp.dot(low[:, cut], ones, preferred_element_type=F32)
        parts.append((exact[:, cut] * lax.rsqrt(total + 1e-06)).astype(BF16))
    return parts


def norm_rows(values, gain, offset):
    average = jnp.mean(values, axis=-1, keepdims=True)
    centred = values - average
    variance = jnp.mean(centred * centred, axis=-1, keepdims=True)
    return centred * lax.rsqrt(variance + 1e-05) * gain + offset


def attention_kernel(
    core_ref,
    scale_ref,
    tall_ref,
    bias_ref,
    arrange_ref,
    patch_select_ref,
    select_ref,
    gain_ref,
    offset_ref,
    mine_ref,
    other_ref,
    out_ref,
    weight,
    queries,
    keys,
    values,
    heads,
    patch_select,
    select,
    sems,
):
    core = core_ref[0]
    copies = []
    for m in range(16):
        for part, (ref, of) in enumerate(((mine_ref, core), (other_ref, 1 - core))):
            y_hi, x, y_lo = place(m, of)
            row = pl.multiple_of(y_lo * 16, 16)
            column = pl.multiple_of((y_hi * 8 + x * 2 + of) * 128, 128)
            copies.append(
                pltpu.make_async_copy(
                    ref.at[m],
                    weight.at[:, pl.ds(row, 16), pl.ds(column, 128)],
                    sems.at[m * 2 + part],
                )
            )
    late = [
        pltpu.make_async_copy(select_ref, select, sems.at[32]),
        pltpu.make_async_copy(patch_select_ref, patch_select, sems.at[33]),
    ]
    for copy in copies + late:
        copy.start()
    for copy in copies:
        copy.wait()

    row = lax.broadcasted_iota(jnp.int32, (256, 256), 0)
    lane = lax.broadcasted_iota(jnp.int32, (256, 256), 1)
    ones = jnp.where(row // 64 == lane // 64, 1.0, 0.0).astype(BF16)
    row2 = lax.broadcasted_iota(jnp.int32, (256, 128), 0)
    lane2 = lax.broadcasted_iota(jnp.int32, (256, 128), 1)
    counts = jnp.where((row2 >= 128) == (lane2 >= 64), 1.0, 0.0).astype(BF16)
    low_half = lax.broadcasted_iota(jnp.int32, (WIN_PAD, 128), 1) < 64
    zero = jnp.zeros((WIN_PAD, 128), BF16)
    gap = jnp.zeros((KEY_PAD - WIN_PAD, 128), BF16)

    def columns(start, width):
        return weight[:, :, start : start + width].reshape(D, width)

    def both(block):
        return jnp.concatenate(
            [jnp.where(low_half, block, zero), gap, jnp.where(low_half, zero, block), gap], axis=0
        )

    done = 0
    for band in range(BANDS):
        strip = tall_ref[band * WIN_ROWS : (band + 1) * WIN_ROWS].reshape(WIN_ROWS * 48, D)
        tokens = jnp.dot(arrange_ref[...], strip, preferred_element_type=F32).astype(BF16)
        for target, start in ((queries, 0), (keys, D)):
            total = jnp.dot(tokens, columns(start, D), preferred_element_type=F32)
            for i, part in enumerate(unit_norm(total, ones)):
                target[:, i * 256 : i * 256 + 256] = part
        values[...] = jnp.dot(tokens, columns(2 * D, D), preferred_element_type=F32).astype(BF16)
        first, count = QUERY_ROWS[band]

        def window(w, _, band=band, first=first, count=count, done=done):
            base = pl.multiple_of(w * WIN_PAD, WIN_PAD)
            all_scores = []
            for pair in range(HEAD_COUNT // 2):
                cut = slice(pair * 128, pair * 128 + 128)
                query = queries[pl.ds(base + first, count), cut]
                key = both(keys[pl.ds(base, WIN_PAD), cut])
                all_scores.append(
                    lax.dot_general(
                        query, key, (((1,), (1,)), ((), ())), preferred_element_type=F32
                    )
                )
            for pair in range(HEAD_COUNT // 2):
                cut = slice(pair * 128, pair * 128 + 128)
                value = both(values[pl.ds(base, WIN_PAD), cut])
                scores = all_scores[pair]
                expo = []
                for h in range(2):
                    head = pair * 2 + h
                    one = scores[:, h * 128 : h * 128 + 128] * scale_ref[head]
                    one = one + bias_ref[band, head, first : first + count, :]
                    peak = jnp.max(one, axis=-1, keepdims=True)
                    expo.append(jnp.exp(one - peak).astype(BF16))
                mixed = jnp.dot(
                    jnp.concatenate(expo, axis=1),
                    jnp.concatenate([value, counts], axis=1),
                    preferred_element_type=F32,
                )
                place = pl.multiple_of(done + w * count, 16)
                heads[pl.ds(place, count), cut] = (mixed[:, :128] / mixed[:, 128:]).astype(BF16)
            return 0

        lax.fori_loop(0, WINS, window, 0, unroll=True)
        done += WINS * count

    for copy in late:
        copy.wait()
    own = jnp.dot(select[...], heads[...], preferred_element_type=F32).astype(BF16)
    projected = jnp.dot(own, columns(3 * D, D), preferred_element_type=F32)
    branch = norm_rows(projected, gain_ref[...], offset_ref[...]).astype(BF16)
    patches = jnp.dot(
        patch_select[...], tall_ref[...].reshape(18 * 48, D), preferred_element_type=F32
    )
    out_ref[...] = (patches + branch.astype(F32)).astype(BF16)


def feedforward_kernel(
    where_ref, first_ref, gain_ref, offset_ref, merge_gain_ref, merge_offset_ref, *refs
):
    pieces, (out_ref, up, down, merge, tokens_in, up_sems, down_sems, merge_sems) = refs[:10], refs[10:]
    core, me_x, me_y = where_ref[0], where_ref[1], where_ref[2]
    ups, downs, merges = [], [], []
    for step in range(4):
        for inner in range(4):
            for part, of in enumerate((core, 1 - core)):
                if step == 2:
                    ref = pieces[6 + inner // 2 * 2 + part].at[inner % 2]
                else:
                    ref = pieces[(step + 1) // 2 * 2 + part].at[inner]
                at = (step * 4 + inner) * 2 + part
                y_hi, x, y_lo = place_by(step, inner, of, me_x, me_y)
                row = pl.multiple_of(y_lo * 16, 16)
                column = pl.multiple_of((y_hi * 8 + x * 2 + of) * 128, 128)
                ups.append(
                    pltpu.make_async_copy(
                        ref.at[:, pl.ds(0, 16), :],
                        up.at[:, pl.ds(row, 16), pl.ds(column, 128)],
                        up_sems.at[at],
                    )
                )
                row = pl.multiple_of(y_lo * 64 + of * 32 + y_hi * 16, 16)
                column = pl.multiple_of(x * 128, 128)
                downs.append(
                    pltpu.make_async_copy(
                        ref.at[:, pl.ds(16, 16), :],
                        down.at[:, pl.ds(row, 16), pl.ds(column, 128)],
                        down_sems.at[at],
                    )
                )
                row = pl.multiple_of(y_lo * 64 + of * 32, 32)
                column = pl.multiple_of((y_hi * 4 + x) * 128, 128)
                merges.append(
                    pltpu.make_async_copy(
                        ref.at[:, pl.ds(32, 32), :],
                        merge.at[:, pl.ds(row, 32), pl.ds(column, 128)],
                        merge_sems.at[at],
                    )
                )
    ups.append(pltpu.make_async_copy(first_ref, tokens_in, up_sems.at[32]))
    for copy in ups + downs + merges:
        copy.start()
    for copy in ups:
        copy.wait()
    tokens = tokens_in[...]
    total = None
    for n in range(FFN // 512):
        cut = slice(n * 512, n * 512 + 512)
        hidden = jnp.dot(tokens, up[:, :, cut].reshape(D, 512), preferred_element_type=F32)
        hidden = (0.5 * hidden * (1.0 + lax.erf(hidden * (0.5**0.5)))).astype(BF16)
        if n == 0:
            for copy in downs:
                copy.wait()
        piece = jnp.dot(
            hidden, down[n * 4 : n * 4 + 4].reshape(512, D), preferred_element_type=F32
        )
        total = piece if total is None else total + piece
    branch = norm_rows(total, gain_ref[...], offset_ref[...])
    second = (tokens.astype(F32) + branch).astype(BF16)
    for copy in merges:
        copy.wait()
    total = None
    for n in range(4):
        piece = jnp.dot(
            second[n * QUAD_ROWS : (n + 1) * QUAD_ROWS],
            merge[n * 4 : n * 4 + 4].reshape(512, 2 * D),
            preferred_element_type=F32,
        )
        total = piece if total is None else total + piece
    reduced = norm_rows(total, merge_gain_ref[...], merge_offset_ref[...])
    for i in range(6):
        out_ref[i] = reduced[i * 18 : i * 18 + 18].astype(BF16)


def quads_order(place):
    order = place.reshape(6, 2, 18, 2).transpose(3, 1, 0, 2).reshape(4, 108)
    return np.pad(order, ((0, 0), (0, QUAD_ROWS - 108)), constant_values=-1).reshape(-1)


def one_hot_rows(order, size):
    return (order[:, None] == np.arange(size)[None]).astype(np.float32)


def selection():
    place = np.full((12, 36), -1)
    done = 0
    for band in range(BANDS):
        first, count = QUERY_ROWS[band]
        for w in range(WINS):
            for r in range(count):
                a, b = (first + r) // PAD_COLS, (first + r) % PAD_COLS
                i = band * WIN_ROWS + a - SHIFT_ROWS
                j = w * WIN_COLS + b - SHIFT_COLS
                if b < WIN_COLS and 0 <= j < 36:
                    place[i, j] = done + r
            done += count
    return one_hot_rows(quads_order(place), done)


def patch_selection():
    i, j = np.arange(12)[:, None] + SHIFT_ROWS, np.arange(36)[None] + SHIFT_COLS
    return one_hot_rows(quads_order(i * 48 + j), 18 * 48)


def arrangement():
    r = np.arange(WINS * WIN_PAD)
    w, a, b = r // WIN_PAD, r % WIN_PAD // PAD_COLS, r % PAD_COLS
    return one_hot_rows(np.where(b < WIN_COLS, a * 48 + w * WIN_COLS + b, -1), WIN_ROWS * 48)


def local(
    patches,
    query_key_value_weight,
    attention_output_weight,
    feedforward_in_weight,
    feedforward_out_weight,
    merging_reduction_weight,
    head_scale_logarithm,
    bias_network_first_weight,
    bias_network_first_bias,
    bias_network_second_weight,
    attention_norm_gain,
    attention_norm_offset,
    feedforward_norm_gain,
    feedforward_norm_offset,
    merging_norm_gain,
    merging_norm_offset,
):
    lat = lax.axis_index(LAT)
    core = lax.axis_index("core")
    x = lax.axis_index("x")

    mine = jnp.concatenate(
        [query_key_value_weight, attention_output_weight, feedforward_in_weight], axis=1
    )
    theirs = shifted(mine, "core", 1, True)
    rows = jnp.concatenate(
        [jnp.where(core == 0, mine, theirs), jnp.where(core == 0, theirs, mine)], axis=0
    )
    at = (lat * 2 + core) * 128
    units = jnp.concatenate(
        [
            lax.dynamic_slice(rows, (0, at), (16, 128)),
            lax.dynamic_slice(rows, (0, 2048 + at), (16, 128)),
            lax.dynamic_slice(
                feedforward_out_weight, (lax.axis_index("y_hi") * 16, x * 128), (16, 128)
            ),
            lax.dynamic_slice(merging_reduction_weight, (0, lat * 128), (32, 128)),
        ]
    )

    units, patches = lax.optimization_barrier((units, patches))
    along_z = spread(units, "z")
    south = shifted(patches[:SHIFT_ROWS], LAT, -1, False)
    north = shifted(patches[12 - SHIFT_ROWS :], LAT, 1, False)
    strip = jnp.concatenate([north, patches, south], axis=0)

    table = bias_entries(
        bias_network_first_weight, bias_network_first_bias, bias_network_second_weight
    )
    lookup = bias_lookup()
    entries = table.shape[1]
    one_hot = (
        jnp.asarray(lookup.reshape(-1), jnp.int32)[None, :]
        == jnp.arange(entries, dtype=jnp.int32)[:, None]
    ).astype(F32)
    bias = jnp.dot(table, one_hot, precision=lax.Precision.HIGHEST)
    bias = bias.reshape(HEAD_COUNT, WIN_PAD, KEY_PAD)
    key = np.arange(KEY_PAD)
    held = (key < WIN_PAD) & (key % PAD_COLS < WIN_COLS)
    bias = jnp.where(jnp.asarray(held), bias, OFF)
    apart = (np.arange(WIN_PAD)[:, None] // 48) != (key[None] // 48)
    seam = jnp.stack([lat == 0, jnp.bool_(False), lat == 7])
    bias = jnp.where(seam[:, None, None, None] & jnp.asarray(apart), OFF, bias[None])
    head_scale = jnp.exp(jnp.minimum(head_scale_logarithm, jnp.log(100.0)))

    along_z, strip, bias = lax.optimization_barrier((along_z, strip, bias))
    in_ring = spread_ring(four(along_z), 0)
    east = shifted(strip[:, :SHIFT_COLS], LON, -1, True)
    west = shifted(strip[:, 36 - SHIFT_COLS :], LON, 1, True)
    tall = jnp.concatenate([west, strip, east], axis=1)
    in_ring, tall = lax.optimization_barrier((in_ring, tall))
    attn_copies, rest = lax.optimization_barrier((four(in_ring[:, :, :16]), in_ring[:, :, 16:]))
    attn_mine = spread_ring(attn_copies, 1).reshape(16, 16, 16, 128)
    rest_other = shifted(rest, "core", 1, True)
    one, three = ring_shift(rest, 1, 1), ring_shift(rest, 1, 3)
    attn_mine, rest_other, one, three = lax.optimization_barrier((attn_mine, rest_other, one, three))
    attn_other = shifted(attn_mine, "core", 1, True)
    two_low, two_high = ring_shift(one[:2], 1, 1), ring_shift(three[2:], 1, 3)
    one_other, three_other = shifted(one, "core", 1, True), shifted(three, "core", 1, True)

    vmem = pl.BlockSpec(memory_space=pltpu.VMEM)
    smem = pl.BlockSpec(memory_space=pltpu.SMEM)
    hbm = pl.BlockSpec(memory_space=pltpu.HBM)
    anywhere = pl.BlockSpec(memory_space=pl.ANY)

    def far(block):
        return pltpu.with_memory_space_constraint(block, pltpu.HBM)

    params = pltpu.CompilerParams(vmem_limit_bytes=24 * 1024 * 1024)
    core_index = core.astype(jnp.int32).reshape(1)
    half = WINS * WIN_PAD
    first = pl.pallas_call(
        attention_kernel,
        out_shape=jax.ShapeDtypeStruct((4 * QUAD_ROWS, D), BF16),
        in_specs=[smem, smem] + [vmem] * 3 + [hbm] * 2 + [vmem] * 2 + [anywhere] * 2,
        out_specs=vmem,
        scratch_shapes=[
            pltpu.VMEM((16, 32, 2048), BF16),
            pltpu.VMEM((half, D), BF16),
            pltpu.VMEM((half, D), BF16),
            pltpu.VMEM((half, D), BF16),
            pltpu.VMEM((768, D), BF16),
            pltpu.VMEM((4 * QUAD_ROWS, 864), BF16),
            pltpu.VMEM((4 * QUAD_ROWS, 768), BF16),
            pltpu.SemaphoreType.DMA((34,)),
        ],
        compiler_params=params,
        cost_estimate=pl.CostEstimate(
            flops=20_000_000_000, bytes_accessed=20_000_000, transcendentals=1_000_000
        ),
        name="attention",
    )(
        core_index,
        head_scale,
        tall,
        bias,
        jnp.asarray(arrangement(), BF16),
        far(jnp.asarray(patch_selection(), BF16)),
        far(jnp.asarray(selection(), BF16)),
        attention_norm_gain.reshape(1, D),
        attention_norm_offset.reshape(1, D),
        attn_mine,
        attn_other,
    )
    first, two_low, two_high = lax.optimization_barrier((first, two_low, two_high))
    pieces = [rest, far(rest_other), one, one_other, three, three_other, two_low]
    pieces += [shifted(two_low, "core", 1, True), two_high, shifted(two_high, "core", 1, True)]
    return pl.pallas_call(
        feedforward_kernel,
        out_shape=jax.ShapeDtypeStruct((6, 18, 2 * D), BF16),
        in_specs=[smem, hbm] + [vmem] * 4 + [anywhere] * 10,
        out_specs=vmem,
        scratch_shapes=[
            pltpu.VMEM((16, 32, FFN), BF16),
            pltpu.VMEM((16, 128, D), BF16),
            pltpu.VMEM((16, 128, 2 * D), BF16),
            pltpu.VMEM((4 * QUAD_ROWS, D), BF16),
            pltpu.SemaphoreType.DMA((33,)),
            pltpu.SemaphoreType.DMA((32,)),
            pltpu.SemaphoreType.DMA((32,)),
        ],
        compiler_params=params,
        cost_estimate=pl.CostEstimate(
            flops=6_000_000_000, bytes_accessed=20_000_000, transcendentals=1_000_000
        ),
        name="feedforward",
    )(
        jnp.stack([core, x, lax.axis_index(("y_hi", "y_lo"))]).astype(jnp.int32),
        far(first),
        feedforward_norm_gain.reshape(1, D),
        feedforward_norm_offset.reshape(1, D),
        merging_norm_gain.reshape(1, 2 * D),
        merging_norm_offset.reshape(1, 2 * D),
        *pieces,
    )


def solution(mesh):
    fine = Mesh(mesh.devices.reshape(2, 4, 16, 2, 2), ("y_hi", "x", "z", "y_lo", "core"))
    in_specs = (P(LAT, LON, None),) + (P(LON, None),) * 5 + (P(),) * 10
    return jax.shard_map(
        local, mesh=fine, in_specs=in_specs, out_specs=P(LAT, LON, None), check_vma=False
    )
```

```python
import jax
import jax.numpy as jnp
import numpy as np
from jax import lax
from jax.experimental import pallas as pl
from jax.experimental.pallas import tpu as pltpu
from jax.sharding import Mesh
from jax.sharding import PartitionSpec as P

D = 512
HEAD_COUNT = 8
WIN_ROWS = 6
WIN_COLS = 12
PAD_COLS = 16
SHIFT_ROWS = 3
SHIFT_COLS = 6
FFN = 2048
WIN_PAD = WIN_ROWS * PAD_COLS
KEY_PAD = 128
BANDS = 3
WINS = 4
QUAD_ROWS = 112
LAT = ("y_hi", "x")
LON = ("z", "y_lo", "core")
ALL = ("y_hi", "x", "z", "y_lo", "core")
OFF = -1e30
BF16 = jnp.bfloat16
F32 = jnp.float32
QUERY_ROWS = ((48, 48), (0, 96), (0, 48))


def shifted(block, axes, by, wrap):
    size = lax.axis_size(axes)
    pairs = [(i, (i + by) % size) for i in range(size) if wrap or 0 <= i + by < size]
    return lax.ppermute(block, axes, pairs)


def spread(block, axes):
    size = lax.axis_size(axes)
    return lax.all_to_all(jnp.broadcast_to(block[None], (size,) + block.shape), axes, 0, 0)


def rings(x_core):
    ids = np.arange(512).reshape(2, 4, 16, 2, 2)
    along_x = ids.transpose(0, 2, 3, 4, 1)[:, :, :, x_core].reshape(-1, 4)
    along_y = ids.transpose(1, 2, 4, 0, 3)[:, :, 1 - x_core].reshape(-1, 4)
    return np.concatenate([along_x, along_y]).tolist()


def four(block):
    return jnp.broadcast_to(block[None], (4,) + block.shape)


def fan_kernel(ring_ref, out_ref, sems):
    copies = [
        pltpu.make_async_copy(ring_ref.at[:, :, pl.ds(16, 64), :], out_ref.at[i], sems.at[i])
        for i in range(4)
    ]
    for copy in copies:
        copy.start()
    for copy in copies:
        copy.wait()


def fan(in_ring):
    anywhere = pl.BlockSpec(memory_space=pl.ANY)
    return pl.pallas_call(
        fan_kernel,
        out_shape=jax.ShapeDtypeStruct((4, 4, 16, 64, 128), BF16),
        in_specs=[anywhere],
        out_specs=anywhere,
        scratch_shapes=[pltpu.SemaphoreType.DMA((4,))],
        compiler_params=pltpu.CompilerParams(vmem_limit_bytes=24 * 1024 * 1024),
        cost_estimate=pl.CostEstimate(flops=0, bytes_accessed=30_000_000, transcendentals=0),
        name="fan",
    )(in_ring)


def spread_ring(copies, x_core):
    return lax.all_to_all(copies, ALL, 0, 0, axis_index_groups=rings(x_core))


def place(m, of):
    outer, inner = m // 4, m % 4

    def pick(on_first, on_second):
        return on_first + of * (on_second - on_first)

    return pick(outer // 2, inner // 2), pick(inner, outer), pick(outer % 2, inner % 2)


def bias_entries(first_weight, first_bias, second_weight):
    span_rows = 2 * WIN_ROWS - 1
    span_cols = 2 * WIN_COLS - 1
    entry = np.arange(span_rows * span_cols)
    coordinates = np.stack(
        [
            (entry // span_cols - (WIN_ROWS - 1)) * (8.0 / (WIN_ROWS - 1)),
            (entry % span_cols - (WIN_COLS - 1)) * (8.0 / (WIN_COLS - 1)),
        ],
        axis=1,
    )
    coordinates = np.sign(coordinates) * np.log2(np.abs(coordinates) + 1.0) / 3.0
    coordinates = jnp.asarray(coordinates, F32)
    hidden = jax.nn.relu(
        coordinates[:, :1] * first_weight[:1] + coordinates[:, 1:] * first_weight[1:] + first_bias
    )
    return 16.0 * jax.nn.sigmoid(
        lax.dot_general(
            second_weight, hidden, (((0,), (1,)), ((), ())), precision=lax.Precision.HIGHEST
        )
    )


def bias_lookup():
    q = np.arange(WIN_PAD)
    k = np.arange(KEY_PAD)
    qa, qb = q // PAD_COLS, np.minimum(q % PAD_COLS, WIN_COLS - 1)
    ka, kb = np.minimum(k // PAD_COLS, WIN_ROWS - 1), np.minimum(k % PAD_COLS, WIN_COLS - 1)
    rows = qa[:, None] - ka[None] + WIN_ROWS - 1
    cols = qb[:, None] - kb[None] + WIN_COLS - 1
    return rows * (2 * WIN_COLS - 1) + cols


def unit_norm(triple, ones):
    rounded = triple.astype(BF16)
    exact = rounded.astype(F32)
    square = exact * exact
    high = square.astype(BF16)
    low = (square - high.astype(F32)).astype(BF16)
    parts = []
    for i in range(D // 256):
        cut = slice(i * 256, i * 256 + 256)
        total = jnp.dot(high[:, cut], ones, preferred_element_type=F32)
        total += jnp.dot(low[:, cut], ones, preferred_element_type=F32)
        parts.append((exact[:, cut] * lax.rsqrt(total + 1e-06)).astype(BF16))
    return parts


def norm_rows(values, gain, offset):
    average = jnp.mean(values, axis=-1, keepdims=True)
    centred = values - average
    variance = jnp.mean(centred * centred, axis=-1, keepdims=True)
    return centred * lax.rsqrt(variance + 1e-05) * gain + offset


def attention_kernel(
    core_ref,
    scale_ref,
    tall_ref,
    bias_ref,
    arrange_ref,
    patch_select_ref,
    select_ref,
    gain_ref,
    offset_ref,
    mine_ref,
    other_ref,
    out_ref,
    weight,
    queries,
    keys,
    values,
    heads,
    patch_select,
    select,
    sems,
):
    core = core_ref[0]
    copies = []
    for m in range(16):
        for part, (ref, of) in enumerate(((mine_ref, core), (other_ref, 1 - core))):
            y_hi, x, y_lo = place(m, of)
            row = pl.multiple_of(y_lo * 16, 16)
            column = pl.multiple_of((y_hi * 8 + x * 2 + of) * 128, 128)
            copies.append(
                pltpu.make_async_copy(
                    ref.at[m],
                    weight.at[:, pl.ds(row, 16), pl.ds(column, 128)],
                    sems.at[m * 2 + part],
                )
            )
    late = [
        pltpu.make_async_copy(select_ref, select, sems.at[32]),
        pltpu.make_async_copy(patch_select_ref, patch_select, sems.at[33]),
    ]
    for copy in copies + late:
        copy.start()
    for copy in copies:
        copy.wait()

    row = lax.broadcasted_iota(jnp.int32, (256, 256), 0)
    lane = lax.broadcasted_iota(jnp.int32, (256, 256), 1)
    ones = jnp.where(row // 64 == lane // 64, 1.0, 0.0).astype(BF16)
    row2 = lax.broadcasted_iota(jnp.int32, (256, 128), 0)
    lane2 = lax.broadcasted_iota(jnp.int32, (256, 128), 1)
    counts = jnp.where((row2 >= 128) == (lane2 >= 64), 1.0, 0.0).astype(BF16)
    low_half = lax.broadcasted_iota(jnp.int32, (WIN_PAD, 128), 1) < 64
    zero = jnp.zeros((WIN_PAD, 128), BF16)
    gap = jnp.zeros((KEY_PAD - WIN_PAD, 128), BF16)

    def columns(start, width):
        return weight[:, :, start : start + width].reshape(D, width)

    def both(block):
        return jnp.concatenate(
            [jnp.where(low_half, block, zero), gap, jnp.where(low_half, zero, block), gap], axis=0
        )

    done = 0
    for band in range(BANDS):
        strip = tall_ref[band * WIN_ROWS : (band + 1) * WIN_ROWS].reshape(WIN_ROWS * 48, D)
        tokens = jnp.dot(arrange_ref[...], strip, preferred_element_type=F32).astype(BF16)
        for target, start in ((queries, 0), (keys, D)):
            total = jnp.dot(tokens, columns(start, D), preferred_element_type=F32)
            for i, part in enumerate(unit_norm(total, ones)):
                target[:, i * 256 : i * 256 + 256] = part
        values[...] = jnp.dot(tokens, columns(2 * D, D), preferred_element_type=F32).astype(BF16)
        first, count = QUERY_ROWS[band]

        def window(w, _, band=band, first=first, count=count, done=done):
            base = pl.multiple_of(w * WIN_PAD, WIN_PAD)
            all_scores = []
            for pair in range(HEAD_COUNT // 2):
                cut = slice(pair * 128, pair * 128 + 128)
                query = queries[pl.ds(base + first, count), cut]
                key = both(keys[pl.ds(base, WIN_PAD), cut])
                all_scores.append(
                    lax.dot_general(
                        query, key, (((1,), (1,)), ((), ())), preferred_element_type=F32
                    )
                )
            for pair in range(HEAD_COUNT // 2):
                cut = slice(pair * 128, pair * 128 + 128)
                value = both(values[pl.ds(base, WIN_PAD), cut])
                scores = all_scores[pair]
                expo = []
                for h in range(2):
                    head = pair * 2 + h
                    one = scores[:, h * 128 : h * 128 + 128] * scale_ref[head]
                    one = one + bias_ref[band, head, first : first + count, :]
                    peak = jnp.max(one, axis=-1, keepdims=True)
                    expo.append(jnp.exp(one - peak).astype(BF16))
                mixed = jnp.dot(
                    jnp.concatenate(expo, axis=1),
                    jnp.concatenate([value, counts], axis=1),
                    preferred_element_type=F32,
                )
                place = pl.multiple_of(done + w * count, 16)
                heads[pl.ds(place, count), cut] = (mixed[:, :128] / mixed[:, 128:]).astype(BF16)
            return 0

        lax.fori_loop(0, WINS, window, 0, unroll=True)
        done += WINS * count

    for copy in late:
        copy.wait()
    own = jnp.dot(select[...], heads[...], preferred_element_type=F32).astype(BF16)
    projected = jnp.dot(own, columns(3 * D, D), preferred_element_type=F32)
    branch = norm_rows(projected, gain_ref[...], offset_ref[...]).astype(BF16)
    patches = jnp.dot(
        patch_select[...], tall_ref[...].reshape(18 * 48, D), preferred_element_type=F32
    )
    out_ref[...] = (patches + branch.astype(F32)).astype(BF16)


def feedforward_kernel(
    core_ref,
    first_ref,
    gain_ref,
    offset_ref,
    merge_gain_ref,
    merge_offset_ref,
    mine_ref,
    other_ref,
    out_ref,
    up,
    down,
    merge,
    tokens_in,
    up_sems,
    down_sems,
    merge_sems,
):
    core = core_ref[0]
    ups, downs, merges = [], [], []
    for m in range(16):
        for part, (ref, of) in enumerate(((mine_ref, core), (other_ref, 1 - core))):
            y_hi, x, y_lo = place(m, of)
            row = pl.multiple_of(y_lo * 16, 16)
            column = pl.multiple_of((y_hi * 8 + x * 2 + of) * 128, 128)
            ups.append(
                pltpu.make_async_copy(
                    ref.at[m, :, pl.ds(0, 16), :],
                    up.at[:, pl.ds(row, 16), pl.ds(column, 128)],
                    up_sems.at[m * 2 + part],
                )
            )
            row = pl.multiple_of(y_lo * 64 + of * 32 + y_hi * 16, 16)
            column = pl.multiple_of(x * 128, 128)
            downs.append(
                pltpu.make_async_copy(
                    ref.at[m, :, pl.ds(16, 16), :],
                    down.at[:, pl.ds(row, 16), pl.ds(column, 128)],
                    down_sems.at[m * 2 + part],
                )
            )
            row = pl.multiple_of(y_lo * 64 + of * 32, 32)
            column = pl.multiple_of((y_hi * 4 + x) * 128, 128)
            merges.append(
                pltpu.make_async_copy(
                    ref.at[m, :, pl.ds(32, 32), :],
                    merge.at[:, pl.ds(row, 32), pl.ds(column, 128)],
                    merge_sems.at[m * 2 + part],
                )
            )
    ups.append(pltpu.make_async_copy(first_ref, tokens_in, up_sems.at[32]))
    for copy in ups + downs + merges:
        copy.start()
    for copy in ups:
        copy.wait()
    tokens = tokens_in[...]
    total = None
    for n in range(FFN // 512):
        cut = slice(n * 512, n * 512 + 512)
        hidden = jnp.dot(tokens, up[:, :, cut].reshape(D, 512), preferred_element_type=F32)
        hidden = (0.5 * hidden * (1.0 + lax.erf(hidden * (0.5**0.5)))).astype(BF16)
        if n == 0:
            for copy in downs:
                copy.wait()
        piece = jnp.dot(
            hidden, down[n * 4 : n * 4 + 4].reshape(512, D), preferred_element_type=F32
        )
        total = piece if total is None else total + piece
    branch = norm_rows(total, gain_ref[...], offset_ref[...])
    second = (tokens.astype(F32) + branch).astype(BF16)
    for copy in merges:
        copy.wait()
    total = None
    for n in range(4):
        piece = jnp.dot(
            second[n * QUAD_ROWS : (n + 1) * QUAD_ROWS],
            merge[n * 4 : n * 4 + 4].reshape(512, 2 * D),
            preferred_element_type=F32,
        )
        total = piece if total is None else total + piece
    reduced = norm_rows(total, merge_gain_ref[...], merge_offset_ref[...])
    for i in range(6):
        out_ref[i] = reduced[i * 18 : i * 18 + 18].astype(BF16)


def quads_order(place):
    order = place.reshape(6, 2, 18, 2).transpose(3, 1, 0, 2).reshape(4, 108)
    return np.pad(order, ((0, 0), (0, QUAD_ROWS - 108)), constant_values=-1).reshape(-1)


def one_hot_rows(order, size):
    return (order[:, None] == np.arange(size)[None]).astype(np.float32)


def selection():
    place = np.full((12, 36), -1)
    done = 0
    for band in range(BANDS):
        first, count = QUERY_ROWS[band]
        for w in range(WINS):
            for r in range(count):
                a, b = (first + r) // PAD_COLS, (first + r) % PAD_COLS
                i = band * WIN_ROWS + a - SHIFT_ROWS
                j = w * WIN_COLS + b - SHIFT_COLS
                if b < WIN_COLS and 0 <= j < 36:
                    place[i, j] = done + r
            done += count
    return one_hot_rows(quads_order(place), done)


def patch_selection():
    i, j = np.arange(12)[:, None] + SHIFT_ROWS, np.arange(36)[None] + SHIFT_COLS
    return one_hot_rows(quads_order(i * 48 + j), 18 * 48)


def arrangement():
    r = np.arange(WINS * WIN_PAD)
    w, a, b = r // WIN_PAD, r % WIN_PAD // PAD_COLS, r % PAD_COLS
    return one_hot_rows(np.where(b < WIN_COLS, a * 48 + w * WIN_COLS + b, -1), WIN_ROWS * 48)


def local(
    patches,
    query_key_value_weight,
    attention_output_weight,
    feedforward_in_weight,
    feedforward_out_weight,
    merging_reduction_weight,
    head_scale_logarithm,
    bias_network_first_weight,
    bias_network_first_bias,
    bias_network_second_weight,
    attention_norm_gain,
    attention_norm_offset,
    feedforward_norm_gain,
    feedforward_norm_offset,
    merging_norm_gain,
    merging_norm_offset,
):
    lat = lax.axis_index(LAT)
    core = lax.axis_index("core")
    x = lax.axis_index("x")

    mine = jnp.concatenate(
        [query_key_value_weight, attention_output_weight, feedforward_in_weight], axis=1
    )
    theirs = shifted(mine, "core", 1, True)
    rows = jnp.concatenate(
        [jnp.where(core == 0, mine, theirs), jnp.where(core == 0, theirs, mine)], axis=0
    )
    at = (lat * 2 + core) * 128
    units = jnp.concatenate(
        [
            lax.dynamic_slice(rows, (0, at), (16, 128)),
            lax.dynamic_slice(rows, (0, 2048 + at), (16, 128)),
            lax.dynamic_slice(
                feedforward_out_weight, (lax.axis_index("y_hi") * 16, x * 128), (16, 128)
            ),
            lax.dynamic_slice(merging_reduction_weight, (0, lat * 128), (32, 128)),
        ]
    )

    units, patches = lax.optimization_barrier((units, patches))
    along_z = spread(units, "z")
    south = shifted(patches[:SHIFT_ROWS], LAT, -1, False)
    north = shifted(patches[12 - SHIFT_ROWS :], LAT, 1, False)
    strip = jnp.concatenate([north, patches, south], axis=0)

    table = bias_entries(
        bias_network_first_weight, bias_network_first_bias, bias_network_second_weight
    )
    lookup = bias_lookup()
    entries = table.shape[1]
    one_hot = (
        jnp.asarray(lookup.reshape(-1), jnp.int32)[None, :]
        == jnp.arange(entries, dtype=jnp.int32)[:, None]
    ).astype(F32)
    bias = jnp.dot(table, one_hot, precision=lax.Precision.HIGHEST)
    bias = bias.reshape(HEAD_COUNT, WIN_PAD, KEY_PAD)
    key = np.arange(KEY_PAD)
    held = (key < WIN_PAD) & (key % PAD_COLS < WIN_COLS)
    bias = jnp.where(jnp.asarray(held), bias, OFF)
    apart = (np.arange(WIN_PAD)[:, None] // 48) != (key[None] // 48)
    seam = jnp.stack([lat == 0, jnp.bool_(False), lat == 7])
    bias = jnp.where(seam[:, None, None, None] & jnp.asarray(apart), OFF, bias[None])
    head_scale = jnp.exp(jnp.minimum(head_scale_logarithm, jnp.log(100.0)))

    along_z, strip, bias = lax.optimization_barrier((along_z, strip, bias))
    in_ring = spread_ring(four(along_z), 0)
    east = shifted(strip[:, :SHIFT_COLS], LON, -1, True)
    west = shifted(strip[:, 36 - SHIFT_COLS :], LON, 1, True)
    tall = jnp.concatenate([west, strip, east], axis=1)
    in_ring, tall = lax.optimization_barrier((in_ring, tall))
    attn_mine = spread_ring(four(in_ring[:, :, :16]), 1).reshape(16, 16, 16, 128)
    rest_copies = fan(in_ring)
    attn_mine, rest_copies = lax.optimization_barrier((attn_mine, rest_copies))
    attn_other = shifted(attn_mine, "core", 1, True)
    rest_mine = spread_ring(rest_copies, 1).reshape(16, 16, 64, 128)

    vmem = pl.BlockSpec(memory_space=pltpu.VMEM)
    smem = pl.BlockSpec(memory_space=pltpu.SMEM)
    hbm = pl.BlockSpec(memory_space=pltpu.HBM)
    anywhere = pl.BlockSpec(memory_space=pl.ANY)

    def far(block):
        return pltpu.with_memory_space_constraint(block, pltpu.HBM)

    params = pltpu.CompilerParams(vmem_limit_bytes=24 * 1024 * 1024)
    core_index = core.astype(jnp.int32).reshape(1)
    half = WINS * WIN_PAD
    first = pl.pallas_call(
        attention_kernel,
        out_shape=jax.ShapeDtypeStruct((4 * QUAD_ROWS, D), BF16),
        in_specs=[smem, smem] + [vmem] * 3 + [hbm] * 2 + [vmem] * 2 + [anywhere] * 2,
        out_specs=vmem,
        scratch_shapes=[
            pltpu.VMEM((16, 32, 2048), BF16),
            pltpu.VMEM((half, D), BF16),
            pltpu.VMEM((half, D), BF16),
            pltpu.VMEM((half, D), BF16),
            pltpu.VMEM((768, D), BF16),
            pltpu.VMEM((4 * QUAD_ROWS, 864), BF16),
            pltpu.VMEM((4 * QUAD_ROWS, 768), BF16),
            pltpu.SemaphoreType.DMA((34,)),
        ],
        compiler_params=params,
        cost_estimate=pl.CostEstimate(
            flops=20_000_000_000, bytes_accessed=20_000_000, transcendentals=1_000_000
        ),
        name="attention",
    )(
        core_index,
        head_scale,
        tall,
        bias,
        jnp.asarray(arrangement(), BF16),
        far(jnp.asarray(patch_selection(), BF16)),
        far(jnp.asarray(selection(), BF16)),
        attention_norm_gain.reshape(1, D),
        attention_norm_offset.reshape(1, D),
        attn_mine,
        attn_other,
    )
    first, rest_mine = lax.optimization_barrier((first, rest_mine))
    rest_other = shifted(rest_mine, "core", 1, True)
    return pl.pallas_call(
        feedforward_kernel,
        out_shape=jax.ShapeDtypeStruct((6, 18, 2 * D), BF16),
        in_specs=[smem, hbm] + [vmem] * 4 + [anywhere] * 2,
        out_specs=vmem,
        scratch_shapes=[
            pltpu.VMEM((16, 32, FFN), BF16),
            pltpu.VMEM((16, 128, D), BF16),
            pltpu.VMEM((16, 128, 2 * D), BF16),
            pltpu.VMEM((4 * QUAD_ROWS, D), BF16),
            pltpu.SemaphoreType.DMA((33,)),
            pltpu.SemaphoreType.DMA((32,)),
            pltpu.SemaphoreType.DMA((32,)),
        ],
        compiler_params=params,
        cost_estimate=pl.CostEstimate(
            flops=6_000_000_000, bytes_accessed=20_000_000, transcendentals=1_000_000
        ),
        name="feedforward",
    )(
        core_index,
        far(first),
        feedforward_norm_gain.reshape(1, D),
        feedforward_norm_offset.reshape(1, D),
        merging_norm_gain.reshape(1, 2 * D),
        merging_norm_offset.reshape(1, 2 * D),
        rest_mine,
        rest_other,
    )


def solution(mesh):
    fine = Mesh(mesh.devices.reshape(2, 4, 16, 2, 2), ("y_hi", "x", "z", "y_lo", "core"))
    in_specs = (P(LAT, LON, None),) + (P(LON, None),) * 5 + (P(),) * 10
    return jax.shard_map(
        local, mesh=fine, in_specs=in_specs, out_specs=P(LAT, LON, None), check_vma=False
    )
```

```python
import jax
import jax.numpy as jnp
import numpy as np
from jax import lax
from jax.experimental import pallas as pl
from jax.experimental.pallas import tpu as pltpu
from jax.sharding import Mesh
from jax.sharding import PartitionSpec as P

D = 512
HEAD_COUNT = 8
WIN_ROWS = 6
WIN_COLS = 12
PAD_COLS = 16
SHIFT_ROWS = 3
SHIFT_COLS = 6
FFN = 2048
WIN_PAD = WIN_ROWS * PAD_COLS
KEY_PAD = 128
BANDS = 3
WINS = 4
QUAD_ROWS = 112
LAT = ("y_hi", "x")
LON = ("z", "y_lo", "core")
ALL = ("y_hi", "x", "z", "y_lo", "core")
OFF = -1e30
BF16 = jnp.bfloat16
F32 = jnp.float32
QUERY_ROWS = ((48, 48), (0, 96), (0, 48))


def shifted(block, axes, by, wrap):
    size = lax.axis_size(axes)
    pairs = [(i, (i + by) % size) for i in range(size) if wrap or 0 <= i + by < size]
    return lax.ppermute(block, axes, pairs)


def spread(block, axes):
    size = lax.axis_size(axes)
    return lax.all_to_all(jnp.broadcast_to(block[None], (size,) + block.shape), axes, 0, 0)


def rings(x_core):
    ids = np.arange(512).reshape(2, 4, 16, 2, 2)
    along_x = ids.transpose(0, 2, 3, 4, 1)[:, :, :, x_core].reshape(-1, 4)
    along_y = ids.transpose(1, 2, 4, 0, 3)[:, :, 1 - x_core].reshape(-1, 4)
    return np.concatenate([along_x, along_y]).tolist()


def four(block):
    return jnp.broadcast_to(block[None], (4,) + block.shape)


def fan_kernel(ring_ref, out_ref, sems):
    copies = [
        pltpu.make_async_copy(ring_ref.at[:, :, pl.ds(48, 32), :], out_ref.at[i], sems.at[i])
        for i in range(4)
    ]
    for copy in copies:
        copy.start()
    for copy in copies:
        copy.wait()


def fan(in_ring):
    anywhere = pl.BlockSpec(memory_space=pl.ANY)
    return pl.pallas_call(
        fan_kernel,
        out_shape=jax.ShapeDtypeStruct((4, 4, 16, 32, 128), BF16),
        in_specs=[anywhere],
        out_specs=anywhere,
        scratch_shapes=[pltpu.SemaphoreType.DMA((4,))],
        compiler_params=pltpu.CompilerParams(vmem_limit_bytes=24 * 1024 * 1024),
        cost_estimate=pl.CostEstimate(flops=0, bytes_accessed=30_000_000, transcendentals=0),
        name="fan",
    )(in_ring)


def spread_ring(copies, x_core):
    return lax.all_to_all(copies, ALL, 0, 0, axis_index_groups=rings(x_core))


def place(m, of):
    outer, inner = m // 4, m % 4

    def pick(on_first, on_second):
        return on_first + of * (on_second - on_first)

    return pick(outer // 2, inner // 2), pick(inner, outer), pick(outer % 2, inner % 2)


def bias_entries(first_weight, first_bias, second_weight):
    span_rows = 2 * WIN_ROWS - 1
    span_cols = 2 * WIN_COLS - 1
    entry = np.arange(span_rows * span_cols)
    coordinates = np.stack(
        [
            (entry // span_cols - (WIN_ROWS - 1)) * (8.0 / (WIN_ROWS - 1)),
            (entry % span_cols - (WIN_COLS - 1)) * (8.0 / (WIN_COLS - 1)),
        ],
        axis=1,
    )
    coordinates = np.sign(coordinates) * np.log2(np.abs(coordinates) + 1.0) / 3.0
    coordinates = jnp.asarray(coordinates, F32)
    hidden = jax.nn.relu(
        coordinates[:, :1] * first_weight[:1] + coordinates[:, 1:] * first_weight[1:] + first_bias
    )
    return 16.0 * jax.nn.sigmoid(
        lax.dot_general(
            second_weight, hidden, (((0,), (1,)), ((), ())), precision=lax.Precision.HIGHEST
        )
    )


def bias_lookup():
    q = np.arange(WIN_PAD)
    k = np.arange(KEY_PAD)
    qa, qb = q // PAD_COLS, np.minimum(q % PAD_COLS, WIN_COLS - 1)
    ka, kb = np.minimum(k // PAD_COLS, WIN_ROWS - 1), np.minimum(k % PAD_COLS, WIN_COLS - 1)
    rows = qa[:, None] - ka[None] + WIN_ROWS - 1
    cols = qb[:, None] - kb[None] + WIN_COLS - 1
    return rows * (2 * WIN_COLS - 1) + cols


def unit_norm(triple, ones):
    rounded = triple.astype(BF16)
    exact = rounded.astype(F32)
    square = exact * exact
    high = square.astype(BF16)
    low = (square - high.astype(F32)).astype(BF16)
    parts = []
    for i in range(D // 256):
        cut = slice(i * 256, i * 256 + 256)
        total = jnp.dot(high[:, cut], ones, preferred_element_type=F32)
        total += jnp.dot(low[:, cut], ones, preferred_element_type=F32)
        parts.append((exact[:, cut] * lax.rsqrt(total + 1e-06)).astype(BF16))
    return parts


def norm_rows(values, gain, offset):
    average = jnp.mean(values, axis=-1, keepdims=True)
    centred = values - average
    variance = jnp.mean(centred * centred, axis=-1, keepdims=True)
    return centred * lax.rsqrt(variance + 1e-05) * gain + offset


def attention_kernel(
    core_ref,
    scale_ref,
    tall_ref,
    bias_ref,
    arrange_ref,
    patch_select_ref,
    select_ref,
    gain_ref,
    offset_ref,
    mine_ref,
    other_ref,
    out_ref,
    weight,
    queries,
    keys,
    values,
    heads,
    patch_select,
    select,
    sems,
):
    core = core_ref[0]
    copies = []
    for m in range(16):
        for part, (ref, of) in enumerate(((mine_ref, core), (other_ref, 1 - core))):
            y_hi, x, y_lo = place(m, of)
            row = pl.multiple_of(y_lo * 16, 16)
            column = pl.multiple_of((y_hi * 8 + x * 2 + of) * 128, 128)
            copies.append(
                pltpu.make_async_copy(
                    ref.at[m, :, pl.ds(0, 16), :],
                    weight.at[:, pl.ds(row, 16), pl.ds(column, 128)],
                    sems.at[m * 2 + part],
                )
            )
    late = [
        pltpu.make_async_copy(select_ref, select, sems.at[32]),
        pltpu.make_async_copy(patch_select_ref, patch_select, sems.at[33]),
    ]
    for copy in copies + late:
        copy.start()
    for copy in copies:
        copy.wait()

    row = lax.broadcasted_iota(jnp.int32, (256, 256), 0)
    lane = lax.broadcasted_iota(jnp.int32, (256, 256), 1)
    ones = jnp.where(row // 64 == lane // 64, 1.0, 0.0).astype(BF16)
    row2 = lax.broadcasted_iota(jnp.int32, (256, 128), 0)
    lane2 = lax.broadcasted_iota(jnp.int32, (256, 128), 1)
    counts = jnp.where((row2 >= 128) == (lane2 >= 64), 1.0, 0.0).astype(BF16)
    low_half = lax.broadcasted_iota(jnp.int32, (WIN_PAD, 128), 1) < 64
    zero = jnp.zeros((WIN_PAD, 128), BF16)
    gap = jnp.zeros((KEY_PAD - WIN_PAD, 128), BF16)

    def columns(start, width):
        return weight[:, :, start : start + width].reshape(D, width)

    def both(block):
        return jnp.concatenate(
            [jnp.where(low_half, block, zero), gap, jnp.where(low_half, zero, block), gap], axis=0
        )

    done = 0
    for band in range(BANDS):
        strip = tall_ref[band * WIN_ROWS : (band + 1) * WIN_ROWS].reshape(WIN_ROWS * 48, D)
        tokens = jnp.dot(arrange_ref[...], strip, preferred_element_type=F32).astype(BF16)
        for target, start in ((queries, 0), (keys, D)):
            total = jnp.dot(tokens, columns(start, D), preferred_element_type=F32)
            for i, part in enumerate(unit_norm(total, ones)):
                target[:, i * 256 : i * 256 + 256] = part
        values[...] = jnp.dot(tokens, columns(2 * D, D), preferred_element_type=F32).astype(BF16)
        first, count = QUERY_ROWS[band]

        def window(w, _, band=band, first=first, count=count, done=done):
            base = pl.multiple_of(w * WIN_PAD, WIN_PAD)
            all_scores = []
            for pair in range(HEAD_COUNT // 2):
                cut = slice(pair * 128, pair * 128 + 128)
                query = queries[pl.ds(base + first, count), cut]
                key = both(keys[pl.ds(base, WIN_PAD), cut])
                all_scores.append(
                    lax.dot_general(
                        query, key, (((1,), (1,)), ((), ())), preferred_element_type=F32
                    )
                )
            for pair in range(HEAD_COUNT // 2):
                cut = slice(pair * 128, pair * 128 + 128)
                value = both(values[pl.ds(base, WIN_PAD), cut])
                scores = all_scores[pair]
                expo = []
                for h in range(2):
                    head = pair * 2 + h
                    one = scores[:, h * 128 : h * 128 + 128] * scale_ref[head]
                    one = one + bias_ref[band, head, first : first + count, :]
                    peak = jnp.max(one, axis=-1, keepdims=True)
                    expo.append(jnp.exp(one - peak).astype(BF16))
                mixed = jnp.dot(
                    jnp.concatenate(expo, axis=1),
                    jnp.concatenate([value, counts], axis=1),
                    preferred_element_type=F32,
                )
                place = pl.multiple_of(done + w * count, 16)
                heads[pl.ds(place, count), cut] = (mixed[:, :128] / mixed[:, 128:]).astype(BF16)
            return 0

        lax.fori_loop(0, WINS, window, 0, unroll=True)
        done += WINS * count

    for copy in late:
        copy.wait()
    own = jnp.dot(select[...], heads[...], preferred_element_type=F32).astype(BF16)
    projected = jnp.dot(own, columns(3 * D, D), preferred_element_type=F32)
    branch = norm_rows(projected, gain_ref[...], offset_ref[...]).astype(BF16)
    patches = jnp.dot(
        patch_select[...], tall_ref[...].reshape(18 * 48, D), preferred_element_type=F32
    )
    out_ref[...] = (patches + branch.astype(F32)).astype(BF16)


def feedforward_kernel(
    core_ref,
    first_ref,
    gain_ref,
    offset_ref,
    mine_ref,
    other_ref,
    out_ref,
    up,
    down,
    tokens_in,
    up_sems,
    down_sems,
):
    core = core_ref[0]
    ups, downs = [], []
    for m in range(16):
        for part, (ref, of) in enumerate(((mine_ref, core), (other_ref, 1 - core))):
            y_hi, x, y_lo = place(m, of)
            row = pl.multiple_of(y_lo * 16, 16)
            column = pl.multiple_of((y_hi * 8 + x * 2 + of) * 128, 128)
            ups.append(
                pltpu.make_async_copy(
                    ref.at[m, :, pl.ds(16, 16), :],
                    up.at[:, pl.ds(row, 16), pl.ds(column, 128)],
                    up_sems.at[m * 2 + part],
                )
            )
            row = pl.multiple_of(y_lo * 64 + of * 32 + y_hi * 16, 16)
            column = pl.multiple_of(x * 128, 128)
            downs.append(
                pltpu.make_async_copy(
                    ref.at[m, :, pl.ds(32, 16), :],
                    down.at[:, pl.ds(row, 16), pl.ds(column, 128)],
                    down_sems.at[m * 2 + part],
                )
            )
    ups.append(pltpu.make_async_copy(first_ref, tokens_in, up_sems.at[32]))
    for copy in ups + downs:
        copy.start()
    for copy in ups:
        copy.wait()
    tokens = tokens_in[...]
    total = None
    for n in range(FFN // 512):
        cut = slice(n * 512, n * 512 + 512)
        hidden = jnp.dot(tokens, up[:, :, cut].reshape(D, 512), preferred_element_type=F32)
        hidden = (0.5 * hidden * (1.0 + lax.erf(hidden * (0.5**0.5)))).astype(BF16)
        if n == 0:
            for copy in downs:
                copy.wait()
        piece = jnp.dot(
            hidden, down[n * 4 : n * 4 + 4].reshape(512, D), preferred_element_type=F32
        )
        total = piece if total is None else total + piece
    branch = norm_rows(total, gain_ref[...], offset_ref[...])
    out_ref[...] = (tokens.astype(F32) + branch).astype(BF16)


def merge_kernel(
    core_ref, second_ref, gain_ref, offset_ref, mine_ref, other_ref, out_ref, merge, sems
):
    core = core_ref[0]
    copies = []
    for m in range(16):
        for part, (ref, of) in enumerate(((mine_ref, core), (other_ref, 1 - core))):
            y_hi, x, y_lo = place(m, of)
            row = pl.multiple_of(y_lo * 64 + of * 32, 32)
            column = pl.multiple_of((y_hi * 4 + x) * 128, 128)
            copies.append(
                pltpu.make_async_copy(
                    ref.at[m],
                    merge.at[:, pl.ds(row, 32), pl.ds(column, 128)],
                    sems.at[m * 2 + part],
                )
            )
    for copy in copies:
        copy.start()
    for copy in copies:
        copy.wait()
    total = None
    for n in range(4):
        piece = jnp.dot(
            second_ref[n * QUAD_ROWS : (n + 1) * QUAD_ROWS],
            merge[n * 4 : n * 4 + 4].reshape(512, 2 * D),
            preferred_element_type=F32,
        )
        total = piece if total is None else total + piece
    reduced = norm_rows(total, gain_ref[...], offset_ref[...])
    for i in range(6):
        out_ref[i] = reduced[i * 18 : i * 18 + 18].astype(BF16)


def quads_order(place):
    order = place.reshape(6, 2, 18, 2).transpose(3, 1, 0, 2).reshape(4, 108)
    return np.pad(order, ((0, 0), (0, QUAD_ROWS - 108)), constant_values=-1).reshape(-1)


def one_hot_rows(order, size):
    return (order[:, None] == np.arange(size)[None]).astype(np.float32)


def selection():
    place = np.full((12, 36), -1)
    done = 0
    for band in range(BANDS):
        first, count = QUERY_ROWS[band]
        for w in range(WINS):
            for r in range(count):
                a, b = (first + r) // PAD_COLS, (first + r) % PAD_COLS
                i = band * WIN_ROWS + a - SHIFT_ROWS
                j = w * WIN_COLS + b - SHIFT_COLS
                if b < WIN_COLS and 0 <= j < 36:
                    place[i, j] = done + r
            done += count
    return one_hot_rows(quads_order(place), done)


def patch_selection():
    i, j = np.arange(12)[:, None] + SHIFT_ROWS, np.arange(36)[None] + SHIFT_COLS
    return one_hot_rows(quads_order(i * 48 + j), 18 * 48)


def arrangement():
    r = np.arange(WINS * WIN_PAD)
    w, a, b = r // WIN_PAD, r % WIN_PAD // PAD_COLS, r % PAD_COLS
    return one_hot_rows(np.where(b < WIN_COLS, a * 48 + w * WIN_COLS + b, -1), WIN_ROWS * 48)


def local(
    patches,
    query_key_value_weight,
    attention_output_weight,
    feedforward_in_weight,
    feedforward_out_weight,
    merging_reduction_weight,
    head_scale_logarithm,
    bias_network_first_weight,
    bias_network_first_bias,
    bias_network_second_weight,
    attention_norm_gain,
    attention_norm_offset,
    feedforward_norm_gain,
    feedforward_norm_offset,
    merging_norm_gain,
    merging_norm_offset,
):
    lat = lax.axis_index(LAT)
    core = lax.axis_index("core")
    x = lax.axis_index("x")

    mine = jnp.concatenate(
        [query_key_value_weight, attention_output_weight, feedforward_in_weight], axis=1
    )
    theirs = shifted(mine, "core", 1, True)
    rows = jnp.concatenate(
        [jnp.where(core == 0, mine, theirs), jnp.where(core == 0, theirs, mine)], axis=0
    )
    at = (lat * 2 + core) * 128
    units = jnp.concatenate(
        [
            lax.dynamic_slice(rows, (0, at), (16, 128)),
            lax.dynamic_slice(rows, (0, 2048 + at), (16, 128)),
            lax.dynamic_slice(
                feedforward_out_weight, (lax.axis_index("y_hi") * 16, x * 128), (16, 128)
            ),
            lax.dynamic_slice(merging_reduction_weight, (0, lat * 128), (32, 128)),
        ]
    )

    units, patches = lax.optimization_barrier((units, patches))
    along_z = spread(units, "z")
    south = shifted(patches[:SHIFT_ROWS], LAT, -1, False)
    north = shifted(patches[12 - SHIFT_ROWS :], LAT, 1, False)
    strip = jnp.concatenate([north, patches, south], axis=0)

    table = bias_entries(
        bias_network_first_weight, bias_network_first_bias, bias_network_second_weight
    )
    lookup = bias_lookup()
    entries = table.shape[1]
    one_hot = (
        jnp.asarray(lookup.reshape(-1), jnp.int32)[None, :]
        == jnp.arange(entries, dtype=jnp.int32)[:, None]
    ).astype(F32)
    bias = jnp.dot(table, one_hot, precision=lax.Precision.HIGHEST)
    bias = bias.reshape(HEAD_COUNT, WIN_PAD, KEY_PAD)
    key = np.arange(KEY_PAD)
    held = (key < WIN_PAD) & (key % PAD_COLS < WIN_COLS)
    bias = jnp.where(jnp.asarray(held), bias, OFF)
    apart = (np.arange(WIN_PAD)[:, None] // 48) != (key[None] // 48)
    seam = jnp.stack([lat == 0, jnp.bool_(False), lat == 7])
    bias = jnp.where(seam[:, None, None, None] & jnp.asarray(apart), OFF, bias[None])
    head_scale = jnp.exp(jnp.minimum(head_scale_logarithm, jnp.log(100.0)))

    along_z, strip, bias = lax.optimization_barrier((along_z, strip, bias))
    in_ring = spread_ring(four(along_z), 0)
    east = shifted(strip[:, :SHIFT_COLS], LON, -1, True)
    west = shifted(strip[:, 36 - SHIFT_COLS :], LON, 1, True)
    tall = jnp.concatenate([west, strip, east], axis=1)
    in_ring, tall = lax.optimization_barrier((in_ring, tall))
    attn_mine = spread_ring(four(in_ring[:, :, :48]), 1).reshape(16, 16, 48, 128)
    rest_copies = fan(in_ring)
    attn_mine, rest_copies = lax.optimization_barrier((attn_mine, rest_copies))
    attn_other = shifted(attn_mine, "core", 1, True)
    rest_mine = spread_ring(rest_copies, 1).reshape(16, 16, 32, 128)

    vmem = pl.BlockSpec(memory_space=pltpu.VMEM)
    smem = pl.BlockSpec(memory_space=pltpu.SMEM)
    hbm = pl.BlockSpec(memory_space=pltpu.HBM)
    anywhere = pl.BlockSpec(memory_space=pl.ANY)

    def far(block):
        return pltpu.with_memory_space_constraint(block, pltpu.HBM)

    params = pltpu.CompilerParams(vmem_limit_bytes=24 * 1024 * 1024)
    core_index = core.astype(jnp.int32).reshape(1)
    half = WINS * WIN_PAD
    first = pl.pallas_call(
        attention_kernel,
        out_shape=jax.ShapeDtypeStruct((4 * QUAD_ROWS, D), BF16),
        in_specs=[smem, smem] + [vmem] * 3 + [hbm] * 2 + [vmem] * 2 + [anywhere] * 2,
        out_specs=vmem,
        scratch_shapes=[
            pltpu.VMEM((16, 32, 2048), BF16),
            pltpu.VMEM((half, D), BF16),
            pltpu.VMEM((half, D), BF16),
            pltpu.VMEM((half, D), BF16),
            pltpu.VMEM((768, D), BF16),
            pltpu.VMEM((4 * QUAD_ROWS, 864), BF16),
            pltpu.VMEM((4 * QUAD_ROWS, 768), BF16),
            pltpu.SemaphoreType.DMA((34,)),
        ],
        compiler_params=params,
        cost_estimate=pl.CostEstimate(
            flops=20_000_000_000, bytes_accessed=20_000_000, transcendentals=1_000_000
        ),
        name="attention",
    )(
        core_index,
        head_scale,
        tall,
        bias,
        jnp.asarray(arrangement(), BF16),
        far(jnp.asarray(patch_selection(), BF16)),
        far(jnp.asarray(selection(), BF16)),
        attention_norm_gain.reshape(1, D),
        attention_norm_offset.reshape(1, D),
        attn_mine,
        attn_other,
    )
    first, rest_mine = lax.optimization_barrier((first, rest_mine))
    rest_other = shifted(rest_mine, "core", 1, True)
    second = pl.pallas_call(
        feedforward_kernel,
        out_shape=jax.ShapeDtypeStruct((4 * QUAD_ROWS, D), BF16),
        in_specs=[smem, hbm] + [vmem] * 2 + [anywhere] * 2,
        out_specs=vmem,
        scratch_shapes=[
            pltpu.VMEM((16, 32, FFN), BF16),
            pltpu.VMEM((16, 128, D), BF16),
            pltpu.VMEM((4 * QUAD_ROWS, D), BF16),
            pltpu.SemaphoreType.DMA((33,)),
            pltpu.SemaphoreType.DMA((32,)),
        ],
        compiler_params=params,
        cost_estimate=pl.CostEstimate(
            flops=6_000_000_000, bytes_accessed=20_000_000, transcendentals=1_000_000
        ),
        name="feedforward",
    )(
        core_index,
        far(first),
        feedforward_norm_gain.reshape(1, D),
        feedforward_norm_offset.reshape(1, D),
        attn_mine,
        attn_other,
    )
    return pl.pallas_call(
        merge_kernel,
        out_shape=jax.ShapeDtypeStruct((6, 18, 2 * D), BF16),
        in_specs=[smem] + [vmem] * 3 + [anywhere] * 2,
        out_specs=vmem,
        scratch_shapes=[pltpu.VMEM((16, 128, 2 * D), BF16), pltpu.SemaphoreType.DMA((32,))],
        compiler_params=params,
        cost_estimate=pl.CostEstimate(
            flops=1_000_000_000, bytes_accessed=8_000_000, transcendentals=0
        ),
        name="merging",
    )(
        core_index,
        second,
        merging_norm_gain.reshape(1, 2 * D),
        merging_norm_offset.reshape(1, 2 * D),
        rest_mine,
        rest_other,
    )


def solution(mesh):
    fine = Mesh(mesh.devices.reshape(2, 4, 16, 2, 2), ("y_hi", "x", "z", "y_lo", "core"))
    in_specs = (P(LAT, LON, None),) + (P(LON, None),) * 5 + (P(),) * 10
    return jax.shard_map(
        local, mesh=fine, in_specs=in_specs, out_specs=P(LAT, LON, None), check_vma=False
    )
```

```python
import jax
import jax.numpy as jnp
import numpy as np
from jax import lax
from jax.experimental import pallas as pl
from jax.experimental.pallas import tpu as pltpu
from jax.sharding import Mesh
from jax.sharding import PartitionSpec as P

D = 512
HEAD_COUNT = 8
WIN_ROWS = 6
WIN_COLS = 12
PAD_COLS = 16
SHIFT_ROWS = 3
SHIFT_COLS = 6
FFN = 2048
WIN_PAD = WIN_ROWS * PAD_COLS
KEY_PAD = 128
BANDS = 3
WINS = 4
QUAD_ROWS = 112
LAT = ("y_hi", "x")
LON = ("z", "y_lo", "core")
ALL = ("y_hi", "x", "z", "y_lo", "core")
OFF = -1e30
BF16 = jnp.bfloat16
F32 = jnp.float32
QUERY_ROWS = ((48, 48), (0, 96), (0, 48))


def shifted(block, axes, by, wrap):
    size = lax.axis_size(axes)
    pairs = [(i, (i + by) % size) for i in range(size) if wrap or 0 <= i + by < size]
    return lax.ppermute(block, axes, pairs)


def spread(block, axes):
    size = lax.axis_size(axes)
    return lax.all_to_all(jnp.broadcast_to(block[None], (size,) + block.shape), axes, 0, 0)


def rings(x_core):
    ids = np.arange(512).reshape(2, 4, 16, 2, 2)
    along_x = ids.transpose(0, 2, 3, 4, 1)[:, :, :, x_core].reshape(-1, 4)
    along_y = ids.transpose(1, 2, 4, 0, 3)[:, :, 1 - x_core].reshape(-1, 4)
    return np.concatenate([along_x, along_y]).tolist()


def four(block):
    return jnp.broadcast_to(block[None], (4,) + block.shape)


def fan_kernel(ring_ref, out_ref, sems):
    copies = [
        pltpu.make_async_copy(ring_ref.at[:, :, pl.ds(48, 32), :], out_ref.at[i], sems.at[i])
        for i in range(4)
    ]
    for copy in copies:
        copy.start()
    for copy in copies:
        copy.wait()


def fan(in_ring):
    anywhere = pl.BlockSpec(memory_space=pl.ANY)
    return pl.pallas_call(
        fan_kernel,
        out_shape=jax.ShapeDtypeStruct((4, 4, 16, 32, 128), BF16),
        in_specs=[anywhere],
        out_specs=anywhere,
        scratch_shapes=[pltpu.SemaphoreType.DMA((4,))],
        compiler_params=pltpu.CompilerParams(vmem_limit_bytes=24 * 1024 * 1024),
        cost_estimate=pl.CostEstimate(flops=0, bytes_accessed=30_000_000, transcendentals=0),
        name="fan",
    )(in_ring)


def spread_ring(copies, x_core):
    return lax.all_to_all(copies, ALL, 0, 0, axis_index_groups=rings(x_core))


def place(m, of):
    outer, inner = m // 4, m % 4

    def pick(on_first, on_second):
        return on_first + of * (on_second - on_first)

    return pick(outer // 2, inner // 2), pick(inner, outer), pick(outer % 2, inner % 2)


def bias_entries(first_weight, first_bias, second_weight):
    span_rows = 2 * WIN_ROWS - 1
    span_cols = 2 * WIN_COLS - 1
    entry = np.arange(span_rows * span_cols)
    coordinates = np.stack(
        [
            (entry // span_cols - (WIN_ROWS - 1)) * (8.0 / (WIN_ROWS - 1)),
            (entry % span_cols - (WIN_COLS - 1)) * (8.0 / (WIN_COLS - 1)),
        ],
        axis=1,
    )
    coordinates = np.sign(coordinates) * np.log2(np.abs(coordinates) + 1.0) / 3.0
    coordinates = jnp.asarray(coordinates, F32)
    hidden = jax.nn.relu(
        coordinates[:, :1] * first_weight[:1] + coordinates[:, 1:] * first_weight[1:] + first_bias
    )
    return 16.0 * jax.nn.sigmoid(
        lax.dot_general(
            second_weight, hidden, (((0,), (1,)), ((), ())), precision=lax.Precision.HIGHEST
        )
    )


def bias_lookup():
    q = np.arange(WIN_PAD)
    k = np.arange(KEY_PAD)
    qa, qb = q // PAD_COLS, np.minimum(q % PAD_COLS, WIN_COLS - 1)
    ka, kb = np.minimum(k // PAD_COLS, WIN_ROWS - 1), np.minimum(k % PAD_COLS, WIN_COLS - 1)
    rows = qa[:, None] - ka[None] + WIN_ROWS - 1
    cols = qb[:, None] - kb[None] + WIN_COLS - 1
    return rows * (2 * WIN_COLS - 1) + cols


def unit_norm(triple, ones):
    rounded = triple.astype(BF16)
    exact = rounded.astype(F32)
    square = exact * exact
    high = square.astype(BF16)
    low = (square - high.astype(F32)).astype(BF16)
    parts = []
    for i in range(D // 256):
        cut = slice(i * 256, i * 256 + 256)
        total = jnp.dot(high[:, cut], ones, preferred_element_type=F32)
        total += jnp.dot(low[:, cut], ones, preferred_element_type=F32)
        parts.append((exact[:, cut] * lax.rsqrt(total + 1e-06)).astype(BF16))
    return parts


def norm_rows(values, gain, offset):
    average = jnp.mean(values, axis=-1, keepdims=True)
    centred = values - average
    variance = jnp.mean(centred * centred, axis=-1, keepdims=True)
    return centred * lax.rsqrt(variance + 1e-05) * gain + offset


def attention_kernel(
    core_ref,
    scale_ref,
    tall_in,
    bias_ref,
    arrange_in,
    patch_select_ref,
    select_ref,
    gain_ref,
    offset_ref,
    mine_ref,
    other_ref,
    out_ref,
    weight,
    queries,
    keys,
    values,
    heads,
    patch_select,
    select,
    tall_ref,
    arrange_ref,
    sems,
):
    core = core_ref[0]
    copies = []
    for m in range(16):
        for part, (ref, of) in enumerate(((mine_ref, core), (other_ref, 1 - core))):
            y_hi, x, y_lo = place(m, of)
            row = pl.multiple_of(y_lo * 16, 16)
            column = pl.multiple_of((y_hi * 8 + x * 2 + of) * 128, 128)
            copies.append(
                pltpu.make_async_copy(
                    ref.at[m, :, pl.ds(0, 16), :],
                    weight.at[:, pl.ds(row, 16), pl.ds(column, 128)],
                    sems.at[m * 2 + part],
                )
            )
    copies.append(pltpu.make_async_copy(tall_in, tall_ref, sems.at[34]))
    copies.append(pltpu.make_async_copy(arrange_in, arrange_ref, sems.at[35]))
    late = [
        pltpu.make_async_copy(select_ref, select, sems.at[32]),
        pltpu.make_async_copy(patch_select_ref, patch_select, sems.at[33]),
    ]
    for copy in copies + late:
        copy.start()
    for copy in copies:
        copy.wait()

    row = lax.broadcasted_iota(jnp.int32, (256, 256), 0)
    lane = lax.broadcasted_iota(jnp.int32, (256, 256), 1)
    ones = jnp.where(row // 64 == lane // 64, 1.0, 0.0).astype(BF16)
    row2 = lax.broadcasted_iota(jnp.int32, (256, 128), 0)
    lane2 = lax.broadcasted_iota(jnp.int32, (256, 128), 1)
    counts = jnp.where((row2 >= 128) == (lane2 >= 64), 1.0, 0.0).astype(BF16)
    low_half = lax.broadcasted_iota(jnp.int32, (WIN_PAD, 128), 1) < 64
    zero = jnp.zeros((WIN_PAD, 128), BF16)
    gap = jnp.zeros((KEY_PAD - WIN_PAD, 128), BF16)

    def columns(start, width):
        return weight[:, :, start : start + width].reshape(D, width)

    def both(block):
        return jnp.concatenate(
            [jnp.where(low_half, block, zero), gap, jnp.where(low_half, zero, block), gap], axis=0
        )

    done = 0
    for band in range(BANDS):
        strip = tall_ref[band * WIN_ROWS : (band + 1) * WIN_ROWS].reshape(WIN_ROWS * 48, D)
        tokens = jnp.dot(arrange_ref[...], strip, preferred_element_type=F32).astype(BF16)
        for target, start in ((queries, 0), (keys, D)):
            total = jnp.dot(tokens, columns(start, D), preferred_element_type=F32)
            for i, part in enumerate(unit_norm(total, ones)):
                target[:, i * 256 : i * 256 + 256] = part
        values[...] = jnp.dot(tokens, columns(2 * D, D), preferred_element_type=F32).astype(BF16)
        first, count = QUERY_ROWS[band]

        def window(w, _, band=band, first=first, count=count, done=done):
            base = pl.multiple_of(w * WIN_PAD, WIN_PAD)
            all_scores = []
            for pair in range(HEAD_COUNT // 2):
                cut = slice(pair * 128, pair * 128 + 128)
                query = queries[pl.ds(base + first, count), cut]
                key = both(keys[pl.ds(base, WIN_PAD), cut])
                all_scores.append(
                    lax.dot_general(
                        query, key, (((1,), (1,)), ((), ())), preferred_element_type=F32
                    )
                )
            for pair in range(HEAD_COUNT // 2):
                cut = slice(pair * 128, pair * 128 + 128)
                value = both(values[pl.ds(base, WIN_PAD), cut])
                scores = all_scores[pair]
                expo = []
                for h in range(2):
                    head = pair * 2 + h
                    one = scores[:, h * 128 : h * 128 + 128] * scale_ref[head]
                    one = one + bias_ref[band, head, first : first + count, :]
                    peak = jnp.max(one, axis=-1, keepdims=True)
                    expo.append(jnp.exp(one - peak).astype(BF16))
                mixed = jnp.dot(
                    jnp.concatenate(expo, axis=1),
                    jnp.concatenate([value, counts], axis=1),
                    preferred_element_type=F32,
                )
                place = pl.multiple_of(done + w * count, 16)
                heads[pl.ds(place, count), cut] = (mixed[:, :128] / mixed[:, 128:]).astype(BF16)
            return 0

        lax.fori_loop(0, WINS, window, 0, unroll=True)
        done += WINS * count

    for copy in late:
        copy.wait()
    own = jnp.dot(select[...], heads[...], preferred_element_type=F32).astype(BF16)
    projected = jnp.dot(own, columns(3 * D, D), preferred_element_type=F32)
    branch = norm_rows(projected, gain_ref[...], offset_ref[...]).astype(BF16)
    patches = jnp.dot(
        patch_select[...], tall_ref[...].reshape(18 * 48, D), preferred_element_type=F32
    )
    out_ref[...] = (patches + branch.astype(F32)).astype(BF16)


def feedforward_kernel(
    core_ref,
    first_ref,
    gain_ref,
    offset_ref,
    mine_ref,
    other_ref,
    out_ref,
    up,
    down,
    tokens_in,
    up_sems,
    down_sems,
):
    core = core_ref[0]
    ups, downs = [], []
    for m in range(16):
        for part, (ref, of) in enumerate(((mine_ref, core), (other_ref, 1 - core))):
            y_hi, x, y_lo = place(m, of)
            row = pl.multiple_of(y_lo * 16, 16)
            column = pl.multiple_of((y_hi * 8 + x * 2 + of) * 128, 128)
            ups.append(
                pltpu.make_async_copy(
                    ref.at[m, :, pl.ds(16, 16), :],
                    up.at[:, pl.ds(row, 16), pl.ds(column, 128)],
                    up_sems.at[m * 2 + part],
                )
            )
            row = pl.multiple_of(y_lo * 64 + of * 32 + y_hi * 16, 16)
            column = pl.multiple_of(x * 128, 128)
            downs.append(
                pltpu.make_async_copy(
                    ref.at[m, :, pl.ds(32, 16), :],
                    down.at[:, pl.ds(row, 16), pl.ds(column, 128)],
                    down_sems.at[m * 2 + part],
                )
            )
    ups.append(pltpu.make_async_copy(first_ref, tokens_in, up_sems.at[32]))
    for copy in ups + downs:
        copy.start()
    for copy in ups:
        copy.wait()
    tokens = tokens_in[...]
    total = None
    for n in range(FFN // 512):
        cut = slice(n * 512, n * 512 + 512)
        hidden = jnp.dot(tokens, up[:, :, cut].reshape(D, 512), preferred_element_type=F32)
        hidden = (0.5 * hidden * (1.0 + lax.erf(hidden * (0.5**0.5)))).astype(BF16)
        if n == 0:
            for copy in downs:
                copy.wait()
        piece = jnp.dot(
            hidden, down[n * 4 : n * 4 + 4].reshape(512, D), preferred_element_type=F32
        )
        total = piece if total is None else total + piece
    branch = norm_rows(total, gain_ref[...], offset_ref[...])
    out_ref[...] = (tokens.astype(F32) + branch).astype(BF16)


def merge_kernel(
    core_ref, second_ref, gain_ref, offset_ref, mine_ref, other_ref, out_ref, merge, sems
):
    core = core_ref[0]
    copies = []
    for m in range(16):
        for part, (ref, of) in enumerate(((mine_ref, core), (other_ref, 1 - core))):
            y_hi, x, y_lo = place(m, of)
            row = pl.multiple_of(y_lo * 64 + of * 32, 32)
            column = pl.multiple_of((y_hi * 4 + x) * 128, 128)
            copies.append(
                pltpu.make_async_copy(
                    ref.at[m],
                    merge.at[:, pl.ds(row, 32), pl.ds(column, 128)],
                    sems.at[m * 2 + part],
                )
            )
    for copy in copies:
        copy.start()
    for copy in copies:
        copy.wait()
    total = None
    for n in range(4):
        piece = jnp.dot(
            second_ref[n * QUAD_ROWS : (n + 1) * QUAD_ROWS],
            merge[n * 4 : n * 4 + 4].reshape(512, 2 * D),
            preferred_element_type=F32,
        )
        total = piece if total is None else total + piece
    reduced = norm_rows(total, gain_ref[...], offset_ref[...])
    for i in range(6):
        out_ref[i] = reduced[i * 18 : i * 18 + 18].astype(BF16)


def quads_order(place):
    order = place.reshape(6, 2, 18, 2).transpose(3, 1, 0, 2).reshape(4, 108)
    return np.pad(order, ((0, 0), (0, QUAD_ROWS - 108)), constant_values=-1).reshape(-1)


def one_hot_rows(order, size):
    return (order[:, None] == np.arange(size)[None]).astype(np.float32)


def selection():
    place = np.full((12, 36), -1)
    done = 0
    for band in range(BANDS):
        first, count = QUERY_ROWS[band]
        for w in range(WINS):
            for r in range(count):
                a, b = (first + r) // PAD_COLS, (first + r) % PAD_COLS
                i = band * WIN_ROWS + a - SHIFT_ROWS
                j = w * WIN_COLS + b - SHIFT_COLS
                if b < WIN_COLS and 0 <= j < 36:
                    place[i, j] = done + r
            done += count
    return one_hot_rows(quads_order(place), done)


def patch_selection():
    i, j = np.arange(12)[:, None] + SHIFT_ROWS, np.arange(36)[None] + SHIFT_COLS
    return one_hot_rows(quads_order(i * 48 + j), 18 * 48)


def arrangement():
    r = np.arange(WINS * WIN_PAD)
    w, a, b = r // WIN_PAD, r % WIN_PAD // PAD_COLS, r % PAD_COLS
    return one_hot_rows(np.where(b < WIN_COLS, a * 48 + w * WIN_COLS + b, -1), WIN_ROWS * 48)


def local(
    patches,
    query_key_value_weight,
    attention_output_weight,
    feedforward_in_weight,
    feedforward_out_weight,
    merging_reduction_weight,
    head_scale_logarithm,
    bias_network_first_weight,
    bias_network_first_bias,
    bias_network_second_weight,
    attention_norm_gain,
    attention_norm_offset,
    feedforward_norm_gain,
    feedforward_norm_offset,
    merging_norm_gain,
    merging_norm_offset,
):
    lat = lax.axis_index(LAT)
    core = lax.axis_index("core")
    x = lax.axis_index("x")

    mine = jnp.concatenate(
        [query_key_value_weight, attention_output_weight, feedforward_in_weight], axis=1
    )
    theirs = shifted(mine, "core", 1, True)
    rows = jnp.concatenate(
        [jnp.where(core == 0, mine, theirs), jnp.where(core == 0, theirs, mine)], axis=0
    )
    at = (lat * 2 + core) * 128
    units = jnp.concatenate(
        [
            lax.dynamic_slice(rows, (0, at), (16, 128)),
            lax.dynamic_slice(rows, (0, 2048 + at), (16, 128)),
            lax.dynamic_slice(
                feedforward_out_weight, (lax.axis_index("y_hi") * 16, x * 128), (16, 128)
            ),
            lax.dynamic_slice(merging_reduction_weight, (0, lat * 128), (32, 128)),
        ]
    )

    units, patches = lax.optimization_barrier((units, patches))
    along_z = spread(units, "z")
    south = shifted(patches[:SHIFT_ROWS], LAT, -1, False)
    north = shifted(patches[12 - SHIFT_ROWS :], LAT, 1, False)
    strip = jnp.concatenate([north, patches, south], axis=0)

    table = bias_entries(
        bias_network_first_weight, bias_network_first_bias, bias_network_second_weight
    )
    lookup = bias_lookup()
    entries = table.shape[1]
    one_hot = (
        jnp.asarray(lookup.reshape(-1), jnp.int32)[None, :]
        == jnp.arange(entries, dtype=jnp.int32)[:, None]
    ).astype(F32)
    bias = jnp.dot(table, one_hot, precision=lax.Precision.HIGHEST)
    bias = bias.reshape(HEAD_COUNT, WIN_PAD, KEY_PAD)
    key = np.arange(KEY_PAD)
    held = (key < WIN_PAD) & (key % PAD_COLS < WIN_COLS)
    bias = jnp.where(jnp.asarray(held), bias, OFF)
    apart = (np.arange(WIN_PAD)[:, None] // 48) != (key[None] // 48)
    seam = jnp.stack([lat == 0, jnp.bool_(False), lat == 7])
    bias = jnp.where(seam[:, None, None, None] & jnp.asarray(apart), OFF, bias[None])
    head_scale = jnp.exp(jnp.minimum(head_scale_logarithm, jnp.log(100.0)))

    along_z, strip, bias = lax.optimization_barrier((along_z, strip, bias))
    in_ring = spread_ring(four(along_z), 0)
    east = shifted(strip[:, :SHIFT_COLS], LON, -1, True)
    west = shifted(strip[:, 36 - SHIFT_COLS :], LON, 1, True)
    tall = jnp.concatenate([west, strip, east], axis=1)
    in_ring, tall = lax.optimization_barrier((in_ring, tall))
    attn_mine = spread_ring(four(in_ring[:, :, :48]), 1).reshape(16, 16, 48, 128)
    rest_copies = fan(in_ring)
    attn_mine, rest_copies = lax.optimization_barrier((attn_mine, rest_copies))
    attn_other = shifted(attn_mine, "core", 1, True)
    rest_mine = spread_ring(rest_copies, 1).reshape(16, 16, 32, 128)

    vmem = pl.BlockSpec(memory_space=pltpu.VMEM)
    smem = pl.BlockSpec(memory_space=pltpu.SMEM)
    hbm = pl.BlockSpec(memory_space=pltpu.HBM)
    anywhere = pl.BlockSpec(memory_space=pl.ANY)

    def far(block):
        return pltpu.with_memory_space_constraint(block, pltpu.HBM)

    params = pltpu.CompilerParams(vmem_limit_bytes=24 * 1024 * 1024)
    core_index = core.astype(jnp.int32).reshape(1)
    half = WINS * WIN_PAD
    first = pl.pallas_call(
        attention_kernel,
        out_shape=jax.ShapeDtypeStruct((4 * QUAD_ROWS, D), BF16),
        in_specs=[smem, smem, hbm, vmem] + [hbm] * 3 + [vmem] * 2 + [anywhere] * 2,
        out_specs=vmem,
        scratch_shapes=[
            pltpu.VMEM((16, 32, 2048), BF16),
            pltpu.VMEM((half, D), BF16),
            pltpu.VMEM((half, D), BF16),
            pltpu.VMEM((half, D), BF16),
            pltpu.VMEM((768, D), BF16),
            pltpu.VMEM((4 * QUAD_ROWS, 864), BF16),
            pltpu.VMEM((4 * QUAD_ROWS, 768), BF16),
            pltpu.VMEM((18, 48, D), BF16),
            pltpu.VMEM((WINS * WIN_PAD, WIN_ROWS * 48), BF16),
            pltpu.SemaphoreType.DMA((36,)),
        ],
        compiler_params=params,
        cost_estimate=pl.CostEstimate(
            flops=20_000_000_000, bytes_accessed=20_000_000, transcendentals=1_000_000
        ),
        name="attention",
    )(
        core_index,
        head_scale,
        far(tall),
        bias,
        far(jnp.asarray(arrangement(), BF16)),
        far(jnp.asarray(patch_selection(), BF16)),
        far(jnp.asarray(selection(), BF16)),
        attention_norm_gain.reshape(1, D),
        attention_norm_offset.reshape(1, D),
        attn_mine,
        attn_other,
    )
    first, rest_mine = lax.optimization_barrier((first, rest_mine))
    rest_other = shifted(rest_mine, "core", 1, True)
    second = pl.pallas_call(
        feedforward_kernel,
        out_shape=jax.ShapeDtypeStruct((4 * QUAD_ROWS, D), BF16),
        in_specs=[smem, hbm] + [vmem] * 2 + [anywhere] * 2,
        out_specs=vmem,
        scratch_shapes=[
            pltpu.VMEM((16, 32, FFN), BF16),
            pltpu.VMEM((16, 128, D), BF16),
            pltpu.VMEM((4 * QUAD_ROWS, D), BF16),
            pltpu.SemaphoreType.DMA((33,)),
            pltpu.SemaphoreType.DMA((32,)),
        ],
        compiler_params=params,
        cost_estimate=pl.CostEstimate(
            flops=6_000_000_000, bytes_accessed=20_000_000, transcendentals=1_000_000
        ),
        name="feedforward",
    )(
        core_index,
        far(first),
        feedforward_norm_gain.reshape(1, D),
        feedforward_norm_offset.reshape(1, D),
        attn_mine,
        attn_other,
    )
    return pl.pallas_call(
        merge_kernel,
        out_shape=jax.ShapeDtypeStruct((6, 18, 2 * D), BF16),
        in_specs=[smem] + [vmem] * 3 + [anywhere] * 2,
        out_specs=vmem,
        scratch_shapes=[pltpu.VMEM((16, 128, 2 * D), BF16), pltpu.SemaphoreType.DMA((32,))],
        compiler_params=params,
        cost_estimate=pl.CostEstimate(
            flops=1_000_000_000, bytes_accessed=8_000_000, transcendentals=0
        ),
        name="merging",
    )(
        core_index,
        second,
        merging_norm_gain.reshape(1, 2 * D),
        merging_norm_offset.reshape(1, 2 * D),
        rest_mine,
        rest_other,
    )


def solution(mesh):
    fine = Mesh(mesh.devices.reshape(2, 4, 16, 2, 2), ("y_hi", "x", "z", "y_lo", "core"))
    in_specs = (P(LAT, LON, None),) + (P(LON, None),) * 5 + (P(),) * 10
    return jax.shard_map(
        local, mesh=fine, in_specs=in_specs, out_specs=P(LAT, LON, None), check_vma=False
    )
```
